32 devices in a mesh: section: 4 (over z), dp: 8 (over y, x, core).
Axes of the slice: x: 2, y: 2, z: 4, core: 2. Of those that a mesh axis runs over, the one named last changes fastest.
Arguments:
- tokens_in: bfloat16 [8, 2048, 640], P('dp'), may hold values from -6 to 6
- doc_starts: int32 [8, 2048], P('dp'), may hold values from 0 to 1
- cotangent: bfloat16 [8, 2048, 640], P('dp'), may hold values from -6 to 6
- tap_weight: bfloat16 [4, 640, 1920], P('section', 'dp'), may hold values from -0.15625 to 0.15625
- gate_bias: bfloat16 [2, 1920], replicated, may hold values from -8.5 to 8.5
Outputs:
- hidden_out: bfloat16 [8, 2048, 640], P('dp', 'section')
- input_grad: float32 [8, 2048, 640], P('dp', 'section')
- weight_grad: float32 [4, 640, 1920], P('section', 'dp')
- bias_grad: float32 [2, 1920], replicated
- last_states: float32 [2, 8, 640], P(None, 'dp')
The draws below stay inside these ranges and needn't reach their ends.
All inputs are finite; a program needn't handle non-finite values.
Results may differ from the reference program's by a relative error of at most 0.012.
Values may be sent and summed in bfloat16 or wider, within the bound.
No kernel may reach another device: no remote copies, remote signals or barrier semaphores. Data moves between devices by JAX's collectives and lax.ppermute only.
A program may use at most 256 MiB of HBM per device.

```python
import jax
import jax.numpy as jnp
from jax import lax

D = 640
LENGTH = 2048
STREAMS = 8


def draw_doc_starts(key, part):
    key = jax.random.fold_in(key, 11)
    count_key, whole_key, place_key = jax.random.split(key, 3)
    counts = jax.random.randint(count_key, (STREAMS,), 1, 4)
    whole_stream = jax.random.randint(whole_key, (), 0, STREAMS)
    counts = jnp.where(jnp.arange(STREAMS) == whole_stream, 0, counts)
    positions = jax.random.randint(place_key, (STREAMS, 3), 1, LENGTH)
    used = jnp.arange(3)[None, :] < counts[:, None]
    hits = (positions[:, :, None] == jnp.arange(LENGTH)[None, None, :]) & used[:, :, None]
    return jnp.any(hits, axis=1).astype(jnp.int32)


def draw_gate_bias(key, part):
    key = jax.random.fold_in(key, 5)
    keys = jax.random.split(key, 6)
    slow_share = 0.5
    sign_share = 0.5
    slow = jax.random.bernoulli(keys[0], slow_share, (2, D))
    forget_bias = jnp.where(slow, jax.random.uniform(keys[1], (2, D), jnp.float32, 6.0, 8.5), jax.random.uniform(keys[2], (2, D), jnp.float32, -2.0, 2.0))
    signs = jnp.where(jax.random.bernoulli(keys[3], sign_share, (2, D)), 1.0, -1.0)
    candidate_bias = signs * jax.random.uniform(keys[4], (2, D), jnp.float32, 0.8, 1.8)
    output_bias = jax.random.uniform(keys[5], (2, D), jnp.float32, -1.0, 1.0)
    return jnp.concatenate([candidate_bias, forget_bias, output_bias], axis=1).astype(jnp.bfloat16)


def steps_of(key, dims, cuts, smallest, largest):
    loudness = 1.0
    for dim, shards_of in cuts:
        steps = jax.random.uniform(jax.random.fold_in(jax.random.fold_in(key, 6), dim), (shards_of,), jnp.float32, smallest / len(cuts), largest / len(cuts))
        loudness = loudness * jnp.repeat(jnp.exp(steps), dims[dim] // shards_of).reshape((-1,) + (1,) * (len(dims) - 1 - dim))
    return loudness


def centred(key, shape, width, most, pieces=(), dtype=jnp.bfloat16):
    level = steps_of(key, shape, pieces, -0.22, 0.18) if pieces else 1.0
    entries = jax.random.normal(key, shape, jnp.float32) * width * level
    return jnp.minimum(jnp.maximum(entries, -most), most).astype(dtype)


def setup_inputs(seed: int = 0) -> dict:
    key_of = jax.random.split(jax.random.key(seed), 6)
    return {
        "tokens_in": centred(key_of[0], (STREAMS, LENGTH, D), 1.0, 6.0, ((0, 8),)),
        "doc_starts": draw_doc_starts(jax.random.fold_in(key_of[5], 71), 0),
        "cotangent": centred(key_of[2], (STREAMS, LENGTH, D), 1.0, 6.0, ((0, 8),)),
        "tap_weight": centred(key_of[3], (4, D, 3 * D), (2 * D) ** -0.5, 0.15625, ((0, 4), (1, 8))),
        "gate_bias": draw_gate_bias(jax.random.fold_in(key_of[5], 71), 0),
    }


@jax.custom_vjp
def lower_section(v):
    return lax.optimization_barrier(v.astype(jnp.bfloat16)).astype(jnp.float32)

@jax.custom_vjp
def lower_section_backward(v):
    return v

def low_keep(v):
    return (lower_section(v), None)

def low_pass(kept, grad):
    return (grad,)

def back_keep(v):
    return (v, None)

def back_low(kept, grad):
    return (lower_section(grad),)
lower_section.defvjp(low_keep, low_pass)
lower_section_backward.defvjp(back_keep, back_low)

def fo_pool(decay, drive):

    def stepper(memory, pair):
        memory = pair[0] * memory + pair[1]
        return (memory, memory)
    initial = jnp.zeros((decay.shape[0], decay.shape[2]), jnp.float32)
    final, memory = lax.scan(jax.checkpoint(stepper), initial, (jnp.swapaxes(decay, 0, 1), jnp.swapaxes(drive, 0, 1)))
    return (jnp.swapaxes(memory, 0, 1), final)

def qrnn_layer(present_input, odd_copy, keep_mask, present_weight, preceding_weight, bias_vector_row):
    model_width = present_input.shape[-1]
    delayed_input = jnp.concatenate([jnp.zeros_like(odd_copy[:, :1]), odd_copy[:, :-1]], axis=1) * keep_mask[..., None]
    value_portion = lower_section(jnp.einsum('oyg,gq->oyq', present_input, present_weight, precision=lax.Precision.HIGHEST))
    pre_activation = lower_section_backward(jnp.einsum('oyg,gq->oyq', delayed_input, preceding_weight, precision=lax.Precision.HIGHEST) + value_portion + bias_vector_row)
    candid = jnp.tanh(pre_activation[..., :model_width])
    forget = jax.nn.sigmoid(pre_activation[..., model_width:2 * model_width])
    output_gate = jax.nn.sigmoid(pre_activation[..., 2 * model_width:])
    memory, final = fo_pool(forget * keep_mask[..., None], (1.0 - forget) * candid)
    return (lower_section(output_gate * memory), final)

def reference(tokens_in, doc_starts, cotangent, tap_weight, gate_bias):
    keep_mask = (1 - doc_starts).astype(jnp.float32)

    def forward(inputs, weights, biases):
        first, state_one = qrnn_layer(inputs, lower_section_backward(inputs), keep_mask, weights[0], weights[1], biases[0])
        rounded = lower_section_backward(first)
        second, state_two = qrnn_layer(rounded, lower_section_backward(rounded), keep_mask, weights[2], weights[3], biases[1])
        return (second, jnp.stack([state_one, state_two]))
    hidden, pull, states = jax.vjp(forward, tokens_in.astype(jnp.float32), tap_weight.astype(jnp.float32), gate_bias.astype(jnp.float32), has_aux=True)
    input_grad, weight_grad, bias_grad = pull(cotangent.astype(jnp.float32))
    return (hidden.astype(jnp.bfloat16), input_grad, weight_grad, bias_grad, states)
```

```python
import functools

import jax
import jax.numpy as jnp
from jax import lax
from jax.experimental import pallas as pl
from jax.experimental.pallas import tpu as pltpu
from jax.sharding import PartitionSpec as P

F32 = jnp.float32
BF16 = jnp.bfloat16
LANES = 128
SUBS = 8
VMEM_BYTES = 56 * 2**20
ANY = pl.BlockSpec(memory_space=pl.ANY)
VMEM = pl.BlockSpec(memory_space=pltpu.VMEM)
SMEM = pl.BlockSpec(memory_space=pltpu.SMEM)


def tiles_of(ref):
    return range(ref.shape[0])


def columns_of(tile):
    return slice(tile * LANES, (tile + 1) * LANES)


def joined(tiles):
    return jnp.concatenate(tiles, axis=1)


def row_of(ref, row):
    return joined([ref[tile, row : row + 1, :] for tile in tiles_of(ref)])


def rows_at(base, step, steps):
    return pl.ds(base + step, SUBS, stride=steps)


def forward_summary(decay, drive, base, steps):
    gains, cells = [], []
    for tile in tiles_of(decay):
        gain = jnp.ones((SUBS, LANES), F32)
        cell = jnp.zeros((SUBS, LANES), F32)
        for step in range(steps):
            here = rows_at(base, step, steps)
            now = decay[tile, here, :]
            cell = now * cell + drive[tile, here, :]
            gain = gain * now
        gains.append(gain)
        cells.append(cell)
    return joined(gains), joined(cells)


def forward_entries(gain, cell, carry):
    entries = []
    for sub in range(SUBS):
        entries.append(carry)
        carry = cell[sub : sub + 1] + gain[sub : sub + 1] * carry
    return jnp.concatenate(entries, axis=0), carry


def backward_summary(decay, emit, base, steps):
    gains, backs, first_gains, firsts = [], [], [], []
    for tile in tiles_of(decay):
        gain = jnp.ones((SUBS, LANES), F32)
        back = jnp.zeros((SUBS, LANES), F32)
        for step in reversed(range(steps)):
            here = rows_at(base, step, steps)
            now = decay[tile, here, :]
            first = emit[tile, here, :] + back
            first_gain = gain
            back = now * first
            gain = gain * now
        gains.append(gain)
        backs.append(back)
        first_gains.append(first_gain)
        firsts.append(first)
    return joined(gains), joined(backs), joined(first_gains), joined(firsts)


def backward_entries(gain, back, carry):
    entries = []
    for sub in reversed(range(SUBS)):
        entries.append(carry)
        carry = back[sub : sub + 1] + gain[sub : sub + 1] * carry
    return jnp.concatenate(entries[::-1], axis=0), carry


def backward_fill(decay, emit, base, steps, entries, out):
    for tile in tiles_of(decay):
        back = entries[:, columns_of(tile)]
        for step in reversed(range(steps)):
            here = rows_at(base, step, steps)
            now = emit[tile, here, :] + back
            out[tile, here, :] = now
            back = decay[tile, here, :] * now


def chunk_backward_summary(decay, emit, rows, block):
    width = decay.shape[0] * LANES
    steps = block // SUBS
    gain_all = jnp.ones((1, width), F32)
    back_all = jnp.zeros((1, width), F32)
    for base in reversed(range(0, rows, block)):
        gain, back, first_gain, first = backward_summary(decay, emit, base, steps)
        for sub in reversed(range(SUBS)):
            entry_gain, entry_back = gain_all, back_all
            gain_all = gain[sub : sub + 1] * entry_gain
            back_all = back[sub : sub + 1] + gain[sub : sub + 1] * entry_back
    row_gain = first_gain[0:1] * entry_gain
    row_value = first[0:1] + first_gain[0:1] * entry_back
    return gain_all, back_all, row_gain, row_value


def store_gates(pre, keep, here, candid_out, forget_out, gate_out, decay, drive, place):
    tiles = decay.shape[0]
    for tile in range(tiles):
        candid = jnp.tanh(pre[:, columns_of(tile)])
        forget = jax.nn.sigmoid(pre[:, columns_of(tiles + tile)])
        decay[tile, place, :] = forget * keep
        drive[tile, place, :] = (1.0 - forget) * candid
        if candid_out is not None:
            candid_out[tile, here, :] = candid
            forget_out[tile, here, :] = forget
            gate_out[tile, here, :] = jax.nn.sigmoid(pre[:, columns_of(2 * tiles + tile)])


class Weights:
    def __init__(self, place, layer, near, far, target, sems):
        self.place, self.layer, self.target, self.sems = place, layer, target, sems
        self.near, self.far = near, far

    def each(self, pieces, act):
        section, stream = self.place[0], self.place[1]
        width = self.target.shape[0] // 2
        for tap, masks in enumerate(pieces):
            for mask, piece in enumerate(masks):
                height = piece.shape[0]
                slot = (section % 2) ^ tap
                row = slot * width + (stream ^ mask) * height
                row = pl.multiple_of(row, 16)
                act(
                    pltpu.make_async_copy(
                        piece, self.target.at[pl.ds(row, height), :], self.sems.at[tap * len(masks) + mask]
                    )
                )

    def both(self, act):
        if self.far is None:
            width = self.target.shape[0] // 2
            for tap in range(2):
                act(
                    pltpu.make_async_copy(
                        self.near.at[2 * self.layer + tap],
                        self.target.at[pl.ds(tap * width, width), :],
                        self.sems.at[tap],
                    )
                )
            return
        is_near = self.place[0] // 2 == self.layer

        @pl.when(is_near)
        def _():
            self.each(self.near, act)

        @pl.when(jnp.logical_not(is_near))
        def _():
            self.each(self.far, act)

    def start(self):
        self.both(lambda copy: copy.start())

    def wait(self):
        self.both(lambda copy: copy.wait())


def weight_refs(refs, plan):
    if plan is None:
        return refs[0], None
    near = [refs[tap * plan : (tap + 1) * plan] for tap in range(2)]
    far = [refs[(2 + tap) * plan : (3 + tap) * plan] for tap in range(2)]
    return near, far


def weight_operands(weights):
    if isinstance(weights, jax.Array):
        return [weights], None
    return [piece for tap in weights for piece in tap], len(weights[0])


def first_forward_kernel(plan, rows, block, *refs):
    place, x_hbm, prev_hbm, keep_hbm, bias = refs[:5]
    count = 1 if plan is None else 4 * plan
    near, far = weight_refs(refs[5 : 5 + count], plan)
    (
        candid_out,
        forget_out,
        gate_out,
        cell_out,
        before_out,
        hidden_out,
        delayed_out,
        last_out,
        both,
        keep,
        matrix,
        decay,
        drive,
        delayed,
        sems,
        weight_sems,
    ) = refs[5 + count :]
    section = place[0]
    width = both.shape[1] // 2
    steps = block // SUBS
    weights = Weights(place, 0, near, far, matrix, weight_sems)
    weights.start()
    copies = [
        pltpu.make_async_copy(x_hbm, both.at[:, pl.ds(0, width)], sems.at[0]),
        pltpu.make_async_copy(prev_hbm, both.at[:, pl.ds(width, width)], sems.at[1]),
        pltpu.make_async_copy(keep_hbm, keep, sems.at[2]),
    ]
    for copy in copies:
        copy.start()
    for copy in copies:
        copy.wait()
    weights.wait()
    whole = slice(0, block)

    def earlier(index, carry):
        row = pl.multiple_of(index * block, block)
        pre = jnp.dot(
            both[pl.ds(row, block), :], matrix[:, : 2 * width], preferred_element_type=F32
        ) + bias[:, : 2 * width]
        store_gates(pre, keep[pl.ds(row, block), :], None, None, None, None, decay, drive, whole)
        gain, cell = forward_summary(decay, drive, 0, steps)
        return forward_entries(gain, cell, carry)[1]

    start = section * rows
    carry = lax.fori_loop(0, section * (rows // block), earlier, jnp.zeros((1, width), F32))
    tail = pl.multiple_of(jnp.maximum(start - 16, 0), 16)
    tail_gate = jax.nn.sigmoid(
        jnp.dot(both[pl.ds(tail, 16), :], matrix[:, 2 * width :], preferred_element_type=F32)
        + bias[:, 2 * width :]
    )
    tail_hidden = jnp.where(section > 0, tail_gate[15:16] * carry, 0.0)
    for tile in tiles_of(decay):
        delayed[tile, 0:1, :] = tail_hidden[:, columns_of(tile)]
    for base in range(0, rows, block):
        row = pl.multiple_of(start + base, block)
        here = pl.ds(base, block)
        pre = jnp.dot(both[pl.ds(row, block), :], matrix[...], preferred_element_type=F32) + bias[...]
        store_gates(
            pre, keep[pl.ds(row, block), :], here, candid_out, forget_out, gate_out, decay, drive, whole
        )
        gain, cell = forward_summary(decay, drive, 0, steps)
        entries, carry = forward_entries(gain, cell, carry)
        for tile in tiles_of(decay):
            cell = entries[:, columns_of(tile)]
            for step in range(steps):
                spot = rows_at(0, step, steps)
                out_spot = rows_at(base, step, steps)
                before_out[tile, out_spot, :] = cell
                cell = decay[tile, spot, :] * cell + drive[tile, spot, :]
                cell_out[tile, out_spot, :] = cell
                delayed[tile, rows_at(base + 1, step, steps), :] = gate_out[tile, out_spot, :] * cell
            hidden_out[here, columns_of(tile)] = (gate_out[tile, here, :] * cell_out[tile, here, :]).astype(BF16)
    for base in range(0, rows, block):
        row = pl.multiple_of(start + base, block)
        here = pl.ds(base, block)
        for tile in tiles_of(decay):
            delayed_out[here, columns_of(tile)] = (
                delayed[tile, here, :].astype(BF16).astype(F32) * keep[pl.ds(row, block), :]
            ).astype(BF16)
    last_out[...] = jnp.broadcast_to(carry, last_out.shape)


def second_forward_kernel(plan, rows, block, *refs):
    place, hidden, delayed, keep, cot, bias, last = refs[:7]
    count = 1 if plan is None else 4 * plan
    near, far = weight_refs(refs[7 : 7 + count], plan)
    (
        candid_out,
        forget_out,
        gate_out,
        summary_out,
        matrix,
        decay,
        drive,
        emit,
        weight_sems,
    ) = refs[7 + count :]
    width = hidden.shape[1]
    steps = block // SUBS
    weights = Weights(place, 1, near, far, matrix, weight_sems)
    weights.start()
    weights.wait()
    cell_all = jnp.zeros((1, width), F32)
    for base in range(0, rows, block):
        here = pl.ds(base, block)
        pre = (
            jnp.dot(hidden[here, :], matrix[:width, :], preferred_element_type=F32)
            + jnp.dot(delayed[here, :], matrix[width:, :], preferred_element_type=F32)
            + bias[...]
        )
        store_gates(pre, keep[here, :], here, candid_out, forget_out, gate_out, decay, drive, here)
        for tile in tiles_of(decay):
            emit[tile, here, :] = cot[here, columns_of(tile)].astype(F32) * gate_out[tile, here, :]
        gain, cell = forward_summary(decay, drive, base, steps)
        cell_all = forward_entries(gain, cell, cell_all)[1]
    gain_all, back_all, row_gain, row_value = chunk_backward_summary(decay, emit, rows, block)
    parts = [
        gain_all,
        cell_all,
        back_all,
        row_gain,
        row_value,
        row_of(candid_out, 0),
        row_of(forget_out, 0),
        row_of(gate_out, 0),
        last[0:1, :],
    ]
    parts += [jnp.zeros((1, width), F32)] * (16 - len(parts))
    summary_out[...] = jnp.concatenate(parts, axis=0)


def gate_grads(dcell, before, cell, candid, forget, gate, arriving):
    return (
        dcell * (1.0 - forget) * (1.0 - candid * candid),
        dcell * (before - candid) * forget * (1.0 - forget),
        arriving * cell * gate * (1.0 - gate),
    )


def pick(values, section):
    out = values[0]
    for index in range(1, len(values)):
        out = jnp.where(section == index, values[index], out)
    return out


def weight_grad_pieces(place, left, right, tap, grads, kept, sent, sems):
    grads[tap] = lax.dot_general(
        left, right, (((0,), (0,)), ((), ())), preferred_element_type=F32
    ).astype(BF16)
    if sent is None:
        return [pltpu.make_async_copy(grads.at[tap], kept.at[tap], sems.at[tap])]
    stream = place[1]
    chips, height = kept.shape[1], kept.shape[2]
    copies = []
    for side, out in enumerate((kept, sent)):
        for chip in range(chips):
            row = pl.multiple_of((stream ^ (2 * chip + side)) * height, 16)
            copies.append(
                pltpu.make_async_copy(
                    grads.at[tap, pl.ds(row, height), :],
                    out.at[tap, chip],
                    sems.at[(tap * 2 + side) * chips + chip],
                )
            )
    return copies


def heads_of(order, summaries, section):
    for index, summary in enumerate(summaries):
        order[section ^ index] = summary[...]
    return [order[index] for index in range(len(summaries))]


def back_entries(heads):
    back = jnp.zeros_like(heads[0][0:1])
    backs = []
    for head in reversed(heads):
        backs.append(back)
        back = head[2:3] + head[0:1] * back
    return backs[::-1]


def following_row(heads, backs, section, keep_firsts, cell, arriving):
    nexts = [min(index + 1, len(heads) - 1) for index in range(len(heads))]
    head = pick([heads[index] for index in nexts], section)
    back = pick([backs[index] for index in nexts], section)
    valid = jnp.where(section < len(heads) - 1, 1.0, 0.0)
    keep = pick([keep_firsts[index : index + 1, :] for index in nexts], section)
    keep = joined([keep] * (cell.shape[1] // LANES))
    candid, forget, gate = head[5:6], head[6:7], head[7:8]
    if arriving is None:
        arriving = head[1:2]
    before = keep * cell
    after = forget * before + (1.0 - forget) * candid
    dcell = (head[4:5] + head[3:4] * back) * valid
    return gate_grads(dcell, before, after, candid, forget, gate, arriving * valid)


def store_grads(
    rows, dcells, befores, cells, candid, forget, gate, arriving, keep, next_keep, extra, shifted, outs
):
    dpre_out, shifted_out, bias_out = outs
    tiles = dcells.shape[0]
    part_rows = 128
    for tile in range(tiles):
        sums = [jnp.zeros((SUBS, LANES), F32)] * 3
        for base in range(0, rows, part_rows):
            here = pl.ds(base, part_rows)
            parts = gate_grads(
                dcells[tile, here, :],
                befores[tile, here, :] * keep[here, :],
                cells[tile, here, :],
                candid[tile, here, :],
                forget[tile, here, :],
                gate[tile, here, :],
                arriving[here, columns_of(tile)].astype(F32),
            )
            for index, part in enumerate(parts):
                rounded = part.astype(BF16)
                dpre_out[here, columns_of(index * tiles + tile)] = rounded
                rounded = rounded.astype(F32)
                shifted[index, here, :] = rounded
                sums[index] = sums[index] + jnp.sum(rounded.reshape(part_rows // SUBS, SUBS, LANES), axis=0)
        for index in range(3):
            columns = columns_of(index * tiles + tile)
            after = extra[index][:, columns_of(tile)].astype(BF16).astype(F32)
            shifted[index, pl.ds(rows, SUBS), :] = jnp.broadcast_to(after, (SUBS, LANES))
            for base in range(0, rows, part_rows):
                here = pl.ds(base, part_rows)
                shifted_out[here, columns] = (
                    shifted[index, pl.ds(base + 1, part_rows), :] * next_keep[here, :]
                ).astype(BF16)
            bias_out[:, columns] = jnp.broadcast_to(
                jnp.sum(sums[index], axis=0, keepdims=True), (bias_out.shape[0], LANES)
            )


def store_weight_grads(place, left, rights, grads, kept, sent, sems):
    copies = []
    for tap, right in enumerate(rights):
        new = weight_grad_pieces(place, left[...], right[...], tap, grads, kept, sent, sems)
        for copy in new:
            copy.start()
        copies += new
    for copy in copies:
        copy.wait()


def second_backward_kernel(rows, block, has_sent, *refs):
    (place, candid, forget, gate, hidden, keep, next_keep, cot, keep_firsts) = refs[:9]
    summaries = refs[9:13]
    outs = refs[13:]
    hidden_out, dpre_out, shifted_out, bias_out, last_out, kept = outs[:6]
    sent = outs[6] if has_sent else None
    order, decay, drive, emit, cells, befores, dcells, shifted, grads, sems = outs[7 if has_sent else 6 :]
    section = place[0]
    width = hidden.shape[1]
    steps = block // SUBS
    heads = heads_of(order, summaries, section)
    carry = jnp.zeros((1, width), F32)
    carries = []
    for head in heads:
        carries.append(carry)
        carry = head[1:2] + head[0:1] * carry
    last_out[...] = jnp.concatenate(
        [jnp.broadcast_to(heads[-1][8:9], (8, width)), jnp.broadcast_to(carry, (8, width))], axis=0
    )
    backs = back_entries(heads)
    carry = pick(carries, section)
    back = pick(backs, section)
    for base in range(0, rows, block):
        here = pl.ds(base, block)
        for tile in tiles_of(decay):
            now = forget[tile, here, :]
            decay[tile, here, :] = now * keep[here, :]
            drive[tile, here, :] = (1.0 - now) * candid[tile, here, :]
            emit[tile, here, :] = cot[here, columns_of(tile)].astype(F32) * gate[tile, here, :]
        gain, cell = forward_summary(decay, drive, base, steps)
        entries, carry = forward_entries(gain, cell, carry)
        for tile in tiles_of(decay):
            cell = entries[:, columns_of(tile)]
            for step in range(steps):
                spot = rows_at(base, step, steps)
                befores[tile, spot, :] = cell
                cell = decay[tile, spot, :] * cell + drive[tile, spot, :]
                cells[tile, spot, :] = cell
            hidden_out[here, columns_of(tile)] = (gate[tile, here, :] * cells[tile, here, :]).astype(BF16)
    for base in reversed(range(0, rows, block)):
        gain, leaving, _, _ = backward_summary(decay, emit, base, steps)
        entries, back = backward_entries(gain, leaving, back)
        backward_fill(decay, emit, base, steps, entries, dcells)
    extra = following_row(heads, backs, section, keep_firsts, carry, cot[rows : rows + 16, :].astype(F32)[0:1])
    store_grads(
        rows, dcells, befores, cells, candid, forget, gate, cot, keep, next_keep, extra, shifted,
        (dpre_out, shifted_out, bias_out),
    )
    store_weight_grads(place, hidden, (dpre_out, shifted_out), grads, kept, sent, sems)


def input_grad_tile(dpre, shifted, matrix, here):
    width = matrix.shape[0] // 2
    contract = (((1,), (1,)), ((), ()))
    return lax.dot_general(
        dpre[here, :], matrix[:width, :], contract, preferred_element_type=F32
    ) + lax.dot_general(shifted[here, :], matrix[width:, :], contract, preferred_element_type=F32)


def middle_kernel(plan, rows, block, *refs):
    place, dpre, shifted, candid, forget, gate, keep = refs[:7]
    count = 1 if plan is None else 4 * plan
    near, far = weight_refs(refs[7 : 7 + count], plan)
    arriving_out, summary_out, matrix, decay, emit, weight_sems = refs[7 + count :]
    weights = Weights(place, 1, near, far, matrix, weight_sems)
    weights.start()
    weights.wait()
    for base in range(0, rows, block):
        here = pl.ds(base, block)
        arriving = input_grad_tile(dpre, shifted, matrix, here).astype(BF16)
        arriving_out[here, :] = arriving
        if base == 0:
            row_arriving = arriving.astype(F32)[0:1]
        for tile in tiles_of(decay):
            emit[tile, here, :] = arriving[:, columns_of(tile)].astype(F32) * gate[tile, here, :]
            decay[tile, here, :] = forget[tile, here, :] * keep[here, :]
    gain_all, back_all, row_gain, row_value = chunk_backward_summary(decay, emit, rows, block)
    parts = [
        gain_all,
        row_arriving,
        back_all,
        row_gain,
        row_value,
        row_of(candid, 0),
        row_of(forget, 0),
        row_of(gate, 0),
    ]
    summary_out[...] = jnp.concatenate(parts, axis=0)


def first_backward_kernel(rows, block, has_sent, *refs):
    (place, candid, forget, gate, cells, befores, last, x, keep, next_keep, arriving, keep_firsts) = refs[:12]
    summaries = refs[12:16]
    outs = refs[16:]
    dpre_out, shifted_out, bias_out, kept = outs[:4]
    sent = outs[4] if has_sent else None
    order, decay, emit, dcells, shifted, grads, sems = outs[5 if has_sent else 4 :]
    section = place[0]
    steps = block // SUBS
    heads = heads_of(order, summaries, section)
    backs = back_entries(heads)
    back = pick(backs, section)
    for base in reversed(range(0, rows, block)):
        here = pl.ds(base, block)
        for tile in tiles_of(decay):
            decay[tile, here, :] = forget[tile, here, :] * keep[here, :]
            emit[tile, here, :] = arriving[here, columns_of(tile)].astype(F32) * gate[tile, here, :]
        gain, leaving, _, _ = backward_summary(decay, emit, base, steps)
        entries, back = backward_entries(gain, leaving, back)
        backward_fill(decay, emit, base, steps, entries, dcells)
    extra = following_row(heads, backs, section, keep_firsts, last[0:1, :], None)
    store_grads(
        rows, dcells, befores, cells, candid, forget, gate, arriving, keep, next_keep, extra, shifted,
        (dpre_out, shifted_out, bias_out),
    )
    store_weight_grads(place, x, (dpre_out, shifted_out), grads, kept, sent, sems)


def last_kernel(plan, rows, block, *refs):
    place, dpre, shifted = refs[:3]
    count = 1 if plan is None else 4 * plan
    near, far = weight_refs(refs[3 : 3 + count], plan)
    out, matrix, weight_sems = refs[3 + count :]
    weights = Weights(place, 0, near, far, matrix, weight_sems)
    weights.start()
    weights.wait()
    for base in range(0, rows, block):
        here = pl.ds(base, block)
        out[here, :] = input_grad_tile(dpre, shifted, matrix, here)


def call(kernel, outs, in_specs, out_specs, scratch, flops, moved, name):
    return pl.pallas_call(
        kernel,
        out_shape=outs,
        in_specs=in_specs,
        out_specs=out_specs,
        scratch_shapes=scratch,
        compiler_params=pltpu.CompilerParams(vmem_limit_bytes=VMEM_BYTES),
        cost_estimate=pl.CostEstimate(flops=flops, bytes_accessed=moved, transcendentals=0),
        name=name,
    )


def swap(value, axis, mask):
    pairs = [(index, index ^ mask) for index in range(lax.axis_size(axis))]
    return lax.ppermute(value, axis, pairs)


def gathered_pieces(shard):
    one = swap(shard, "section", 1)
    two = swap(shard, "section", 2)
    three = swap(two, "section", 1)
    taps = []
    for index, own in enumerate((shard, one, two, three)):
        by_x = swap(own, "dp", 2)
        by_y = swap(own, "dp", 4)
        across_chip = swap(by_y, "dp", 2) if index % 2 == 0 else swap(by_x, "dp", 4)
        mine = [own, by_x, by_y, across_chip]
        taps.append([piece for one_piece in mine for piece in (one_piece, swap(one_piece, "dp", 1))])
    return taps


def total(*parts):
    return functools.reduce(jnp.add, [part.astype(F32) for part in parts]).astype(BF16)


def plane_sums(kept, sent):
    other = swap(sent, "dp", 1)
    sums = [[total(kept[tap, chip], other[tap, chip]) for chip in range(4)] for tap in range(2)]
    by_x = swap(sums[0][3], "dp", 2)
    by_y = swap(sums[1][3], "dp", 4)
    sums[0][2] = total(sums[0][2], by_x)
    sums[1][1] = total(sums[1][1], by_y)
    return [
        total(sums[tap][0], swap(sums[tap][1], "dp", 2), swap(sums[tap][2], "dp", 4)) for tap in range(2)
    ]


def all_sums(value):
    for axis in ("dp", "section"):
        mask = 1
        while mask < lax.axis_size(axis):
            value = value + swap(value, axis, mask)
            mask *= 2
    return value


def per_device(tokens_in, doc_starts, cotangent, tap_weight, gate_bias):
    sections = lax.axis_size("section")
    streams = lax.axis_size("dp")
    section = lax.axis_index("section")
    stream = lax.axis_index("dp")
    _, length, width = tokens_in.shape
    gates = 3 * width
    rows = length // sections
    block = 256
    start = section * rows
    height = tap_weight.shape[1]
    quick = sections == 4 and streams == 8 and height % 16 == 0

    if quick:
        near_far = gathered_pieces(tap_weight[0])
    else:
        near_far = lax.all_gather(
            lax.all_gather(tap_weight, "dp", axis=1, tiled=True), "section", axis=0, tiled=True
        )
    weights, plan = weight_operands(near_far)
    weight_count = 1 if plan is None else 2 * plan

    x = tokens_in[0]
    keep = (1 - doc_starts[0]).astype(F32)
    keep_column = jnp.broadcast_to(keep[:, None], (length, LANES))
    x_before = jnp.concatenate([jnp.zeros_like(x[:1]), x[:-1]], axis=0) * keep[:, None].astype(BF16)
    place = jnp.stack([section, stream]).astype(jnp.int32)
    bias = gate_bias.astype(F32)
    keep_after = jnp.concatenate([keep_column[1:], jnp.zeros((1, LANES), F32)], axis=0)
    keep_firsts = jnp.concatenate([keep_column[::rows], jnp.zeros((8 - sections, LANES), F32)], axis=0)

    def own(value):
        return lax.dynamic_slice_in_dim(value, start, rows, 0)

    keep_own, keep_next, x_own = own(keep_column), own(keep_after), own(x)
    cot = cotangent[0]
    cot_next = lax.dynamic_slice_in_dim(cot, jnp.minimum(start + rows, length - rows), 16, 0)
    cot_own = jnp.concatenate([own(cot), cot_next], axis=0)

    def shape(*dims, dtype=F32):
        return jax.ShapeDtypeStruct(dims, dtype)

    def buffer(*dims, dtype=F32):
        return pltpu.VMEM(dims, dtype)

    dma = pltpu.SemaphoreType.DMA
    layer_flops = 2 * rows * width * gates * 2
    weight_bytes = 4 * width * gates
    half = shape(rows, width, dtype=BF16)
    tiles = width // LANES
    full = shape(tiles, rows, LANES)
    matrix = buffer(2 * width, gates, dtype=BF16)

    candid0, forget0, gate0, cells0, befores0, hidden0, delayed0, last0 = call(
        functools.partial(first_forward_kernel, plan, rows, block),
        [full] * 5 + [half] * 2 + [shape(8, width)],
        [SMEM, ANY, ANY, ANY, VMEM] + [ANY] * len(weights),
        [VMEM] * 8,
        [
            buffer(length, 2 * width, dtype=BF16),
            buffer(length, LANES),
            matrix,
            buffer(tiles, block, LANES),
            buffer(tiles, block, LANES),
            buffer(tiles, rows + 8, LANES),
            dma((3,)),
            dma((weight_count + 1,)),
        ],
        2 * layer_flops,
        weight_bytes + 30 * rows * width,
        "first_forward",
    )(place, x, x_before, keep_column, bias[0:1], *weights)

    candid1, forget1, gate1, summary1 = call(
        functools.partial(second_forward_kernel, plan, rows, block),
        [full] * 3 + [shape(16, width)],
        [SMEM] + [VMEM] * 6 + [ANY] * len(weights),
        [VMEM] * 4,
        [matrix] + [buffer(tiles, rows, LANES)] * 3 + [dma((weight_count + 1,))],
        layer_flops,
        weight_bytes + 20 * rows * width,
        "second_forward",
    )(place, hidden0, delayed0, keep_own, cot_own, bias[1:2], last0, *weights)

    def exchanged(summary):
        one = swap(summary, "section", 1)
        pair = swap(jnp.stack([summary, one]), "section", 2)
        return [summary, one, pair[0], pair[1]]

    if quick:
        kept_shape = [shape(2, 4, height, gates, dtype=BF16)] * 2
        grad_sems = dma((16,))
    else:
        kept_shape = [shape(2, width, gates, dtype=BF16)]
        grad_sems = dma((2,))
    wide = shape(rows, gates, dtype=BF16)
    grads = buffer(2, width, gates, dtype=BF16)

    hidden1, dpre1, shifted1, bias1, lasts, *kept1 = call(
        functools.partial(second_backward_kernel, rows, block, quick),
        [half, wide, wide, shape(8, gates), shape(16, width)] + kept_shape,
        [SMEM] + [VMEM] * 12,
        [VMEM] * 5 + [ANY] * len(kept_shape),
        [buffer(sections, 16, width)]
        + [buffer(tiles, rows, LANES)] * 6
        + [buffer(3, rows + 8, LANES), grads, grad_sems],
        layer_flops,
        weight_bytes + 30 * rows * width,
        "second_backward",
    )(place, candid1, forget1, gate1, hidden0, keep_own, keep_next, cot_own, keep_firsts, *exchanged(summary1))

    arriving, summary0 = call(
        functools.partial(middle_kernel, plan, rows, block),
        [half, shape(8, width)],
        [SMEM] + [VMEM] * 6 + [ANY] * len(weights),
        [VMEM] * 2,
        [matrix] + [buffer(tiles, rows, LANES)] * 2 + [dma((weight_count + 1,))],
        layer_flops,
        weight_bytes + 20 * rows * width,
        "middle",
    )(place, dpre1, shifted1, candid0, forget0, gate0, keep_own, *weights)

    dpre0, shifted0, bias0, *kept0 = call(
        functools.partial(first_backward_kernel, rows, block, quick),
        [wide, wide, shape(8, gates)] + kept_shape,
        [SMEM] + [VMEM] * 15,
        [VMEM] * 3 + [ANY] * len(kept_shape),
        [buffer(sections, 8, width)]
        + [buffer(tiles, rows, LANES)] * 3
        + [buffer(3, rows + 8, LANES), grads, grad_sems],
        layer_flops,
        weight_bytes + 30 * rows * width,
        "first_backward",
    )(
        place,
        candid0,
        forget0,
        gate0,
        cells0,
        befores0,
        last0,
        x_own,
        keep_own,
        keep_next,
        arriving,
        keep_firsts,
        *exchanged(summary0),
    )

    input_grad = call(
        functools.partial(last_kernel, plan, rows, block),
        shape(rows, width),
        [SMEM, VMEM, VMEM] + [ANY] * len(weights),
        VMEM,
        [matrix, dma((weight_count + 1,))],
        layer_flops,
        weight_bytes + 20 * rows * width,
        "last",
    )(place, dpre0, shifted0, *weights)

    bias_grad = all_sums(jnp.concatenate([bias0[0:1], bias1[0:1]], axis=0))
    if quick:
        sums = [plane_sums(*kept0), plane_sums(*kept1)]
        odd = section % 2 == 1
        pairs = []
        for first, second in sums:
            mine = jnp.where(odd, second, first)
            sent = jnp.where(odd, first, second)
            pairs.append(total(mine, swap(sent, "section", 1)))
        upper = section >= 2
        mine = jnp.where(upper, pairs[1], pairs[0])
        sent = jnp.where(upper, pairs[0], pairs[1])
        weight_grad = (mine.astype(F32) + swap(sent, "section", 2).astype(F32))[None]
    else:
        stacked = jnp.concatenate([kept0[0], kept1[0]], axis=0)
        by_rows = lax.psum_scatter(stacked, "dp", scatter_dimension=1, tiled=True)
        weight_grad = lax.psum_scatter(by_rows, "section", scatter_dimension=0, tiled=True).astype(F32)
    last_states = lasts[::8][:, None, :]
    return (hidden1[None], input_grad[None], weight_grad, bias_grad, last_states)


def solution(mesh):
    in_specs = (
        P("dp", None, None),
        P("dp", None),
        P("dp", None, None),
        P("section", "dp", None),
        P(),
    )
    out_specs = (
        P("dp", "section", None),
        P("dp", "section", None),
        P("section", "dp", None),
        P(),
        P(None, "dp", None),
    )
    return jax.shard_map(
        per_device, mesh=mesh, in_specs=in_specs, out_specs=out_specs, check_vma=False
    )
```

```python
import functools

import jax
import jax.numpy as jnp
from jax import lax
from jax.experimental import pallas as pl
from jax.experimental.pallas import tpu as pltpu
from jax.sharding import PartitionSpec as P

F32 = jnp.float32
BF16 = jnp.bfloat16
LANES = 128
SUBS = 8
BIAS_ROWS = 16
UNROLL = 16
LIMITS = (30, 22, 28, 18, 28, 16)
ANY = pl.BlockSpec(memory_space=pl.ANY)
HBM = pl.BlockSpec(memory_space=pltpu.HBM)
VMEM = pl.BlockSpec(memory_space=pltpu.VMEM)
SMEM = pl.BlockSpec(memory_space=pltpu.SMEM)


def tiles_of(ref):
    return range(ref.shape[0])


def columns_of(tile):
    return slice(tile * LANES, (tile + 1) * LANES)


def joined(tiles):
    return jnp.concatenate(tiles, axis=1)


def first_row(ref):
    return joined([ref[tile, 0:1, :] for tile in tiles_of(ref)])


def ones_and_zeros(tiles):
    return [jnp.ones((SUBS, LANES), F32)] * tiles, [jnp.zeros((SUBS, LANES), F32)] * tiles


def over_steps(steps, body, state):
    def turn(index, state):
        for part in range(UNROLL):
            state = body(index * UNROLL + part, state)
        return state

    return lax.fori_loop(0, steps // UNROLL, turn, state)


def group(step):
    row = step * SUBS
    return pl.ds(row if isinstance(row, int) else pl.multiple_of(row, SUBS), SUBS)


def forward_steps(candid, forget, keep, first, steps, gains, cells):
    def body(step, state):
        gains, cells = state
        spot = group(first + step)
        kept = keep[spot, :]
        new_gains, new_cells = [], []
        for tile, (gain, cell) in enumerate(zip(gains, cells, strict=True)):
            share = forget[tile, spot, :]
            now = share * kept
            new_cells.append(now * cell + (1.0 - share) * candid[tile, spot, :])
            new_gains.append(gain * now)
        return new_gains, new_cells

    return over_steps(steps, body, (list(gains), list(cells)))


def forward_entries(gains, cells, carry):
    gain, cell = joined(gains), joined(cells)
    entries = []
    for sub in range(SUBS):
        entries.append(carry)
        carry = cell[sub : sub + 1] + gain[sub : sub + 1] * carry
    return jnp.concatenate(entries, axis=0), carry


def forward_fill(candid, forget, keep, steps, entries, out):
    cells = [entries[:, columns_of(tile)] for tile in tiles_of(out)]
    for tile in tiles_of(out):
        out[tile, group(0), :] = cells[tile]

    def body(step, cells):
        spot = group(step)
        kept = keep[spot, :]
        new_cells = []
        for tile, cell in enumerate(cells):
            share = forget[tile, spot, :]
            cell = share * kept * cell + (1.0 - share) * candid[tile, spot, :]
            out[tile, group(step + 1), :] = cell
            new_cells.append(cell)
        return new_cells

    over_steps(steps, body, cells)


def backward_steps(forget, keep, emit, steps):
    tiles = emit.shape[0]

    def body(step, state):
        gains, backs = state
        spot = group(steps - 1 - step)
        kept = keep[spot, :]
        new_gains, new_backs = [], []
        for tile, (gain, back) in enumerate(zip(gains, backs, strict=True)):
            now = forget[tile, spot, :] * kept
            new_backs.append(now * (emit[tile, spot, :] + back))
            new_gains.append(gain * now)
        return new_gains, new_backs

    state = ones_and_zeros(tiles)
    whole = (steps - 1) // UNROLL * UNROLL
    state = over_steps(whole, body, state)
    for step in range(whole, steps - 1):
        state = body(step, state)
    first_gains, backs = state
    firsts = [emit[tile, group(0), :] + backs[tile] for tile in range(tiles)]
    gains, backs = body(steps - 1, state)
    return joined(gains), joined(backs), joined(first_gains), joined(firsts)


def backward_entries(gain, back, carry):
    entries = []
    for sub in reversed(range(SUBS)):
        entries.append(carry)
        carry = back[sub : sub + 1] + gain[sub : sub + 1] * carry
    return jnp.concatenate(entries[::-1], axis=0)


def backward_fill(forget, keep, emit, steps, entries):
    def body(step, backs):
        spot = group(steps - 1 - step)
        kept = keep[spot, :]
        new_backs = []
        for tile, back in enumerate(backs):
            now = emit[tile, spot, :] + back
            emit[tile, spot, :] = now
            new_backs.append(forget[tile, spot, :] * kept * now)
        return new_backs

    over_steps(steps, body, [entries[:, columns_of(tile)] for tile in tiles_of(emit)])


def chunk_backward_summary(forget, keep, emit, steps):
    gain, back, first_gain, first = backward_steps(forget, keep, emit, steps)
    gain_all = jnp.ones_like(gain[0:1])
    back_all = jnp.zeros_like(gain[0:1])
    for sub in reversed(range(SUBS)):
        entry_gain, entry_back = gain_all, back_all
        gain_all = gain[sub : sub + 1] * entry_gain
        back_all = back[sub : sub + 1] + gain[sub : sub + 1] * entry_back
    row_gain = first_gain[0:1] * entry_gain
    row_value = first[0:1] + first_gain[0:1] * entry_back
    return gain_all, back_all, row_gain, row_value


def store_gates(pre, here, candid_out, forget_out, gate_out):
    tiles = candid_out.shape[0]
    for tile in range(tiles):
        candid_out[tile, here, :] = jnp.tanh(pre[:, columns_of(tile)])
        forget_out[tile, here, :] = jax.nn.sigmoid(pre[:, columns_of(tiles + tile)])
        if gate_out is not None:
            gate_out[tile, here, :] = jax.nn.sigmoid(pre[:, columns_of(2 * tiles + tile)])


class Weights:
    def __init__(self, place, layer, near, far, target, sems):
        self.place, self.layer, self.target, self.sems = place, layer, target, sems
        self.near, self.far = near, far

    def each(self, pieces, act):
        section, stream = self.place[0], self.place[1]
        width = self.target.shape[0] // 2
        for tap, masks in enumerate(pieces):
            for mask, piece in enumerate(masks):
                height = piece.shape[0]
                slot = (section % 2) ^ tap
                row = slot * width + (stream ^ mask) * height
                row = pl.multiple_of(row, 16)
                act(
                    pltpu.make_async_copy(
                        piece, self.target.at[pl.ds(row, height), :], self.sems.at[tap * len(masks) + mask]
                    )
                )

    def both(self, act):
        if self.far is None:
            width = self.target.shape[0] // 2
            for tap in range(2):
                act(
                    pltpu.make_async_copy(
                        self.near.at[2 * self.layer + tap],
                        self.target.at[pl.ds(tap * width, width), :],
                        self.sems.at[tap],
                    )
                )
            return
        is_near = self.place[0] // 2 == self.layer

        @pl.when(is_near)
        def _():
            self.each(self.near, act)

        @pl.when(jnp.logical_not(is_near))
        def _():
            self.each(self.far, act)

    def start(self):
        self.both(lambda copy: copy.start())

    def wait(self):
        self.both(lambda copy: copy.wait())


def weight_refs(refs, plan):
    if plan is None:
        return refs[0], None
    near = [refs[tap * plan : (tap + 1) * plan] for tap in range(2)]
    far = [refs[(2 + tap) * plan : (3 + tap) * plan] for tap in range(2)]
    return near, far


def weight_operands(weights):
    if isinstance(weights, jax.Array):
        return [weights], None
    return [piece for tap in weights for piece in tap], len(weights[0])


def first_forward_kernel(plan, rows, block, *refs):
    place, x, prev, keep, bias = refs[:5]
    count = 1 if plan is None else 4 * plan
    near, far = weight_refs(refs[5 : 5 + count], plan)
    (
        candid_out,
        forget_out,
        gate_out,
        cell_out,
        hidden_out,
        delayed_out,
        last_out,
        matrix,
        delayed,
        weight_sems,
    ) = refs[-10:]
    section = place[0]
    width = x.shape[1]
    tiles = delayed.shape[0]
    block_steps = block // SUBS
    steps = rows // SUBS
    weights = Weights(place, 0, near, far, matrix, weight_sems)
    weights.start()
    weights.wait()

    def pre_of(row, height, first, last):
        here = pl.ds(row, height)
        return (
            jnp.dot(x[here, :], matrix[:width, first:last], preferred_element_type=F32)
            + jnp.dot(prev[here, :], matrix[width:, first:last], preferred_element_type=F32)
            + bias[:, first:last]
        )

    def earlier(index, carry):
        chunk = pl.multiple_of(index * rows, rows)
        keep_chunk = keep.at[pl.ds(chunk, rows), :]

        def part(index, state):
            base = pl.multiple_of(index * block, block)
            pre = pre_of(pl.multiple_of(chunk + base, block), block, 0, 2 * width)
            store_gates(pre, pl.ds(base, block), candid_out, forget_out, None)
            return forward_steps(candid_out, forget_out, keep_chunk, index * block_steps, block_steps, *state)

        gains, cells = lax.fori_loop(0, rows // block, part, ones_and_zeros(tiles))
        return forward_entries(gains, cells, carry)[1]

    start = pl.multiple_of(section * rows, rows)
    keep_own = keep.at[pl.ds(start, rows), :]
    carry = lax.fori_loop(0, section, earlier, jnp.zeros((1, width), F32))
    tail = pl.multiple_of(jnp.maximum(start - 16, 0), 16)
    tail_gate = jax.nn.sigmoid(pre_of(tail, 16, 2 * width, 3 * width))
    tail_hidden = jnp.where(section > 0, tail_gate[15:16] * carry, 0.0)

    def part(index, state):
        base = pl.multiple_of(index * block, block)
        pre = pre_of(pl.multiple_of(start + base, block), block, 0, 3 * width)
        store_gates(pre, pl.ds(base, block), candid_out, forget_out, gate_out)
        return forward_steps(candid_out, forget_out, keep_own, index * block_steps, block_steps, *state)

    gains, cells = lax.fori_loop(0, rows // block, part, ones_and_zeros(tiles))
    entries, carry = forward_entries(gains, cells, carry)
    forward_fill(candid_out, forget_out, keep_own, steps, entries, cell_out)
    for tile in range(tiles):
        delayed[tile, pl.ds(SUBS, rows), :] = gate_out[tile, :, :] * cell_out[tile, pl.ds(SUBS, rows), :]
        delayed[tile, group(0), :] = jnp.concatenate(
            [tail_hidden[:, columns_of(tile)], delayed[tile, rows : rows + SUBS - 1, :]], axis=0
        )
        hidden_out[:, columns_of(tile)] = delayed[tile, pl.ds(SUBS, rows), :].astype(BF16)
        delayed_out[:, columns_of(tile)] = (
            delayed[tile, pl.ds(0, rows), :].astype(BF16).astype(F32) * keep_own[...]
        ).astype(BF16)
    last_out[...] = jnp.broadcast_to(carry, last_out.shape)


def second_forward_kernel(plan, rows, block, *refs):
    place, hidden, delayed, keep, cot, bias, last = refs[:7]
    count = 1 if plan is None else 4 * plan
    near, far = weight_refs(refs[7 : 7 + count], plan)
    candid_out, forget_out, gate_out, summary_out, matrix, emit, weight_sems = refs[7 + count :]
    width = hidden.shape[1]
    tiles = emit.shape[0]
    block_steps = block // SUBS
    weights = Weights(place, 1, near, far, matrix, weight_sems)
    weights.start()
    weights.wait()

    def part(index, state):
        here = pl.ds(pl.multiple_of(index * block, block), block)
        pre = (
            jnp.dot(hidden[here, :], matrix[:width, :], preferred_element_type=F32)
            + jnp.dot(delayed[here, :], matrix[width:, :], preferred_element_type=F32)
            + bias[...]
        )
        store_gates(pre, here, candid_out, forget_out, gate_out)
        for tile in range(tiles):
            emit[tile, here, :] = cot[here, columns_of(tile)].astype(F32) * gate_out[tile, here, :]
        return forward_steps(candid_out, forget_out, keep, index * block_steps, block_steps, *state)

    gains, cells = lax.fori_loop(0, rows // block, part, ones_and_zeros(tiles))
    cell_all = forward_entries(gains, cells, jnp.zeros((1, width), F32))[1]
    gain_all, back_all, row_gain, row_value = chunk_backward_summary(forget_out, keep, emit, rows // SUBS)
    parts = [
        gain_all,
        cell_all,
        back_all,
        row_gain,
        row_value,
        first_row(candid_out),
        first_row(forget_out),
        first_row(gate_out),
        last[0:1, :],
    ]
    parts += [jnp.zeros((1, width), F32)] * (16 - len(parts))
    summary_out[...] = jnp.concatenate(parts, axis=0)


def gate_grads(dcell, before, cell, candid, forget, gate, arriving):
    return (
        dcell * (1.0 - forget) * (1.0 - candid * candid),
        dcell * (before - candid) * forget * (1.0 - forget),
        arriving * cell * gate * (1.0 - gate),
    )


def pick(values, section):
    out = values[0]
    for index in range(1, len(values)):
        out = jnp.where(section == index, values[index], out)
    return out


def store_weight_grads(place, lefts, right, kept, sent):
    for tap, left in enumerate(lefts):
        grads = lax.dot_general(left, right, (((0,), (0,)), ((), ())), preferred_element_type=F32).astype(BF16)
        if sent is None:
            kept[tap] = grads
            continue
        chips, height = kept.shape[1], kept.shape[2]
        stream = place[1]
        odd = stream % 2 == 1
        for chip in range(chips):
            even_rows = grads[2 * chip * height : (2 * chip + 1) * height]
            odd_rows = grads[(2 * chip + 1) * height : (2 * chip + 2) * height]
            kept[tap, chip ^ (stream // 2)] = jnp.where(odd, odd_rows, even_rows)
            sent[tap, chip ^ (stream // 2)] = jnp.where(odd, even_rows, odd_rows)


def heads_of(order, summaries, section):
    for index, summary in enumerate(summaries):
        order[section ^ index] = summary[...]
    return [order[index] for index in range(len(summaries))]


def back_entries(heads):
    back = jnp.zeros_like(heads[0][0:1])
    backs = []
    for head in reversed(heads):
        backs.append(back)
        back = head[2:3] + head[0:1] * back
    return backs[::-1]


def following_row(heads, backs, section, keep_firsts, cell, arriving):
    nexts = [min(index + 1, len(heads) - 1) for index in range(len(heads))]
    head = pick([heads[index] for index in nexts], section)
    back = pick([backs[index] for index in nexts], section)
    valid = jnp.where(section < len(heads) - 1, 1.0, 0.0)
    keep = pick([keep_firsts[index : index + 1, :] for index in nexts], section)
    keep = joined([keep] * (cell.shape[1] // LANES))
    candid, forget, gate = head[5:6], head[6:7], head[7:8]
    if arriving is None:
        arriving = head[1:2]
    before = keep * cell
    after = forget * before + (1.0 - forget) * candid
    dcell = (head[4:5] + head[3:4] * back) * valid
    return gate_grads(dcell, before, after, candid, forget, gate, arriving * valid), keep


def store_grads(rows, dcells, cells, candid, forget, gate, arriving, keep, next_first, extra, shifted, outs):
    dpre_out, shifted_out, bias_out, after = outs
    tiles = dcells.shape[0]
    width = tiles * LANES
    part_rows = 64
    for index in range(3):
        rounded = extra[index].astype(BF16).astype(F32) * joined([next_first[:, :LANES]] * tiles)
        after[:, index * width : (index + 1) * width] = jnp.broadcast_to(rounded, (SUBS, width))

    def of_tile(tile, carry):
        def of_rows(part, sums):
            base = pl.multiple_of(part * part_rows, part_rows)
            here = pl.ds(base, part_rows)
            kept = keep[here, :]
            parts = gate_grads(
                dcells[tile, here, :],
                cells[tile, here, :] * kept,
                cells[tile, pl.ds(pl.multiple_of(base + SUBS, SUBS), part_rows), :],
                candid[tile, here, :],
                forget[tile, here, :],
                gate[tile, here, :],
                arriving[here, pl.ds(pl.multiple_of(tile * LANES, LANES), LANES)].astype(F32),
            )
            new_sums = []
            for index, part in enumerate(parts):
                rounded = part.astype(BF16)
                columns = pl.ds(pl.multiple_of((index * tiles + tile) * LANES, LANES), LANES)
                dpre_out[here, columns] = rounded
                rounded = rounded.astype(F32)
                shifted[index, here, :] = rounded * kept
                new_sums.append(
                    sums[index] + jnp.sum(rounded.reshape(part_rows // SUBS, SUBS, LANES), axis=0)
                )
            return new_sums

        sums = lax.fori_loop(0, rows // part_rows, of_rows, [jnp.zeros((SUBS, LANES), F32)] * 3)
        for index in range(3):
            columns = pl.ds(pl.multiple_of((index * tiles + tile) * LANES, LANES), LANES)
            shifted[index, pl.ds(rows, SUBS), :] = jnp.concatenate(
                [shifted[index, 1:SUBS, :], after[0:1, columns]], axis=0
            )
            shifted_out[:, columns] = shifted[index, pl.ds(SUBS, rows), :].astype(BF16)
            bias_out[:, columns] = jnp.broadcast_to(
                jnp.sum(sums[index], axis=0, keepdims=True), (bias_out.shape[0], LANES)
            )
        return carry

    lax.fori_loop(0, tiles, of_tile, 0)


def second_backward_kernel(rows, has_sent, *refs):
    (place, candid, forget, gate, hidden, delayed, keep, cot, cot_next, keep_firsts) = refs[:10]
    summaries = refs[10:14]
    outs = refs[14:]
    hidden_out, dpre_out, shifted_out, bias_out, last_out, kept = outs[:6]
    sent = outs[6] if has_sent else None
    order, cells, dcells, shifted, after = outs[7 if has_sent else 6 :]
    section = place[0]
    width = hidden.shape[1]
    tiles = dcells.shape[0]
    steps = rows // SUBS
    heads = heads_of(order, summaries, section)
    carry = jnp.zeros((1, width), F32)
    carries = []
    for head in heads:
        carries.append(carry)
        carry = head[1:2] + head[0:1] * carry
    last_out[0] = heads[-1][8:9]
    last_out[1] = carry
    backs = back_entries(heads)
    carry = pick(carries, section)
    back = pick(backs, section)
    for tile in range(tiles):
        dcells[tile, :, :] = cot[:, columns_of(tile)].astype(F32) * gate[tile, :, :]
    gains, ends = forward_steps(candid, forget, keep, 0, steps, *ones_and_zeros(tiles))
    entries, carry = forward_entries(gains, ends, carry)
    forward_fill(candid, forget, keep, steps, entries, cells)
    for tile in range(tiles):
        hidden_out[:, columns_of(tile)] = (gate[tile, :, :] * cells[tile, pl.ds(SUBS, rows), :]).astype(BF16)
    gain, leaving, _, _ = backward_steps(forget, keep, dcells, steps)
    backward_fill(forget, keep, dcells, steps, backward_entries(gain, leaving, back))
    extra, next_first = following_row(heads, backs, section, keep_firsts, carry, cot_next[...].astype(F32)[0:1])
    store_grads(
        rows, dcells, cells, candid, forget, gate, cot, keep, next_first, extra, shifted,
        (dpre_out, shifted_out, bias_out, after),
    )
    store_weight_grads(place, (hidden[...], delayed[...]), dpre_out[...], kept, sent)


def input_grad_tile(dpre, shifted, matrix, here):
    width = matrix.shape[0] // 2
    contract = (((1,), (1,)), ((), ()))
    return lax.dot_general(
        dpre[here, :], matrix[:width, :], contract, preferred_element_type=F32
    ) + lax.dot_general(shifted[here, :], matrix[width:, :], contract, preferred_element_type=F32)


def middle_kernel(rows, block, *refs):
    place, dpre, shifted, candid, forget, gate, keep, matrix = refs[:8]
    arriving_out, summary_out, emit = refs[8:]

    def part(index, carry):
        here = pl.ds(pl.multiple_of(index * block, block), block)
        arriving = input_grad_tile(dpre, shifted, matrix, here).astype(BF16)
        arriving_out[here, :] = arriving
        for tile in tiles_of(emit):
            emit[tile, here, :] = arriving[:, columns_of(tile)].astype(F32) * gate[tile, here, :]
        return carry

    lax.fori_loop(0, rows // block, part, 0)
    row_arriving = arriving_out[0:16, :].astype(F32)[0:1]
    gain_all, back_all, row_gain, row_value = chunk_backward_summary(forget, keep, emit, rows // SUBS)
    parts = [
        gain_all,
        row_arriving,
        back_all,
        row_gain,
        row_value,
        first_row(candid),
        first_row(forget),
        first_row(gate),
    ]
    summary_out[...] = jnp.concatenate(parts, axis=0)


def first_backward_kernel(rows, has_sent, *refs):
    (place, candid, forget, gate, cells, last, x, prev, keep, arriving, keep_firsts, other_bias) = refs[:12]
    summaries = refs[12:16]
    order, dcells, shifted, after = refs[-4:]
    outs = refs[-9:-4] if has_sent else refs[-8:-4]
    dpre_out, shifted_out, bias_out, kept = outs[:4]
    sent = outs[4] if has_sent else None
    section = place[0]
    steps = rows // SUBS
    heads = heads_of(order, summaries, section)
    backs = back_entries(heads)
    back = pick(backs, section)
    for tile in tiles_of(dcells):
        dcells[tile, :, :] = arriving[:, columns_of(tile)].astype(F32) * gate[tile, :, :]
    gain, leaving, _, _ = backward_steps(forget, keep, dcells, steps)
    backward_fill(forget, keep, dcells, steps, backward_entries(gain, leaving, back))
    extra, next_first = following_row(heads, backs, section, keep_firsts, last[0:1, :], None)
    store_grads(
        rows, dcells, cells, candid, forget, gate, arriving, keep, next_first, extra, shifted,
        (dpre_out, shifted_out, bias_out.at[pl.ds(0, SUBS), :], after),
    )
    bias_out[SUBS:, :] = other_bias[...]
    store_weight_grads(place, (x[...], prev[...]), dpre_out[...], kept, sent)


def last_kernel(rows, block, *refs):
    dpre, shifted, matrix, out = refs

    def part(index, carry):
        here = pl.ds(pl.multiple_of(index * block, block), block)
        out[here, :] = input_grad_tile(dpre, shifted, matrix, here)
        return carry

    lax.fori_loop(0, rows // block, part, 0)


def added(*parts):
    return functools.reduce(jnp.add, [part.astype(F32) for part in parts])


def bias_rows(bias):
    rows = []
    for row in (bias[0:1], bias[SUBS : SUBS + 1]):
        high = row.astype(BF16).astype(F32)
        rows += [high, row - high]
    rows.append(jnp.zeros((BIAS_ROWS - len(rows), bias.shape[1]), F32))
    return jnp.concatenate(rows, axis=0).astype(BF16)


def bias_of(rows):
    rows = rows.astype(F32)
    return jnp.concatenate([rows[0:1] + rows[1:2], rows[2:3] + rows[3:4]], axis=0)


def sum_in_order(order, values, position):
    for index, value in enumerate(values):
        order[position ^ index] = value
    out = order[0]
    for index in range(1, len(values)):
        out = out + order[index]
    return out


def corner_kernel(has_bias, *refs):
    if has_bias:
        kept, got, bias, got_bias = refs[:4]
        rows = bias_rows(bias[...] + got_bias[...])
    else:
        kept, got = refs[:2]
    by_x, by_y = refs[-2:]
    height = kept.shape[2]
    for tap, out in enumerate((by_x, by_y)):
        out[0:height, :] = added(kept[tap, 3], got[tap, 3]).astype(BF16)
        if has_bias:
            out[height:, :] = rows


def sides_kernel(has_bias, *refs):
    kept, got, from_x, from_y = refs[:4]
    by_x, by_y = refs[-2:]
    height = kept.shape[2]
    for tap in range(2):
        here = pl.ds(tap * height, height)
        parts = [kept[tap, 1], got[tap, 1]] + ([from_y[0:height, :]] if tap == 1 else [])
        by_x[here, :] = added(*parts).astype(BF16)
        parts = [kept[tap, 2], got[tap, 2]] + ([from_x[0:height, :]] if tap == 0 else [])
        by_y[here, :] = added(*parts).astype(BF16)
    if has_bias:
        by_x[2 * height :, :] = from_y[height:, :]


def plane_kernel(has_bias, *refs):
    if has_bias:
        place, kept, got, from_x, from_y, bias, got_bias, corner_x, corner_y = refs[:9]
        out, order = refs[-2:]
    else:
        kept, got, from_x, from_y = refs[:4]
        out = refs[-1]
    height = kept.shape[2]
    for tap in range(2):
        here = pl.ds(tap * height, height)
        out[here, :] = added(kept[tap, 0], got[tap, 0], from_x[here, :], from_y[here, :]).astype(BF16)
    if has_bias:
        parts = [bias_rows(bias[...] + got_bias[...]), corner_x[height:, :], corner_y[height:, :], from_x[2 * height :, :]]
        whole = sum_in_order(order, [bias_of(part) for part in parts], place[1] // 2)
        whole = jnp.concatenate([whole[0:1]] * SUBS + [whole[1:2]] * SUBS, axis=0)
        out[2 * height :, :] = bias_rows(whole)


def messages_kernel(*refs):
    place, first, second = refs[:3]
    outs = refs[-3:]
    height = (first.shape[0] - BIAS_ROWS) // 2
    for index, out in enumerate(outs):
        to = place[0] ^ (index + 1)
        row = pl.ds(pl.multiple_of((to % 2) * height, 16), height)

        @pl.when(to < 2)
        def _(out=out, row=row):
            out[0:height, :] = first[row, :]

        @pl.when(to >= 2)
        def _(out=out, row=row):
            out[0:height, :] = second[row, :]

        out[height:, :] = first[2 * height :, :]


def whole_kernel(*refs):
    place, first, second = refs[:3]
    got = refs[3:6]
    out, bias_out, order = refs[-3:]
    section = place[0]
    height = out.shape[0]
    row = pl.ds(pl.multiple_of((section % 2) * height, 16), height)
    rest = added(*[part[0:height, :] for part in got])

    @pl.when(section < 2)
    def _():
        out[...] = first[row, :].astype(F32) + rest

    @pl.when(section >= 2)
    def _():
        out[...] = second[row, :].astype(F32) + rest

    parts = [first[2 * height :, :]] + [part[height:, :] for part in got]
    bias_out[...] = sum_in_order(order, [bias_of(part) for part in parts], section)


def call(kernel, outs, in_specs, out_specs, scratch, flops, moved, megabytes, name):
    return pl.pallas_call(
        kernel,
        out_shape=outs,
        in_specs=in_specs,
        out_specs=out_specs,
        scratch_shapes=scratch,
        compiler_params=pltpu.CompilerParams(vmem_limit_bytes=megabytes * 2**20),
        cost_estimate=pl.CostEstimate(flops=flops, bytes_accessed=moved, transcendentals=0),
        name=name,
    )


def small_call(kernel, outs, operands, name, ties=(), scratch=()):
    has_place = operands[0].dtype == jnp.int32
    specs = [SMEM if has_place and index == 0 else VMEM for index in range(len(operands))]
    return call(
        kernel,
        outs,
        specs + [ANY] * len(ties),
        [VMEM] * len(outs),
        list(scratch),
        1000000,
        1000000,
        12,
        name,
    )(*operands, *ties)


def swap(value, axis, mask):
    pairs = [(index, index ^ mask) for index in range(lax.axis_size(axis))]
    return lax.ppermute(value, axis, pairs)


def gathered_pieces(shard):
    one = swap(shard, "section", 1)
    two = swap(shard, "section", 2)
    three = swap(two, "section", 1)
    taps = []
    for index, own in enumerate((shard, one, two, three)):
        by_x = swap(own, "dp", 2)
        by_y = swap(own, "dp", 4)
        across_chip = swap(by_y, "dp", 2) if index % 2 == 0 else swap(by_x, "dp", 4)
        mine = [own, by_x, by_y, across_chip]
        taps.append([piece for one_piece in mine for piece in (one_piece, swap(one_piece, "dp", 1))])
    return taps


class LayerSum:
    def __init__(self, kept, sent, bias=None, place=None):
        self.kept, self.got = kept, swap(sent, "dp", 1)
        self.bias, self.place = bias, place
        self.got_bias = None if bias is None else swap(bias, "dp", 1)
        self.height, self.gates = kept.shape[2], kept.shape[3]
        self.extra = 0 if bias is None else BIAS_ROWS

    def rows(self, taps, extra):
        return jax.ShapeDtypeStruct((taps * self.height + extra, self.gates), BF16)

    def has_bias(self):
        return self.bias is not None

    def corners(self, ties=()):
        operands = [self.kept, self.got] + ([self.bias, self.got_bias] if self.has_bias() else [])
        by_x, by_y = small_call(
            functools.partial(corner_kernel, self.has_bias()), [self.rows(1, self.extra)] * 2, operands, "corners", ties
        )
        self.corner_x, self.corner_y = swap(by_x, "dp", 2), swap(by_y, "dp", 4)

    def sides(self, ties=()):
        by_x, by_y = small_call(
            functools.partial(sides_kernel, self.has_bias()),
            [self.rows(2, self.extra), self.rows(2, 0)],
            [self.kept, self.got, self.corner_x, self.corner_y],
            "sides",
            ties,
        )
        self.by = (by_x, by_y)
        self.side_x, self.side_y = swap(by_x, "dp", 2), swap(by_y, "dp", 4)

    def plane(self, ties=()):
        operands = [self.kept, self.got, self.side_x, self.side_y]
        scratch = []
        if self.has_bias():
            operands = [self.place, *operands, self.bias, self.got_bias, self.corner_x, self.corner_y]
            scratch = [pltpu.VMEM((4, 2, self.gates), F32)]
        (out,) = small_call(
            functools.partial(plane_kernel, self.has_bias()), [self.rows(2, self.extra)], operands, "plane", ties, scratch
        )
        return out


def whole_sums(place, first, second, ties=()):
    height = (first.shape[0] - BIAS_ROWS) // 2
    gates = first.shape[1]
    message = jax.ShapeDtypeStruct((height + BIAS_ROWS, gates), BF16)
    sent = small_call(messages_kernel, [message] * 3, [place, first, second], "messages", ties)
    got = [swap(part, "section", index + 1) for index, part in enumerate(sent)]
    return small_call(
        whole_kernel,
        [jax.ShapeDtypeStruct((height, gates), F32), jax.ShapeDtypeStruct((2, gates), F32)],
        [place, first, second, *got],
        "whole",
        scratch=[pltpu.VMEM((4, 2, gates), F32)],
    )


def all_sums(value):
    for axis in ("dp", "section"):
        mask = 1
        while mask < lax.axis_size(axis):
            value = value + swap(value, axis, mask)
            mask *= 2
    return value


def grouped(value, rows):
    length, width = value.shape
    return value.reshape(length // rows, SUBS, rows // SUBS, width).swapaxes(1, 2).reshape(length, width)


def ungrouped(value):
    rows, width = value.shape
    return value.reshape(rows // SUBS, SUBS, width).swapaxes(0, 1).reshape(rows, width)


def per_device(tokens_in, doc_starts, cotangent, tap_weight, gate_bias):
    sections = lax.axis_size("section")
    streams = lax.axis_size("dp")
    section = lax.axis_index("section")
    stream = lax.axis_index("dp")
    _, length, width = tokens_in.shape
    gates = 3 * width
    tiles = width // LANES
    rows = length // sections
    block = 256
    start = section * rows
    height = tap_weight.shape[1]
    quick = sections == 4 and streams == 8 and height % 16 == 0

    if quick:
        near_far = gathered_pieces(tap_weight[0])
    else:
        near_far = lax.all_gather(
            lax.all_gather(tap_weight, "dp", axis=1, tiled=True), "section", axis=0, tiled=True
        )
    weights, plan = weight_operands(near_far)
    weight_count = 1 if plan is None else 2 * plan

    def own(value):
        return lax.dynamic_slice_in_dim(value, start, rows, 0)

    keep = (1 - doc_starts[0]).astype(F32)[:, None]
    x_before = jnp.concatenate([jnp.zeros_like(tokens_in[0, :1]), tokens_in[0, :-1]], axis=0)
    x = grouped(tokens_in[0], rows)
    prev = grouped(x_before * keep.astype(BF16), rows)
    keep_all = grouped(jnp.broadcast_to(keep, (length, LANES)), rows)
    keep_firsts = jnp.concatenate([keep_all[::rows], jnp.zeros((8 - sections, LANES), F32)], axis=0)
    keep_own, x_own, prev_own = own(keep_all), own(x), own(prev)
    place = jnp.stack([section, stream]).astype(jnp.int32)
    bias = gate_bias.astype(F32)
    cot = grouped(own(cotangent[0]), rows)
    cot_next = lax.dynamic_slice_in_dim(cotangent[0], jnp.minimum(start + rows, length - 16), 16, 0)

    def shape(*dims, dtype=F32):
        return jax.ShapeDtypeStruct(dims, dtype)

    def buffer(*dims, dtype=F32):
        return pltpu.VMEM(dims, dtype)

    dma = pltpu.SemaphoreType.DMA
    layer_flops = 2 * rows * width * gates * 2
    weight_bytes = 4 * width * gates
    half = shape(rows, width, dtype=BF16)
    full = shape(tiles, rows, LANES)
    scan = buffer(tiles, rows, LANES)
    matrix = shape(2 * width, gates, dtype=BF16)

    early = [keep_firsts, keep_own, x_own, prev_own, cot, cot_next]
    candid0, forget0, gate0, cells0, hidden0, delayed0, last0, matrix0 = call(
        functools.partial(first_forward_kernel, plan, rows, block),
        [full] * 3 + [shape(tiles, rows + SUBS, LANES)] + [half] * 2 + [shape(8, width), matrix],
        [SMEM] + [VMEM] * 4 + [HBM] * len(weights) + [ANY] * len(early),
        [VMEM] * 8,
        [buffer(tiles, rows + SUBS, LANES), dma((weight_count + 1,))],
        2 * layer_flops,
        weight_bytes + 30 * rows * width,
        LIMITS[0],
        "first_forward",
    )(place, x, prev, keep_all, bias[0:1], *weights, *early)

    candid1, forget1, gate1, summary1, matrix1 = call(
        functools.partial(second_forward_kernel, plan, rows, block),
        [full] * 3 + [shape(16, width), matrix],
        [SMEM] + [VMEM] * 6 + [HBM] * len(weights),
        [VMEM] * 5,
        [scan, dma((weight_count + 1,))],
        layer_flops,
        weight_bytes + 20 * rows * width,
        LIMITS[1],
        "second_forward",
    )(place, hidden0, delayed0, keep_own, cot, bias[1:2], last0, *weights)

    def exchanged(summary):
        return [summary] + [swap(summary, "section", index) for index in range(1, sections)]

    if quick:
        kept_shape = [shape(2, 4, height, gates, dtype=BF16)] * 2
    else:
        kept_shape = [shape(2, width, gates, dtype=BF16)]
    wide = shape(rows, gates, dtype=BF16)

    hidden1, dpre1, shifted1, bias1, lasts, *kept1 = call(
        functools.partial(second_backward_kernel, rows, quick),
        [half, wide, wide, shape(8, gates), shape(2, 1, width)] + kept_shape,
        [SMEM] + [VMEM] * 13,
        [VMEM] * (5 + len(kept_shape)),
        [buffer(sections, 16, width), buffer(tiles, rows + SUBS, LANES), scan, buffer(3, rows + SUBS, LANES), buffer(SUBS, gates)],
        layer_flops,
        weight_bytes + 30 * rows * width,
        LIMITS[2],
        "second_backward",
    )(
        place, candid1, forget1, gate1, hidden0, delayed0, keep_own, cot, cot_next, keep_firsts,
        *exchanged(summary1),
    )

    if quick:
        second = LayerSum(*kept1)
        second.corners()

    arriving, summary0 = call(
        functools.partial(middle_kernel, rows, block),
        [half, shape(8, width)],
        [SMEM] + [VMEM] * 7,
        [VMEM] * 2,
        [scan],
        layer_flops,
        weight_bytes + 20 * rows * width,
        LIMITS[3],
        "middle",
    )(place, dpre1, shifted1, candid0, forget0, gate0, keep_own, matrix1)

    ties = []
    if quick:
        second.sides()
        ties = second.by
    dpre0, shifted0, bias_both, *kept0 = call(
        functools.partial(first_backward_kernel, rows, quick),
        [wide, wide, shape(2 * SUBS, gates)] + kept_shape,
        [SMEM] + [VMEM] * 15 + [ANY] * len(ties),
        [VMEM] * (3 + len(kept_shape)),
        [buffer(sections, 8, width), scan, buffer(3, rows + SUBS, LANES), buffer(SUBS, gates)],
        layer_flops,
        weight_bytes + 30 * rows * width,
        LIMITS[4],
        "first_backward",
    )(
        place, candid0, forget0, gate0, cells0, last0, x_own, prev_own, keep_own, arriving, keep_firsts, bias1,
        *exchanged(summary0), *ties,
    )
    if quick:
        plane1 = second.plane()

    input_grad = call(
        functools.partial(last_kernel, rows, block),
        shape(rows, width),
        [VMEM] * 3,
        VMEM,
        [],
        layer_flops,
        weight_bytes + 20 * rows * width,
        LIMITS[5],
        "last",
    )(dpre0, shifted0, matrix0)

    if quick:
        first = LayerSum(*kept0, bias_both, place)
        first.corners(ties=[plane1, input_grad])
        first.sides()
        weight_grad, bias_grad = whole_sums(place, first.plane(), plane1)
        weight_grad = weight_grad[None]
    else:
        bias_grad = all_sums(bias_both[::8])
        stacked = jnp.concatenate([kept0[0], kept1[0]], axis=0)
        by_rows = lax.psum_scatter(stacked, "dp", scatter_dimension=1, tiled=True)
        weight_grad = lax.psum_scatter(by_rows, "section", scatter_dimension=0, tiled=True).astype(F32)
    return (ungrouped(hidden1)[None], ungrouped(input_grad)[None], weight_grad, bias_grad, lasts)


def solution(mesh):
    in_specs = (
        P("dp", None, None),
        P("dp", None),
        P("dp", None, None),
        P("section", "dp", None),
        P(),
    )
    out_specs = (
        P("dp", "section", None),
        P("dp", "section", None),
        P("section", "dp", None),
        P(),
        P(None, "dp", None),
    )
    return jax.shard_map(
        per_device, mesh=mesh, in_specs=in_specs, out_specs=out_specs, check_vma=False
    )
```

```python
import functools

import jax
import jax.numpy as jnp
from jax import lax
from jax.experimental import pallas as pl
from jax.experimental.pallas import tpu as pltpu
from jax.sharding import PartitionSpec as P

F32 = jnp.float32
BF16 = jnp.bfloat16
LANES = 128
SUBS = 8
BIAS_ROWS = 16
COST = 100
UNROLL = 16
LIMITS = (22, 28, 28, 18, 28, 16)
ANY = pl.BlockSpec(memory_space=pl.ANY)
HBM = pl.BlockSpec(memory_space=pltpu.HBM)
VMEM = pl.BlockSpec(memory_space=pltpu.VMEM)
SMEM = pl.BlockSpec(memory_space=pltpu.SMEM)


def tiles_of(ref):
    return range(ref.shape[0])


def columns_of(tile):
    return slice(tile * LANES, (tile + 1) * LANES)


def joined(tiles):
    return jnp.concatenate(tiles, axis=1)


def first_row(ref):
    return joined([ref[tile, 0:1, :] for tile in tiles_of(ref)])


def ones_and_zeros(tiles):
    return [jnp.ones((SUBS, LANES), F32)] * tiles, [jnp.zeros((SUBS, LANES), F32)] * tiles


def over_steps(steps, body, state):
    def turn(index, state):
        for part in range(UNROLL):
            state = body(index * UNROLL + part, state)
        return state

    return lax.fori_loop(0, steps // UNROLL, turn, state)


def group(step):
    row = step * SUBS
    return pl.ds(row if isinstance(row, int) else pl.multiple_of(row, SUBS), SUBS)


def forward_steps(candid, forget, keep, first, steps, gains, cells):
    def body(step, state):
        gains, cells = state
        spot = group(first + step)
        kept = keep[spot, :]
        new_gains, new_cells = [], []
        for tile, (gain, cell) in enumerate(zip(gains, cells, strict=True)):
            share = forget[tile, spot, :]
            now = share * kept
            new_cells.append(now * cell + (1.0 - share) * candid[tile, spot, :])
            new_gains.append(gain * now)
        return new_gains, new_cells

    return over_steps(steps, body, (list(gains), list(cells)))


def forward_entries(gains, cells, carry):
    gain, cell = joined(gains), joined(cells)
    entries = []
    for sub in range(SUBS):
        entries.append(carry)
        carry = cell[sub : sub + 1] + gain[sub : sub + 1] * carry
    return jnp.concatenate(entries, axis=0), carry


def forward_fill(candid, forget, keep, steps, entries, out):
    cells = [entries[:, columns_of(tile)] for tile in tiles_of(out)]
    for tile in tiles_of(out):
        out[tile, group(0), :] = cells[tile]

    def body(step, cells):
        spot = group(step)
        kept = keep[spot, :]
        new_cells = []
        for tile, cell in enumerate(cells):
            share = forget[tile, spot, :]
            cell = share * kept * cell + (1.0 - share) * candid[tile, spot, :]
            out[tile, group(step + 1), :] = cell
            new_cells.append(cell)
        return new_cells

    over_steps(steps, body, cells)


def backward_steps(forget, keep, emit, steps):
    tiles = emit.shape[0]

    def body(step, state):
        gains, backs = state
        spot = group(steps - 1 - step)
        kept = keep[spot, :]
        new_gains, new_backs = [], []
        for tile, (gain, back) in enumerate(zip(gains, backs, strict=True)):
            now = forget[tile, spot, :] * kept
            new_backs.append(now * (emit[tile, spot, :] + back))
            new_gains.append(gain * now)
        return new_gains, new_backs

    state = ones_and_zeros(tiles)
    whole = (steps - 1) // UNROLL * UNROLL
    state = over_steps(whole, body, state)
    for step in range(whole, steps - 1):
        state = body(step, state)
    first_gains, backs = state
    firsts = [emit[tile, group(0), :] + backs[tile] for tile in range(tiles)]
    gains, backs = body(steps - 1, state)
    return joined(gains), joined(backs), joined(first_gains), joined(firsts)


def backward_entries(gain, back, carry):
    entries = []
    for sub in reversed(range(SUBS)):
        entries.append(carry)
        carry = back[sub : sub + 1] + gain[sub : sub + 1] * carry
    return jnp.concatenate(entries[::-1], axis=0)


def backward_fill(forget, keep, emit, steps, entries):
    def body(step, backs):
        spot = group(steps - 1 - step)
        kept = keep[spot, :]
        new_backs = []
        for tile, back in enumerate(backs):
            now = emit[tile, spot, :] + back
            emit[tile, spot, :] = now
            new_backs.append(forget[tile, spot, :] * kept * now)
        return new_backs

    over_steps(steps, body, [entries[:, columns_of(tile)] for tile in tiles_of(emit)])


def chunk_backward_summary(forget, keep, emit, steps):
    gain, back, first_gain, first = backward_steps(forget, keep, emit, steps)
    gain_all = jnp.ones_like(gain[0:1])
    back_all = jnp.zeros_like(gain[0:1])
    for sub in reversed(range(SUBS)):
        entry_gain, entry_back = gain_all, back_all
        gain_all = gain[sub : sub + 1] * entry_gain
        back_all = back[sub : sub + 1] + gain[sub : sub + 1] * entry_back
    row_gain = first_gain[0:1] * entry_gain
    row_value = first[0:1] + first_gain[0:1] * entry_back
    return gain_all, back_all, row_gain, row_value


def store_gates(pre, here, candid_out, forget_out, gate_out):
    tiles = candid_out.shape[0]
    for tile in range(tiles):
        candid_out[tile, here, :] = jnp.tanh(pre[:, columns_of(tile)])
        forget_out[tile, here, :] = jax.nn.sigmoid(pre[:, columns_of(tiles + tile)])
        if gate_out is not None:
            gate_out[tile, here, :] = jax.nn.sigmoid(pre[:, columns_of(2 * tiles + tile)])


class Weights:
    def __init__(self, place, layer, near, far, target, sems):
        self.place, self.layer, self.target, self.sems = place, layer, target, sems
        self.near, self.far = near, far

    def each(self, pieces, act):
        section, core, chip = self.place[0], self.place[1] % 2, self.place[1] // 2
        width = self.target.shape[0] // 2
        height = pieces[0].shape[0]
        places = []
        for tap in range(2):
            places += [(tap, chip), (tap, chip ^ (2 - core)), (tap, chip ^ (1 + core))]
        places += [(core, chip ^ 3), (1 - core, chip ^ 3)]
        for index, (piece, (tap, rows)) in enumerate(zip(pieces, places, strict=True)):
            row = ((section % 2) ^ tap) * width + rows * height
            target = self.target.at[pl.ds(pl.multiple_of(row, 16), height), :]
            act(pltpu.make_async_copy(piece, target, self.sems.at[index]))

    def both(self, act):
        if self.far is None:
            width = self.target.shape[0] // 2
            for tap in range(2):
                act(
                    pltpu.make_async_copy(
                        self.near.at[2 * self.layer + tap],
                        self.target.at[pl.ds(tap * width, width), :],
                        self.sems.at[tap],
                    )
                )
            return
        is_near = self.place[0] // 2 == self.layer

        @pl.when(is_near)
        def _():
            self.each(self.near, act)

        @pl.when(jnp.logical_not(is_near))
        def _():
            self.each(self.far, act)

    def start(self):
        self.both(lambda copy: copy.start())

    def wait(self):
        self.both(lambda copy: copy.wait())


def weight_refs(refs, count):
    if count == 1:
        return refs[0], None
    return refs[: count // 2], refs[count // 2 : count]


def join_kernel(place, own, got, *refs):
    out = refs[-1]
    height = own.shape[0]
    core = place[1] % 2
    out[pl.ds(pl.multiple_of(core * height, 16), height), :] = own[...]
    out[pl.ds(pl.multiple_of((1 - core) * height, 16), height), :] = got[...]


def pick_kernel(place, first, second, out):
    @pl.when(place[1] % 2 == 0)
    def _():
        out[...] = first[...]

    @pl.when(place[1] % 2 == 1)
    def _():
        out[...] = second[...]


def before_kernel(*refs):
    place, x, tail, keep = refs[:4]
    prev, shifted = refs[-2:]
    rows, width = x.shape
    top = jnp.where(place[0] > 0, tail[...].astype(F32)[15:16], 0.0)
    for tile in range(width // LANES):
        columns = columns_of(tile)
        shifted[tile, pl.ds(SUBS, rows), :] = x[:, columns].astype(F32)
        shifted[tile, group(0), :] = jnp.concatenate(
            [top[:, columns], shifted[tile, rows : rows + SUBS - 1, :]], axis=0
        )
        prev[:, columns] = (shifted[tile, pl.ds(0, rows), :] * keep[...]).astype(BF16)


def forward_gates(x, prev, matrix, bias, keep, block, candid_out, forget_out, gate_out, finish=None):
    rows, width = x.shape
    tiles = candid_out.shape[0]
    block_steps = block // SUBS

    def part(index, state):
        here = pl.ds(pl.multiple_of(index * block, block), block)
        pre = (
            jnp.dot(x[here, :], matrix[:width, :], preferred_element_type=F32)
            + jnp.dot(prev[here, :], matrix[width:, :], preferred_element_type=F32)
            + bias[...]
        )
        store_gates(pre, here, candid_out, forget_out, gate_out)
        if finish is not None:
            finish(here)
        return forward_steps(candid_out, forget_out, keep, index * block_steps, block_steps, *state)

    return lax.fori_loop(0, rows // block, part, ones_and_zeros(tiles))


def first_forward_kernel(plan, block, *refs):
    place, x, prev, keep, bias = refs[:5]
    near, far = weight_refs(refs[5:], plan)
    candid_out, forget_out, gate_out, summary_out, matrix, weight_sems = refs[5 + plan :]
    rows, width = x.shape
    weights = Weights(place, 0, near, far, matrix, weight_sems)
    weights.start()
    weights.wait()
    gains, cells = forward_gates(x, prev, matrix, bias, keep, block, candid_out, forget_out, gate_out)
    gain_all, cell_all = jnp.ones((1, width), F32), jnp.zeros((1, width), F32)
    gain, cell = joined(gains), joined(cells)
    for sub in range(SUBS):
        cell_all = cell[sub : sub + 1] + gain[sub : sub + 1] * cell_all
        gain_all = gain[sub : sub + 1] * gain_all
    last_gate = joined([gate_out[tile, rows - 1 : rows, :] for tile in tiles_of(gate_out)])
    parts = [gain_all, cell_all, last_gate] + [jnp.zeros((1, width), F32)] * 5
    summary_out[...] = jnp.concatenate(parts, axis=0)


def second_forward_kernel(plan, block, *refs):
    place, candid, forget, gate, keep, cot, bias = refs[:7]
    summaries = refs[7:11]
    near, far = weight_refs(refs[11:], plan)
    (
        cell_out,
        hidden,
        delayed,
        last,
        candid_out,
        forget_out,
        gate_out,
        summary_out,
        matrix,
        order,
        emit,
        shifted,
        weight_sems,
    ) = refs[11 + plan :]
    section = place[0]
    rows, width = hidden.shape
    tiles = emit.shape[0]
    steps = rows // SUBS
    weights = Weights(place, 1, near, far, matrix, weight_sems)
    weights.start()

    heads = heads_of(order, summaries, section)
    carry = jnp.zeros((1, width), F32)
    carries, hiddens = [], [jnp.zeros((1, width), F32)]
    for head in heads:
        carries.append(carry)
        carry = head[1:2] + head[0:1] * carry
        hiddens.append(head[2:3] * carry)
    gains, cells = forward_steps(candid, forget, keep, 0, steps, *ones_and_zeros(tiles))
    entries, carry = forward_entries(gains, cells, pick(carries, section))
    last[...] = jnp.broadcast_to(carry, last.shape)
    forward_fill(candid, forget, keep, steps, entries, cell_out)
    top = pick(hiddens[:-1], section)
    for tile in range(tiles):
        columns = columns_of(tile)
        shifted[tile, pl.ds(SUBS, rows), :] = gate[tile, :, :] * cell_out[tile, pl.ds(SUBS, rows), :]
        shifted[tile, group(0), :] = jnp.concatenate(
            [top[:, columns], shifted[tile, rows : rows + SUBS - 1, :]], axis=0
        )
        hidden[:, columns] = shifted[tile, pl.ds(SUBS, rows), :].astype(BF16)
        delayed[:, columns] = (shifted[tile, pl.ds(0, rows), :].astype(BF16).astype(F32) * keep[...]).astype(BF16)

    weights.wait()

    def emitted(here):
        for tile in range(tiles):
            emit[tile, here, :] = cot[here, columns_of(tile)].astype(F32) * gate_out[tile, here, :]

    gains, cells = forward_gates(
        hidden, delayed, matrix, bias, keep, block, candid_out, forget_out, gate_out, emitted
    )
    cell_all = forward_entries(gains, cells, jnp.zeros((1, width), F32))[1]
    gain_all, back_all, row_gain, row_value = chunk_backward_summary(forget_out, keep, emit, steps)
    parts = [
        gain_all,
        cell_all,
        back_all,
        row_gain,
        row_value,
        first_row(candid_out),
        first_row(forget_out),
        first_row(gate_out),
        last[0:1, :],
    ]
    parts += [jnp.zeros((1, width), F32)] * (16 - len(parts))
    summary_out[...] = jnp.concatenate(parts, axis=0)


def gate_grads(dcell, before, cell, candid, forget, gate, arriving):
    return (
        dcell * (1.0 - forget) * (1.0 - candid * candid),
        dcell * (before - candid) * forget * (1.0 - forget),
        arriving * cell * gate * (1.0 - gate),
    )


def pick(values, section):
    out = values[0]
    for index in range(1, len(values)):
        out = jnp.where(section == index, values[index], out)
    return out


def first_weights_kernel(first, *refs):
    place, x, prev, dpre = refs[:4]
    kept, sent = refs[-2:]
    store_weight_grads(place, (x[...], prev[...]), dpre[:, first:], kept, sent)


def store_weight_grads(place, lefts, right, kept, sent):
    for tap, left in enumerate(lefts):
        grads = lax.dot_general(left, right, (((0,), (0,)), ((), ())), preferred_element_type=F32).astype(BF16)
        if sent is None:
            kept[tap] = grads
            continue
        chips, height = kept.shape[1], kept.shape[2]
        stream = place[1]
        odd = stream % 2 == 1
        for chip in range(chips):
            even_rows = grads[2 * chip * height : (2 * chip + 1) * height]
            odd_rows = grads[(2 * chip + 1) * height : (2 * chip + 2) * height]
            kept[tap, chip ^ (stream // 2)] = jnp.where(odd, odd_rows, even_rows)
            sent[tap, chip ^ (stream // 2)] = jnp.where(odd, even_rows, odd_rows)


def heads_of(order, summaries, section):
    for index, summary in enumerate(summaries):
        order[section ^ index] = summary[...]
    return [order[index] for index in range(len(summaries))]


def back_entries(heads):
    back = jnp.zeros_like(heads[0][0:1])
    backs = []
    for head in reversed(heads):
        backs.append(back)
        back = head[2:3] + head[0:1] * back
    return backs[::-1]


def following_row(heads, backs, section, keep_firsts, cell, arriving):
    nexts = [min(index + 1, len(heads) - 1) for index in range(len(heads))]
    head = pick([heads[index] for index in nexts], section)
    back = pick([backs[index] for index in nexts], section)
    valid = jnp.where(section < len(heads) - 1, 1.0, 0.0)
    keep = pick([keep_firsts[index : index + 1, :] for index in nexts], section)
    keep = joined([keep] * (cell.shape[1] // LANES))
    candid, forget, gate = head[5:6], head[6:7], head[7:8]
    if arriving is None:
        arriving = head[1:2]
    before = keep * cell
    after = forget * before + (1.0 - forget) * candid
    dcell = (head[4:5] + head[3:4] * back) * valid
    return gate_grads(dcell, before, after, candid, forget, gate, arriving * valid), keep


def store_grads(rows, dcells, cells, candid, forget, gate, arriving, keep, next_first, extra, shifted, outs):
    dpre_out, shifted_out, bias_out, after = outs
    tiles = dcells.shape[0]
    width = tiles * LANES
    part_rows = 64
    for index in range(3):
        rounded = extra[index].astype(BF16).astype(F32) * joined([next_first[:, :LANES]] * tiles)
        after[:, index * width : (index + 1) * width] = jnp.broadcast_to(rounded, (SUBS, width))

    def of_tile(tile, carry):
        def of_rows(part, sums):
            base = pl.multiple_of(part * part_rows, part_rows)
            here = pl.ds(base, part_rows)
            kept = keep[here, :]
            parts = gate_grads(
                dcells[tile, here, :],
                cells[tile, here, :] * kept,
                cells[tile, pl.ds(pl.multiple_of(base + SUBS, SUBS), part_rows), :],
                candid[tile, here, :],
                forget[tile, here, :],
                gate[tile, here, :],
                arriving[here, pl.ds(pl.multiple_of(tile * LANES, LANES), LANES)].astype(F32),
            )
            new_sums = []
            for index, part in enumerate(parts):
                rounded = part.astype(BF16)
                columns = pl.ds(pl.multiple_of((index * tiles + tile) * LANES, LANES), LANES)
                dpre_out[here, columns] = rounded
                rounded = rounded.astype(F32)
                shifted[index, here, :] = rounded * kept
                new_sums.append(
                    sums[index] + jnp.sum(rounded.reshape(part_rows // SUBS, SUBS, LANES), axis=0)
                )
            return new_sums

        sums = lax.fori_loop(0, rows // part_rows, of_rows, [jnp.zeros((SUBS, LANES), F32)] * 3)
        for index in range(3):
            columns = pl.ds(pl.multiple_of((index * tiles + tile) * LANES, LANES), LANES)
            shifted[index, pl.ds(rows, SUBS), :] = jnp.concatenate(
                [shifted[index, 1:SUBS, :], after[0:1, columns]], axis=0
            )
            shifted_out[:, columns] = shifted[index, pl.ds(SUBS, rows), :].astype(BF16)
            bias_out[:, columns] = jnp.broadcast_to(
                jnp.sum(sums[index], axis=0, keepdims=True), (bias_out.shape[0], LANES)
            )
        return carry

    lax.fori_loop(0, tiles, of_tile, 0)


def second_backward_kernel(rows, has_sent, *refs):
    (place, candid, forget, gate, hidden, delayed, keep, cot, cot_next, keep_firsts) = refs[:10]
    summaries = refs[10:14]
    outs = refs[14:]
    hidden_out, dpre_out, shifted_out, bias_out, last_out, kept = outs[:6]
    sent = outs[6] if has_sent else None
    order, cells, dcells, shifted, after = outs[7 if has_sent else 6 :]
    section = place[0]
    width = hidden.shape[1]
    tiles = dcells.shape[0]
    steps = rows // SUBS
    heads = heads_of(order, summaries, section)
    carry = jnp.zeros((1, width), F32)
    carries = []
    for head in heads:
        carries.append(carry)
        carry = head[1:2] + head[0:1] * carry
    last_out[0] = heads[-1][8:9]
    last_out[1] = carry
    backs = back_entries(heads)
    carry = pick(carries, section)
    back = pick(backs, section)
    for tile in range(tiles):
        dcells[tile, :, :] = cot[:, columns_of(tile)].astype(F32) * gate[tile, :, :]
    gains, ends = forward_steps(candid, forget, keep, 0, steps, *ones_and_zeros(tiles))
    entries, carry = forward_entries(gains, ends, carry)
    forward_fill(candid, forget, keep, steps, entries, cells)
    for tile in range(tiles):
        hidden_out[:, columns_of(tile)] = (gate[tile, :, :] * cells[tile, pl.ds(SUBS, rows), :]).astype(BF16)
    gain, leaving, _, _ = backward_steps(forget, keep, dcells, steps)
    backward_fill(forget, keep, dcells, steps, backward_entries(gain, leaving, back))
    extra, next_first = following_row(heads, backs, section, keep_firsts, carry, cot_next[...].astype(F32)[0:1])
    store_grads(
        rows, dcells, cells, candid, forget, gate, cot, keep, next_first, extra, shifted,
        (dpre_out, shifted_out, bias_out, after),
    )
    store_weight_grads(place, (hidden[...], delayed[...]), dpre_out[...], kept, sent)


def input_grad_tile(dpre, shifted, matrix, here):
    width = matrix.shape[0] // 2
    contract = (((1,), (1,)), ((), ()))
    return lax.dot_general(
        dpre[here, :], matrix[:width, :], contract, preferred_element_type=F32
    ) + lax.dot_general(shifted[here, :], matrix[width:, :], contract, preferred_element_type=F32)


def middle_kernel(rows, block, *refs):
    place, dpre, shifted, candid, forget, gate, keep, matrix = refs[:8]
    arriving_out, summary_out, emit = refs[8:]

    def part(index, carry):
        here = pl.ds(pl.multiple_of(index * block, block), block)
        arriving = input_grad_tile(dpre, shifted, matrix, here).astype(BF16)
        arriving_out[here, :] = arriving
        for tile in tiles_of(emit):
            emit[tile, here, :] = arriving[:, columns_of(tile)].astype(F32) * gate[tile, here, :]
        return carry

    lax.fori_loop(0, rows // block, part, 0)
    row_arriving = arriving_out[0:16, :].astype(F32)[0:1]
    gain_all, back_all, row_gain, row_value = chunk_backward_summary(forget, keep, emit, rows // SUBS)
    parts = [
        gain_all,
        row_arriving,
        back_all,
        row_gain,
        row_value,
        first_row(candid),
        first_row(forget),
        first_row(gate),
    ]
    summary_out[...] = jnp.concatenate(parts, axis=0)


def first_backward_kernel(rows, has_sent, *refs):
    (place, candid, forget, gate, cells, last, x, prev, keep, arriving, keep_firsts, other_bias) = refs[:12]
    summaries = refs[12:16]
    order, dcells, shifted, after = refs[-4:]
    outs = refs[-9:-4] if has_sent else refs[-8:-4]
    dpre_out, shifted_out, bias_out, kept = outs[:4]
    sent = outs[4] if has_sent else None
    section = place[0]
    steps = rows // SUBS
    heads = heads_of(order, summaries, section)
    backs = back_entries(heads)
    back = pick(backs, section)
    for tile in tiles_of(dcells):
        dcells[tile, :, :] = arriving[:, columns_of(tile)].astype(F32) * gate[tile, :, :]
    gain, leaving, _, _ = backward_steps(forget, keep, dcells, steps)
    backward_fill(forget, keep, dcells, steps, backward_entries(gain, leaving, back))
    extra, next_first = following_row(heads, backs, section, keep_firsts, last[0:1, :], None)
    store_grads(
        rows, dcells, cells, candid, forget, gate, arriving, keep, next_first, extra, shifted,
        (dpre_out, shifted_out, bias_out.at[pl.ds(0, SUBS), :], after),
    )
    bias_out[SUBS:, :] = other_bias[...]
    store_weight_grads(place, (x[...], prev[...]), dpre_out[:, : kept.shape[-1]], kept, sent)


def last_kernel(rows, block, *refs):
    dpre, shifted, matrix, out = refs

    def part(index, carry):
        here = pl.ds(pl.multiple_of(index * block, block), block)
        out[here, :] = input_grad_tile(dpre, shifted, matrix, here)
        return carry

    lax.fori_loop(0, rows // block, part, 0)


def added(*parts):
    return functools.reduce(jnp.add, [part.astype(F32) for part in parts])


def bias_rows(bias):
    rows = []
    for row in (bias[0:1], bias[SUBS : SUBS + 1]):
        high = row.astype(BF16).astype(F32)
        rows += [high, row - high]
    rows.append(jnp.zeros((BIAS_ROWS - len(rows), bias.shape[1]), F32))
    return jnp.concatenate(rows, axis=0).astype(BF16)


def bias_of(rows):
    rows = rows.astype(F32)
    return jnp.concatenate([rows[0:1] + rows[1:2], rows[2:3] + rows[3:4]], axis=0)


def sum_in_order(order, values, position):
    for index, value in enumerate(values):
        order[position ^ index] = value
    out = order[0]
    for index in range(1, len(values)):
        out = out + order[index]
    return out


def corner_kernel(columns, *refs):
    kept, got = refs[:2]
    by_x, by_y = refs[-2:]
    height = kept.shape[2]
    for tap, out in enumerate((by_x, by_y)):
        out[0:height, :] = added(kept[tap, 3], got[tap, 3]).astype(BF16)
    if columns is not None:
        bias, got_bias = refs[2:4]
        rows = bias_rows(bias[:, columns] + got_bias[:, columns])
        for out in (by_x, by_y):
            out[height:, :] = rows


def sides_kernel(columns, *refs):
    kept, got, from_x, from_y = refs[:4]
    by_x, by_y = refs[-2:]
    height = kept.shape[2]
    for tap in range(2):
        here = pl.ds(tap * height, height)
        parts = [kept[tap, 1], got[tap, 1]] + ([from_y[0:height, :]] if tap == 1 else [])
        by_x[here, :] = added(*parts).astype(BF16)
        parts = [kept[tap, 2], got[tap, 2]] + ([from_x[0:height, :]] if tap == 0 else [])
        by_y[here, :] = added(*parts).astype(BF16)
    if columns is not None:
        by_x[2 * height :, :] = from_y[height:, :]


def plane_sum(place, kept, got, from_x, from_y, tap):
    here = pl.ds(tap * kept.shape[2], kept.shape[2])
    return added(kept[tap, 0], got[tap, 0], from_x[here, :], from_y[here, :])


def plane_kernel(*refs):
    kept, got, from_x, from_y = refs[:4]
    out = refs[-1]
    height = kept.shape[2]
    for tap in range(2):
        out[pl.ds(tap * height, height), :] = plane_sum(None, kept, got, from_x, from_y, tap).astype(BF16)


def messages_kernel(columns, *refs):
    place, kept, got, from_x, from_y, bias, got_bias, corner_x, corner_y, second = refs[:10]
    outs = refs[-5:-2]
    first, order = refs[-2:]
    height = kept.shape[2]
    for tap in range(2):
        first[pl.ds(tap * height, height), :] = plane_sum(None, kept, got, from_x, from_y, tap).astype(BF16)
    parts = [
        bias_rows(bias[:, columns] + got_bias[:, columns]),
        corner_x[height:, :],
        corner_y[height:, :],
        from_x[2 * height :, :],
    ]
    whole = sum_in_order(order, [bias_of(part) for part in parts], place[1] // 2)
    whole = bias_rows(jnp.concatenate([whole[0:1]] * SUBS + [whole[1:2]] * SUBS, axis=0))
    first[2 * height :, :] = whole
    for index, out in enumerate(outs):
        to = place[0] ^ (index + 1)
        row = pl.ds(pl.multiple_of((to % 2) * height, 16), height)

        @pl.when(to < 2)
        def _(out=out, row=row):
            out[0:height, :] = first[row, :]

        @pl.when(to >= 2)
        def _(out=out, row=row):
            out[0:height, :] = second[row, columns]

        out[height:, :] = whole


def whole_kernel(parts, *refs):
    place, second = refs[:2]
    out, bias_out, *orders = refs[-2 - len(parts) :]
    section = place[0]
    height = out.shape[0]
    row = pl.ds(pl.multiple_of((section % 2) * height, 16), height)
    for index, columns in enumerate(parts):
        first, *got = refs[2 + 4 * index : 6 + 4 * index]
        rest = added(*[part[0:height, :] for part in got])

        @pl.when(section < 2)
        def _(first=first, rest=rest, columns=columns):
            out[:, columns] = first[row, :].astype(F32) + rest

        @pl.when(section >= 2)
        def _(rest=rest, columns=columns):
            out[:, columns] = second[row, columns].astype(F32) + rest

        biases = [first[2 * height :, :]] + [part[height:, :] for part in got]
        bias_out[:, columns] = sum_in_order(orders[index], [bias_of(part) for part in biases], section)


def call(kernel, outs, in_specs, out_specs, scratch, flops, moved, megabytes, name):
    return pl.pallas_call(
        kernel,
        out_shape=outs,
        in_specs=in_specs,
        out_specs=out_specs,
        scratch_shapes=scratch,
        compiler_params=pltpu.CompilerParams(vmem_limit_bytes=megabytes * 2**20),
        cost_estimate=pl.CostEstimate(flops=flops // COST, bytes_accessed=moved // COST, transcendentals=0),
        name=name,
    )


def small_call(kernel, outs, operands, name, ties=(), scratch=()):
    has_place = operands[0].dtype == jnp.int32
    specs = [SMEM if has_place and index == 0 else VMEM for index in range(len(operands))]
    return call(
        kernel,
        outs,
        specs + [ANY] * len(ties),
        [VMEM] * len(outs),
        list(scratch),
        1000000,
        1000000,
        12,
        name,
    )(*operands, *ties)


def swap(value, axis, mask):
    pairs = [(index, index ^ mask) for index in range(lax.axis_size(axis))]
    return lax.ppermute(value, axis, pairs)


def moved(value, axis, target):
    return lax.ppermute(value, axis, [(index, target(index)) for index in range(lax.axis_size(axis))])


def gathered_pieces(place, shard, early):
    height, gates = shard.shape
    chip = jax.ShapeDtypeStruct((2 * height, gates), shard.dtype)

    def joined_cores(own, ties=()):
        return small_call(join_kernel, [chip], [place, own, swap(own, "dp", 1)], "join", ties)[0]

    def beside(unit):
        return moved(unit, "dp", lambda index: index ^ (3 if index % 2 == 0 else 5))

    def opposite(first, second):
        unit = small_call(pick_kernel, [chip], [place, first, second], "pick")[0]
        return moved(unit, "dp", lambda index: index ^ (2 if index % 2 == 0 else 4))

    two = swap(shard, "section", 2)
    one = swap(shard, "section", 1)
    three = swap(two, "section", 1)
    units, got, across = [], [], []
    for own, ties in ((shard, []), (one, [0]), (two, []), (three, [1])):
        ties = [got[index] for index in ties] + (early if len(got) == 1 else [])
        units.append(joined_cores(own, ties))
        got.append(beside(units[-1]))
        if len(got) % 2 == 0:
            across.append(opposite(*got[-2:]))
    out = []
    for pair in range(2):
        for tap in range(2 * pair, 2 * pair + 2):
            out += [units[tap], got[tap], swap(got[tap], "dp", 1)]
        out += [across[pair], swap(across[pair], "dp", 1)]
    return out


class LayerSum:
    def __init__(self, kept, sent, columns=None, bias=None, got_bias=None, place=None):
        self.kept, self.got = kept, swap(sent, "dp", 1)
        self.columns, self.bias, self.got_bias, self.place = columns, bias, got_bias, place
        self.height, self.gates = kept.shape[2], kept.shape[3]
        self.extra = 0 if bias is None else BIAS_ROWS

    def rows(self, taps, extra):
        return jax.ShapeDtypeStruct((taps * self.height + extra, self.gates), BF16)

    def corners(self, ties=()):
        operands = [self.kept, self.got] + ([] if self.bias is None else [self.bias, self.got_bias])
        by_x, by_y = small_call(
            functools.partial(corner_kernel, self.columns), [self.rows(1, self.extra)] * 2, operands, "corners", ties
        )
        self.corner_x, self.corner_y = swap(by_x, "dp", 2), swap(by_y, "dp", 4)

    def sides(self, ties=()):
        self.by = small_call(
            functools.partial(sides_kernel, self.columns),
            [self.rows(2, self.extra), self.rows(2, 0)],
            [self.kept, self.got, self.corner_x, self.corner_y],
            "sides",
            ties,
        )
        self.side_x, self.side_y = swap(self.by[0], "dp", 2), swap(self.by[1], "dp", 4)

    def plane(self, ties=()):
        operands = [self.kept, self.got, self.side_x, self.side_y]
        return small_call(plane_kernel, [self.rows(2, 0)], operands, "plane", ties)[0]

    def messages(self, second, ties=()):
        *sent, plane = small_call(
            functools.partial(messages_kernel, self.columns),
            [self.rows(1, self.extra)] * 3 + [self.rows(2, self.extra)],
            [
                self.place, self.kept, self.got, self.side_x, self.side_y, self.bias, self.got_bias,
                self.corner_x, self.corner_y, second,
            ],
            "messages",
            ties,
            [pltpu.VMEM((4, 2, self.gates), F32)],
        )
        return [plane] + [swap(part, "section", index + 1) for index, part in enumerate(sent)]


def all_sums(value):
    for axis in ("dp", "section"):
        mask = 1
        while mask < lax.axis_size(axis):
            value = value + swap(value, axis, mask)
            mask *= 2
    return value


def grouped(value, rows):
    length, width = value.shape
    return value.reshape(length // rows, SUBS, rows // SUBS, width).swapaxes(1, 2).reshape(length, width)


def ungrouped(value):
    rows, width = value.shape
    return value.reshape(rows // SUBS, SUBS, width).swapaxes(0, 1).reshape(rows, width)


def per_device(tokens_in, doc_starts, cotangent, tap_weight, gate_bias):
    sections = lax.axis_size("section")
    streams = lax.axis_size("dp")
    section = lax.axis_index("section")
    stream = lax.axis_index("dp")
    _, length, width = tokens_in.shape
    gates = 3 * width
    tiles = width // LANES
    rows = length // sections
    block = 256
    start = section * rows
    height = tap_weight.shape[1]
    quick = sections == 4 and streams == 8 and height % 16 == 0

    def own(value):
        return lax.dynamic_slice_in_dim(value, start, rows, 0)

    def own(value):
        return lax.dynamic_slice_in_dim(value, start, rows, 0)

    place = jnp.stack([section, stream]).astype(jnp.int32)
    keep = (1 - doc_starts[0]).astype(F32)[:, None]
    keep_own = grouped(jnp.broadcast_to(own(keep), (rows, LANES)), rows)
    keep_firsts = jnp.broadcast_to(jnp.concatenate([keep[::rows], keep[: 8 - sections]], axis=0), (8, LANES))
    x = grouped(own(tokens_in[0]), rows)
    tail = lax.dynamic_slice_in_dim(tokens_in[0], jnp.maximum(start - 16, 0), 16, 0)
    cot = grouped(own(cotangent[0]), rows)
    cot_next = lax.dynamic_slice_in_dim(cotangent[0], jnp.minimum(start + rows, length - 16), 16, 0)
    bias = gate_bias.astype(F32)

    def shape(*dims, dtype=F32):
        return jax.ShapeDtypeStruct(dims, dtype)

    def buffer(*dims, dtype=F32):
        return pltpu.VMEM(dims, dtype)

    dma = pltpu.SemaphoreType.DMA
    layer_flops = 2 * rows * width * gates * 2
    weight_bytes = 4 * width * gates
    half = shape(rows, width, dtype=BF16)
    full = shape(tiles, rows, LANES)
    scan = buffer(tiles, rows, LANES)
    matrix = shape(2 * width, gates, dtype=BF16)

    half = shape(rows, width, dtype=BF16)
    (prev,) = small_call(
        before_kernel,
        [half],
        [place, x, tail, keep_own],
        "before",
        [keep_firsts, cot, cot_next, bias],
        scratch=[buffer(tiles, rows + SUBS, LANES)],
    )
    early = [prev]
    if quick:
        weights = gathered_pieces(place, tap_weight[0], early)
    else:
        whole = lax.all_gather(tap_weight, "dp", axis=1, tiled=True)
        weights = [lax.all_gather(whole, "section", axis=0, tiled=True)]
    plan = len(weights)
    weight_count = plan

    def exchanged(summary):
        return [summary] + [swap(summary, "section", index) for index in range(1, sections)]

    candid0, forget0, gate0, summary, matrix0 = call(
        functools.partial(first_forward_kernel, plan, block),
        [full] * 3 + [shape(8, width), matrix],
        [SMEM] + [VMEM] * 4 + [HBM] * len(weights),
        [VMEM] * 5,
        [dma((weight_count + 1,))],
        layer_flops,
        weight_bytes + 30 * rows * width,
        LIMITS[0],
        "first_forward",
    )(place, x, prev, keep_own, bias[0:1], *weights)

    cells0, hidden0, delayed0, last0, candid1, forget1, gate1, summary1, matrix1 = call(
        functools.partial(second_forward_kernel, plan, block),
        [shape(tiles, rows + SUBS, LANES), half, half, shape(8, width)]
        + [full] * 3
        + [shape(16, width), matrix],
        [SMEM] + [VMEM] * 10 + [HBM] * len(weights),
        [VMEM] * 9,
        [
            buffer(sections, 8, width),
            scan,
            buffer(tiles, rows + SUBS, LANES),
            dma((weight_count + 1,)),
        ],
        layer_flops,
        weight_bytes + 20 * rows * width,
        LIMITS[1],
        "second_forward",
    )(place, candid0, forget0, gate0, keep_own, cot, bias[1:2], *exchanged(summary), *weights)

    if quick:
        kept_shape = [shape(2, 4, height, gates, dtype=BF16)] * 2
    else:
        kept_shape = [shape(2, width, gates, dtype=BF16)]
    wide = shape(rows, gates, dtype=BF16)

    hidden1, dpre1, shifted1, bias1, lasts, *kept1 = call(
        functools.partial(second_backward_kernel, rows, quick),
        [half, wide, wide, shape(8, gates), shape(2, 1, width)] + kept_shape,
        [SMEM] + [VMEM] * 13,
        [VMEM] * (5 + len(kept_shape)),
        [buffer(sections, 16, width), buffer(tiles, rows + SUBS, LANES), scan, buffer(3, rows + SUBS, LANES), buffer(SUBS, gates)],
        layer_flops,
        weight_bytes + 30 * rows * width,
        LIMITS[2],
        "second_backward",
    )(
        place, candid1, forget1, gate1, hidden0, delayed0, keep_own, cot, cot_next, keep_firsts,
        *exchanged(summary1),
    )

    if quick:
        second = LayerSum(*kept1)
        second.corners()

    arriving, summary0 = call(
        functools.partial(middle_kernel, rows, block),
        [half, shape(8, width)],
        [SMEM] + [VMEM] * 7,
        [VMEM] * 2,
        [scan],
        layer_flops,
        weight_bytes + 20 * rows * width,
        LIMITS[3],
        "middle",
    )(place, dpre1, shifted1, candid0, forget0, gate0, keep_own, matrix1)

    ties = []
    first_shape, first_columns = kept_shape, gates
    if quick:
        second.sides()
        ties = second.by
        first_columns = gates // LANES // 2 * LANES
        first_shape = [shape(2, 4, height, first_columns, dtype=BF16)] * 2
    dpre0, shifted0, bias_both, *kept0 = call(
        functools.partial(first_backward_kernel, rows, quick),
        [wide, wide, shape(2 * SUBS, gates)] + first_shape,
        [SMEM] + [VMEM] * 15 + [ANY] * len(ties),
        [VMEM] * (3 + len(kept_shape)),
        [buffer(sections, 8, width), scan, buffer(3, rows + SUBS, LANES), buffer(SUBS, gates)],
        layer_flops,
        weight_bytes + 30 * rows * width,
        LIMITS[4],
        "first_backward",
    )(
        place, candid0, forget0, gate0, cells0, last0, x, prev, keep_own, arriving, keep_firsts, bias1,
        *exchanged(summary0), *ties,
    )
    if quick:
        later_shape = shape(2, 4, height, gates - first_columns, dtype=BF16)
        later = small_call(
            functools.partial(first_weights_kernel, first_columns),
            [later_shape] * 2,
            [place, x, prev, dpre0],
            "first_weights",
        )
        plane1 = second.plane()

    input_grad = call(
        functools.partial(last_kernel, rows, block),
        shape(rows, width),
        [VMEM] * 3,
        VMEM,
        [],
        layer_flops,
        weight_bytes + 20 * rows * width,
        LIMITS[5],
        "last",
    )(dpre0, shifted0, matrix0)

    if quick:
        got_bias = swap(bias_both, "dp", 1)
        parts = [slice(0, first_columns), slice(first_columns, gates)]
        sums = [
            LayerSum(*pieces, columns, bias_both, got_bias, place)
            for pieces, columns in zip((kept0, later), parts, strict=True)
        ]
        sums[0].corners()
        sums[1].corners(ties=[input_grad])
        sums[0].sides(ties=[plane1])
        sums[1].sides(ties=sums[0].by)
        got = [part.messages(plane1) for part in sums]
        weight_grad, bias_grad = small_call(
            functools.partial(whole_kernel, parts),
            [shape(height, gates), shape(2, gates)],
            [place, plane1] + got[0] + got[1],
            "whole",
            scratch=[buffer(4, 2, columns.stop - columns.start) for columns in parts],
        )
        weight_grad = weight_grad[None]
    else:
        bias_grad = all_sums(bias_both[::8])
        stacked = jnp.concatenate([kept0[0], kept1[0]], axis=0)
        by_rows = lax.psum_scatter(stacked, "dp", scatter_dimension=1, tiled=True)
        weight_grad = lax.psum_scatter(by_rows, "section", scatter_dimension=0, tiled=True).astype(F32)
    return (ungrouped(hidden1)[None], ungrouped(input_grad)[None], weight_grad, bias_grad, lasts)


def solution(mesh):
    in_specs = (
        P("dp", None, None),
        P("dp", None),
        P("dp", None, None),
        P("section", "dp", None),
        P(),
    )
    out_specs = (
        P("dp", "section", None),
        P("dp", "section", None),
        P("section", "dp", None),
        P(),
        P(None, "dp", None),
    )
    return jax.shard_map(
        per_device, mesh=mesh, in_specs=in_specs, out_specs=out_specs, check_vma=False
    )
```

```python
import functools

import jax
import jax.numpy as jnp
from jax import lax
from jax.experimental import pallas as pl
from jax.experimental.pallas import tpu as pltpu
from jax.sharding import PartitionSpec as P

F32 = jnp.float32
BF16 = jnp.bfloat16
LANES = 128
SUBS = 8
BIAS_ROWS = 16
COST = 100
UNROLL = 16
LIMITS = (16, 20, 20, 14, 20, 14)
ANY = pl.BlockSpec(memory_space=pl.ANY)
HBM = pl.BlockSpec(memory_space=pltpu.HBM)
VMEM = pl.BlockSpec(memory_space=pltpu.VMEM)
SMEM = pl.BlockSpec(memory_space=pltpu.SMEM)


def tiles_of(ref):
    return range(ref.shape[0])


def columns_of(tile):
    return slice(tile * LANES, (tile + 1) * LANES)


def joined(tiles):
    return jnp.concatenate(tiles, axis=1)


def first_row(ref):
    return joined([ref[tile, 0:1, :] for tile in tiles_of(ref)])


def ones_and_zeros(tiles):
    return [jnp.ones((SUBS, LANES), F32)] * tiles, [jnp.zeros((SUBS, LANES), F32)] * tiles


def over_steps(steps, body, state):
    def turn(index, state):
        for part in range(UNROLL):
            state = body(index * UNROLL + part, state)
        return state

    return lax.fori_loop(0, steps // UNROLL, turn, state)


def group(step):
    row = step * SUBS
    return pl.ds(row if isinstance(row, int) else pl.multiple_of(row, SUBS), SUBS)


def forward_steps(candid, forget, keep, first, steps, gains, cells):
    def body(step, state):
        gains, cells = state
        spot = group(first + step)
        kept = keep[spot, :]
        new_gains, new_cells = [], []
        for tile, (gain, cell) in enumerate(zip(gains, cells, strict=True)):
            share = forget[tile, spot, :]
            now = share * kept
            new_cells.append(now * cell + (1.0 - share) * candid[tile, spot, :])
            new_gains.append(gain * now)
        return new_gains, new_cells

    return over_steps(steps, body, (list(gains), list(cells)))


def forward_entries(gains, cells, carry):
    gain, cell = joined(gains), joined(cells)
    entries = []
    for sub in range(SUBS):
        entries.append(carry)
        carry = cell[sub : sub + 1] + gain[sub : sub + 1] * carry
    return jnp.concatenate(entries, axis=0), carry


def forward_fill(candid, forget, keep, steps, entries, out):
    cells = [entries[:, columns_of(tile)] for tile in tiles_of(out)]
    for tile in tiles_of(out):
        out[tile, group(0), :] = cells[tile]

    def body(step, cells):
        spot = group(step)
        kept = keep[spot, :]
        new_cells = []
        for tile, cell in enumerate(cells):
            share = forget[tile, spot, :]
            cell = share * kept * cell + (1.0 - share) * candid[tile, spot, :]
            out[tile, group(step + 1), :] = cell
            new_cells.append(cell)
        return new_cells

    over_steps(steps, body, cells)


def backward_steps(forget, keep, emit, steps):
    tiles = emit.shape[0]

    def body(step, state):
        gains, backs = state
        spot = group(steps - 1 - step)
        kept = keep[spot, :]
        new_gains, new_backs = [], []
        for tile, (gain, back) in enumerate(zip(gains, backs, strict=True)):
            now = forget[tile, spot, :] * kept
            new_backs.append(now * (emit[tile, spot, :] + back))
            new_gains.append(gain * now)
        return new_gains, new_backs

    state = ones_and_zeros(tiles)
    whole = (steps - 1) // UNROLL * UNROLL
    state = over_steps(whole, body, state)
    for step in range(whole, steps - 1):
        state = body(step, state)
    first_gains, backs = state
    firsts = [emit[tile, group(0), :] + backs[tile] for tile in range(tiles)]
    gains, backs = body(steps - 1, state)
    return joined(gains), joined(backs), joined(first_gains), joined(firsts)


def backward_entries(gain, back, carry):
    entries = []
    for sub in reversed(range(SUBS)):
        entries.append(carry)
        carry = back[sub : sub + 1] + gain[sub : sub + 1] * carry
    return jnp.concatenate(entries[::-1], axis=0)


def backward_fill(forget, keep, emit, steps, entries):
    def body(step, backs):
        spot = group(steps - 1 - step)
        kept = keep[spot, :]
        new_backs = []
        for tile, back in enumerate(backs):
            now = emit[tile, spot, :] + back
            emit[tile, spot, :] = now
            new_backs.append(forget[tile, spot, :] * kept * now)
        return new_backs

    over_steps(steps, body, [entries[:, columns_of(tile)] for tile in tiles_of(emit)])


def chunk_backward_summary(forget, keep, emit, steps):
    gain, back, first_gain, first = backward_steps(forget, keep, emit, steps)
    gain_all = jnp.ones_like(gain[0:1])
    back_all = jnp.zeros_like(gain[0:1])
    for sub in reversed(range(SUBS)):
        entry_gain, entry_back = gain_all, back_all
        gain_all = gain[sub : sub + 1] * entry_gain
        back_all = back[sub : sub + 1] + gain[sub : sub + 1] * entry_back
    row_gain = first_gain[0:1] * entry_gain
    row_value = first[0:1] + first_gain[0:1] * entry_back
    return gain_all, back_all, row_gain, row_value


def store_gates(pre, here, candid_out, forget_out, gate_out):
    tiles = candid_out.shape[0]
    for tile in range(tiles):
        candid_out[tile, here, :] = jnp.tanh(pre[:, columns_of(tile)])
        forget_out[tile, here, :] = jax.nn.sigmoid(pre[:, columns_of(tiles + tile)])
        if gate_out is not None:
            gate_out[tile, here, :] = jax.nn.sigmoid(pre[:, columns_of(2 * tiles + tile)])


class Weights:
    def __init__(self, place, layer, near, far, target, sems):
        self.place, self.layer, self.target, self.sems = place, layer, target, sems
        self.near, self.far = near, far

    def each(self, pieces, act):
        section, core, chip = self.place[0], self.place[1] % 2, self.place[1] // 2
        width = self.target.shape[0] // 2
        height = pieces[0].shape[0]
        places = []
        for tap in range(2):
            places += [(tap, chip), (tap, chip ^ (2 - core)), (tap, chip ^ (1 + core))]
        places += [(core, chip ^ 3), (1 - core, chip ^ 3)]
        for index, (piece, (tap, rows)) in enumerate(zip(pieces, places, strict=True)):
            row = ((section % 2) ^ tap) * width + rows * height
            target = self.target.at[pl.ds(pl.multiple_of(row, 16), height), :]
            act(pltpu.make_async_copy(piece, target, self.sems.at[index]))

    def both(self, act):
        if self.far is None:
            width = self.target.shape[0] // 2
            for tap in range(2):
                act(
                    pltpu.make_async_copy(
                        self.near.at[2 * self.layer + tap],
                        self.target.at[pl.ds(tap * width, width), :],
                        self.sems.at[tap],
                    )
                )
            return
        is_near = self.place[0] // 2 == self.layer

        @pl.when(is_near)
        def _():
            self.each(self.near, act)

        @pl.when(jnp.logical_not(is_near))
        def _():
            self.each(self.far, act)

    def start(self):
        self.both(lambda copy: copy.start())

    def wait(self):
        self.both(lambda copy: copy.wait())


def weight_refs(refs, count):
    if count == 1:
        return refs[0], None
    return refs[: count // 2], refs[count // 2 : count]


def join_kernel(place, own, got, *refs):
    out = refs[-1]
    height = own.shape[0]
    core = place[1] % 2
    out[pl.ds(pl.multiple_of(core * height, 16), height), :] = own[...]
    out[pl.ds(pl.multiple_of((1 - core) * height, 16), height), :] = got[...]


def pick_kernel(place, first, second, out):
    @pl.when(place[1] % 2 == 0)
    def _():
        out[...] = first[...]

    @pl.when(place[1] % 2 == 1)
    def _():
        out[...] = second[...]


def before_kernel(*refs):
    place, x, tail, keep = refs[:4]
    prev, shifted = refs[-2:]
    rows, width = x.shape
    top = jnp.where(place[0] > 0, tail[...].astype(F32)[15:16], 0.0)
    for tile in range(width // LANES):
        columns = columns_of(tile)
        shifted[tile, pl.ds(SUBS, rows), :] = x[:, columns].astype(F32)
        shifted[tile, group(0), :] = jnp.concatenate(
            [top[:, columns], shifted[tile, rows : rows + SUBS - 1, :]], axis=0
        )
        prev[:, columns] = (shifted[tile, pl.ds(0, rows), :] * keep[...]).astype(BF16)


def forward_gates(x, prev, matrix, bias, keep, block, candid_out, forget_out, gate_out, finish=None):
    rows, width = x.shape
    tiles = candid_out.shape[0]
    block_steps = block // SUBS

    def part(index, state):
        here = pl.ds(pl.multiple_of(index * block, block), block)
        pre = (
            jnp.dot(x[here, :], matrix[:width, :], preferred_element_type=F32)
            + jnp.dot(prev[here, :], matrix[width:, :], preferred_element_type=F32)
            + bias[...]
        )
        store_gates(pre, here, candid_out, forget_out, gate_out)
        if finish is not None:
            finish(here)
        return forward_steps(candid_out, forget_out, keep, index * block_steps, block_steps, *state)

    return lax.fori_loop(0, rows // block, part, ones_and_zeros(tiles))


def first_forward_kernel(plan, block, *refs):
    place, x, prev, keep, bias = refs[:5]
    near, far = weight_refs(refs[5:], plan)
    candid_out, forget_out, gate_out, summary_out, matrix, weight_sems = refs[5 + plan :]
    rows, width = x.shape
    weights = Weights(place, 0, near, far, matrix, weight_sems)
    weights.start()
    weights.wait()
    gains, cells = forward_gates(x, prev, matrix, bias, keep, block, candid_out, forget_out, gate_out)
    gain_all, cell_all = jnp.ones((1, width), F32), jnp.zeros((1, width), F32)
    gain, cell = joined(gains), joined(cells)
    for sub in range(SUBS):
        cell_all = cell[sub : sub + 1] + gain[sub : sub + 1] * cell_all
        gain_all = gain[sub : sub + 1] * gain_all
    last_gate = joined([gate_out[tile, rows - 1 : rows, :] for tile in tiles_of(gate_out)])
    parts = [gain_all, cell_all, last_gate] + [jnp.zeros((1, width), F32)] * 5
    summary_out[...] = jnp.concatenate(parts, axis=0)


def second_forward_kernel(plan, block, *refs):
    place, candid, forget, gate, keep, cot, bias = refs[:7]
    summaries = refs[7:11]
    near, far = weight_refs(refs[11:], plan)
    (
        cell_out,
        hidden,
        delayed,
        last,
        candid_out,
        forget_out,
        gate_out,
        summary_out,
        matrix,
        order,
        emit,
        shifted,
        weight_sems,
    ) = refs[11 + plan :]
    section = place[0]
    rows, width = hidden.shape
    tiles = emit.shape[0]
    steps = rows // SUBS
    weights = Weights(place, 1, near, far, matrix, weight_sems)
    weights.start()

    heads = heads_of(order, summaries, section)
    carry = jnp.zeros((1, width), F32)
    carries, hiddens = [], [jnp.zeros((1, width), F32)]
    for head in heads:
        carries.append(carry)
        carry = head[1:2] + head[0:1] * carry
        hiddens.append(head[2:3] * carry)
    gains, cells = forward_steps(candid, forget, keep, 0, steps, *ones_and_zeros(tiles))
    entries, carry = forward_entries(gains, cells, pick(carries, section))
    last[...] = jnp.broadcast_to(carry, last.shape)
    forward_fill(candid, forget, keep, steps, entries, cell_out)
    top = pick(hiddens[:-1], section)
    for tile in range(tiles):
        columns = columns_of(tile)
        shifted[tile, pl.ds(SUBS, rows), :] = gate[tile, :, :] * cell_out[tile, pl.ds(SUBS, rows), :]
        shifted[tile, group(0), :] = jnp.concatenate(
            [top[:, columns], shifted[tile, rows : rows + SUBS - 1, :]], axis=0
        )
        hidden[:, columns] = shifted[tile, pl.ds(SUBS, rows), :].astype(BF16)
        delayed[:, columns] = (shifted[tile, pl.ds(0, rows), :].astype(BF16).astype(F32) * keep[...]).astype(BF16)

    weights.wait()

    def emitted(here):
        for tile in range(tiles):
            emit[tile, here, :] = cot[here, columns_of(tile)].astype(F32) * gate_out[tile, here, :]

    gains, cells = forward_gates(
        hidden, delayed, matrix, bias, keep, block, candid_out, forget_out, gate_out, emitted
    )
    cell_all = forward_entries(gains, cells, jnp.zeros((1, width), F32))[1]
    gain_all, back_all, row_gain, row_value = chunk_backward_summary(forget_out, keep, emit, steps)
    parts = [
        gain_all,
        cell_all,
        back_all,
        row_gain,
        row_value,
        first_row(candid_out),
        first_row(forget_out),
        first_row(gate_out),
        last[0:1, :],
    ]
    parts += [jnp.zeros((1, width), F32)] * (16 - len(parts))
    summary_out[...] = jnp.concatenate(parts, axis=0)


def gate_grads(dcell, before, cell, candid, forget, gate, arriving):
    return (
        dcell * (1.0 - forget) * (1.0 - candid * candid),
        dcell * (before - candid) * forget * (1.0 - forget),
        arriving * cell * gate * (1.0 - gate),
    )


def pick(values, section):
    out = values[0]
    for index in range(1, len(values)):
        out = jnp.where(section == index, values[index], out)
    return out


def first_weights_kernel(first, *refs):
    place, x, prev, dpre, bias = refs[:5]
    store_weight_grads(place, (x[...], prev[...]), dpre[:, first:], refs[-2:], bias[:, first:])


def store_weight_grads(place, lefts, right, outs, bias=None):
    for tap, left in enumerate(lefts):
        grads = lax.dot_general(left, right, (((0,), (0,)), ((), ())), preferred_element_type=F32).astype(BF16)
        if len(outs) == 1:
            outs[0][tap] = grads
            continue
        kept, sent = outs
        height = tap_rows(kept)
        chip, odd = place[1] // 2, place[1] % 2 == 1
        for index in range(4):
            even_rows = grads[2 * index * height : (2 * index + 1) * height]
            odd_rows = grads[(2 * index + 1) * height : (2 * index + 2) * height]
            here = block_of(tap, index ^ chip, height)
            kept[here, :] = jnp.where(odd, odd_rows, even_rows)
            sent[here, :] = jnp.where(odd, even_rows, odd_rows)
    if bias is not None and len(outs) > 1:
        for out in outs:
            out[8 * tap_rows(out) :, :] = bias_rows(bias)


def heads_of(order, summaries, section):
    for index, summary in enumerate(summaries):
        order[section ^ index] = summary[...]
    return [order[index] for index in range(len(summaries))]


def back_entries(heads):
    back = jnp.zeros_like(heads[0][0:1])
    backs = []
    for head in reversed(heads):
        backs.append(back)
        back = head[2:3] + head[0:1] * back
    return backs[::-1]


def following_row(heads, backs, section, keep_firsts, cell, arriving):
    nexts = [min(index + 1, len(heads) - 1) for index in range(len(heads))]
    head = pick([heads[index] for index in nexts], section)
    back = pick([backs[index] for index in nexts], section)
    valid = jnp.where(section < len(heads) - 1, 1.0, 0.0)
    keep = pick([keep_firsts[index : index + 1, :] for index in nexts], section)
    keep = joined([keep] * (cell.shape[1] // LANES))
    candid, forget, gate = head[5:6], head[6:7], head[7:8]
    if arriving is None:
        arriving = head[1:2]
    before = keep * cell
    after = forget * before + (1.0 - forget) * candid
    dcell = (head[4:5] + head[3:4] * back) * valid
    return gate_grads(dcell, before, after, candid, forget, gate, arriving * valid), keep


def store_grads(rows, dcells, cells, candid, forget, gate, arriving, keep, next_first, extra, shifted, outs):
    dpre_out, shifted_out, bias_out, after = outs
    tiles = dcells.shape[0]
    width = tiles * LANES
    part_rows = 64
    for index in range(3):
        rounded = extra[index].astype(BF16).astype(F32) * joined([next_first[:, :LANES]] * tiles)
        after[:, index * width : (index + 1) * width] = jnp.broadcast_to(rounded, (SUBS, width))

    def of_tile(tile, carry):
        def of_rows(part, sums):
            base = pl.multiple_of(part * part_rows, part_rows)
            here = pl.ds(base, part_rows)
            kept = keep[here, :]
            parts = gate_grads(
                dcells[tile, here, :],
                cells[tile, here, :] * kept,
                cells[tile, pl.ds(pl.multiple_of(base + SUBS, SUBS), part_rows), :],
                candid[tile, here, :],
                forget[tile, here, :],
                gate[tile, here, :],
                arriving[here, pl.ds(pl.multiple_of(tile * LANES, LANES), LANES)].astype(F32),
            )
            new_sums = []
            for index, part in enumerate(parts):
                rounded = part.astype(BF16)
                columns = pl.ds(pl.multiple_of((index * tiles + tile) * LANES, LANES), LANES)
                dpre_out[here, columns] = rounded
                rounded = rounded.astype(F32)
                shifted[index, here, :] = rounded * kept
                new_sums.append(
                    sums[index] + jnp.sum(rounded.reshape(part_rows // SUBS, SUBS, LANES), axis=0)
                )
            return new_sums

        sums = lax.fori_loop(0, rows // part_rows, of_rows, [jnp.zeros((SUBS, LANES), F32)] * 3)
        for index in range(3):
            columns = pl.ds(pl.multiple_of((index * tiles + tile) * LANES, LANES), LANES)
            shifted[index, pl.ds(rows, SUBS), :] = jnp.concatenate(
                [shifted[index, 1:SUBS, :], after[0:1, columns]], axis=0
            )
            shifted_out[:, columns] = shifted[index, pl.ds(SUBS, rows), :].astype(BF16)
            bias_out[:, columns] = jnp.broadcast_to(
                jnp.sum(sums[index], axis=0, keepdims=True), (bias_out.shape[0], LANES)
            )
        return carry

    lax.fori_loop(0, tiles, of_tile, 0)


def second_backward_kernel(rows, has_sent, *refs):
    (place, candid, forget, gate, hidden, delayed, keep, cot, cot_next, keep_firsts) = refs[:10]
    summaries = refs[10:14]
    outs = refs[14:]
    hidden_out, dpre_out, shifted_out, bias_out, last_out = outs[:5]
    grads = outs[5 : 7 if has_sent else 6]
    order, cells, dcells, shifted, after = refs[-5:]
    section = place[0]
    width = hidden.shape[1]
    tiles = dcells.shape[0]
    steps = rows // SUBS
    heads = heads_of(order, summaries, section)
    carry = jnp.zeros((1, width), F32)
    carries = []
    for head in heads:
        carries.append(carry)
        carry = head[1:2] + head[0:1] * carry
    last_out[0] = heads[-1][8:9]
    last_out[1] = carry
    backs = back_entries(heads)
    carry = pick(carries, section)
    back = pick(backs, section)
    for tile in range(tiles):
        dcells[tile, :, :] = cot[:, columns_of(tile)].astype(F32) * gate[tile, :, :]
    gains, ends = forward_steps(candid, forget, keep, 0, steps, *ones_and_zeros(tiles))
    entries, carry = forward_entries(gains, ends, carry)
    forward_fill(candid, forget, keep, steps, entries, cells)
    for tile in range(tiles):
        hidden_out[:, columns_of(tile)] = (gate[tile, :, :] * cells[tile, pl.ds(SUBS, rows), :]).astype(BF16)
    gain, leaving, _, _ = backward_steps(forget, keep, dcells, steps)
    backward_fill(forget, keep, dcells, steps, backward_entries(gain, leaving, back))
    extra, next_first = following_row(heads, backs, section, keep_firsts, carry, cot_next[...].astype(F32)[0:1])
    store_grads(
        rows, dcells, cells, candid, forget, gate, cot, keep, next_first, extra, shifted,
        (dpre_out, shifted_out, bias_out, after),
    )
    store_weight_grads(place, (hidden[...], delayed[...]), dpre_out[...], grads)


def input_grad_tile(dpre, shifted, matrix, here):
    width = matrix.shape[0] // 2
    contract = (((1,), (1,)), ((), ()))
    return lax.dot_general(
        dpre[here, :], matrix[:width, :], contract, preferred_element_type=F32
    ) + lax.dot_general(shifted[here, :], matrix[width:, :], contract, preferred_element_type=F32)


def middle_kernel(rows, block, *refs):
    place, dpre, shifted, candid, forget, gate, keep, matrix = refs[:8]
    arriving_out, summary_out, emit = refs[8:]

    def part(index, carry):
        here = pl.ds(pl.multiple_of(index * block, block), block)
        arriving = input_grad_tile(dpre, shifted, matrix, here).astype(BF16)
        arriving_out[here, :] = arriving
        for tile in tiles_of(emit):
            emit[tile, here, :] = arriving[:, columns_of(tile)].astype(F32) * gate[tile, here, :]
        return carry

    lax.fori_loop(0, rows // block, part, 0)
    row_arriving = arriving_out[0:16, :].astype(F32)[0:1]
    gain_all, back_all, row_gain, row_value = chunk_backward_summary(forget, keep, emit, rows // SUBS)
    parts = [
        gain_all,
        row_arriving,
        back_all,
        row_gain,
        row_value,
        first_row(candid),
        first_row(forget),
        first_row(gate),
    ]
    summary_out[...] = jnp.concatenate(parts, axis=0)


def first_backward_kernel(rows, has_sent, *refs):
    (place, candid, forget, gate, cells, last, x, prev, keep, arriving, keep_firsts, other_bias) = refs[:12]
    summaries = refs[12:16]
    order, dcells, shifted, after = refs[-4:]
    outs = refs[-9:-4] if has_sent else refs[-8:-4]
    dpre_out, shifted_out, bias_out, *grads = outs
    section = place[0]
    steps = rows // SUBS
    heads = heads_of(order, summaries, section)
    backs = back_entries(heads)
    back = pick(backs, section)
    for tile in tiles_of(dcells):
        dcells[tile, :, :] = arriving[:, columns_of(tile)].astype(F32) * gate[tile, :, :]
    gain, leaving, _, _ = backward_steps(forget, keep, dcells, steps)
    backward_fill(forget, keep, dcells, steps, backward_entries(gain, leaving, back))
    extra, next_first = following_row(heads, backs, section, keep_firsts, last[0:1, :], None)
    store_grads(
        rows, dcells, cells, candid, forget, gate, arriving, keep, next_first, extra, shifted,
        (dpre_out, shifted_out, bias_out.at[pl.ds(0, SUBS), :], after),
    )
    bias_out[SUBS:, :] = other_bias[...]
    columns = slice(0, grads[0].shape[-1])
    store_weight_grads(place, (x[...], prev[...]), dpre_out[:, columns], grads, bias_out[:, columns])


def last_kernel(plan, block, *refs):
    place, dpre, shifted = refs[:3]
    near, far = weight_refs(refs[3:], plan)
    out, matrix, weight_sems = refs[-3:]
    weights = Weights(place, 0, near, far, matrix, weight_sems)
    weights.start()
    weights.wait()

    def part(index, carry):
        here = pl.ds(pl.multiple_of(index * block, block), block)
        out[here, :] = input_grad_tile(dpre, shifted, matrix, here)
        return carry

    lax.fori_loop(0, dpre.shape[0] // block, part, 0)


def added(*parts):
    return functools.reduce(jnp.add, [part.astype(F32) for part in parts])


def bias_rows(bias):
    rows = []
    for row in (bias[0:1], bias[SUBS : SUBS + 1]):
        high = row.astype(BF16).astype(F32)
        rows += [high, row - high]
    rows.append(jnp.zeros((BIAS_ROWS - len(rows), bias.shape[1]), F32))
    return jnp.concatenate(rows, axis=0).astype(BF16)


def bias_of(rows):
    rows = rows.astype(F32)
    return jnp.concatenate([rows[0:1] + rows[1:2], rows[2:3] + rows[3:4]], axis=0)


def sum_in_order(order, values, position):
    for index, value in enumerate(values):
        order[position ^ index] = value
    out = order[0]
    for index in range(1, len(values)):
        out = out + order[index]
    return out


def tap_rows(kept):
    return kept.shape[0] // 8 // 16 * 16


def block_of(tap, chip, height):
    row = (tap * 4 + chip) * height
    return pl.ds(row if isinstance(row, int) else pl.multiple_of(row, 16), height)


def chip_sum(kept, got, tap, chip, *more):
    height = tap_rows(kept)
    here = block_of(tap, chip, height)
    return added(kept[here, :], got[here, :], *more)


def chip_bias(kept, got):
    height = tap_rows(kept)
    whole = bias_of(kept[8 * height :, :]) + bias_of(got[8 * height :, :])
    return bias_rows(jnp.concatenate([whole[0:1]] * SUBS + [whole[1:2]] * SUBS, axis=0))


def corner_kernel(split, *refs):
    kept, got = refs[:2]
    by_x, by_y = refs[-2:]
    height = tap_rows(kept)
    for tap, (out, chip) in enumerate(((by_x, 1), (by_y, 2))):
        out[0:height, :] = chip_sum(kept, got, tap, 3).astype(BF16)
        if split:
            out[height : 2 * height, :] = chip_sum(kept, got, tap, chip).astype(BF16)
            out[2 * height :, :] = chip_bias(kept, got)


def sides_kernel(split, *refs):
    kept, got, from_x, from_y = refs[:4]
    by_x, by_y = refs[-2:]
    height = tap_rows(kept)
    by_x[0:height, :] = chip_sum(kept, got, 1, 1, from_y[0:height, :]).astype(BF16)
    by_y[0:height, :] = chip_sum(kept, got, 0, 2, from_x[0:height, :]).astype(BF16)
    if split:
        by_x[height:, :] = from_y[2 * height :, :]
    else:
        by_x[height:, :] = chip_sum(kept, got, 0, 1).astype(BF16)
        by_y[height:, :] = chip_sum(kept, got, 1, 2).astype(BF16)


def plane_kernel(split, *refs):
    place, kept, got, from_x, from_y, corner_x, corner_y = refs[:7]
    height = tap_rows(kept)
    beside = pl.ds(height, height)
    direct = (corner_x, corner_y) if split else (from_x, from_y)
    sums = [
        chip_sum(kept, got, 0, 0, direct[0][beside, :], from_y[0:height, :]),
        chip_sum(kept, got, 1, 0, direct[1][beside, :], from_x[0:height, :]),
    ]
    if split:
        mine, other, order = refs[-3:]
        parts = [chip_bias(kept, got), corner_x[2 * height :, :], corner_y[2 * height :, :], from_x[height:, :]]
        whole = sum_in_order(order, [bias_of(part) for part in parts], place[1] // 2)
        whole = bias_rows(jnp.concatenate([whole[0:1]] * SUBS + [whole[1:2]] * SUBS, axis=0))
        mine[height:, :] = whole.astype(F32)
        other[height:, :] = whole
    else:
        mine, other = refs[-2:]
    odd = place[0] % 2 == 1
    mine[0:height, :] = jnp.where(odd, sums[1], sums[0])
    other[0:height, :] = jnp.where(odd, sums[0], sums[1]).astype(BF16)


def pair_kernel(*refs):
    mine, got, *_, out = refs
    out[...] = added(mine[...], got[...])


def crossing_kernel(columns, *refs):
    place, mine, got, second = refs[:4]
    kept, out = refs[-2:]
    height = second.shape[0]
    sums = (added(mine[0:height, :], got[0:height, :]), second[:, columns])
    upper = place[0] >= 2
    kept[0:height, :] = jnp.where(upper, sums[1], sums[0])
    out[0:height, :] = jnp.where(upper, sums[0], sums[1]).astype(BF16)
    whole = bias_of(mine[height:, :]) + bias_of(got[height:, :])
    whole = bias_rows(jnp.concatenate([whole[0:1]] * SUBS + [whole[1:2]] * SUBS, axis=0))
    kept[height:, :] = whole.astype(F32)
    out[height:, :] = whole


def whole_kernel(parts, *refs):
    out, bias_out = refs[-2:]
    height = out.shape[0]
    for index, columns in enumerate(parts):
        kept, got = refs[2 * index : 2 + 2 * index]
        out[:, columns] = added(kept[0:height, :], got[0:height, :])
        bias_out[:, columns] = bias_of(kept[height:, :]) + bias_of(got[height:, :])


def call(kernel, outs, in_specs, out_specs, scratch, flops, moved, megabytes, name):
    return pl.pallas_call(
        kernel,
        out_shape=outs,
        in_specs=in_specs,
        out_specs=out_specs,
        scratch_shapes=scratch,
        compiler_params=pltpu.CompilerParams(vmem_limit_bytes=megabytes * 2**20),
        cost_estimate=pl.CostEstimate(flops=flops // COST, bytes_accessed=moved // COST, transcendentals=0),
        name=name,
    )


def small_call(kernel, outs, operands, name, ties=(), scratch=()):
    has_place = operands[0].dtype == jnp.int32
    specs = [SMEM if has_place and index == 0 else VMEM for index in range(len(operands))]
    return call(
        kernel,
        outs,
        specs + [ANY] * len(ties),
        [VMEM] * len(outs),
        list(scratch),
        1000000,
        1000000,
        12,
        name,
    )(*operands, *ties)


def swap(value, axis, mask):
    pairs = [(index, index ^ mask) for index in range(lax.axis_size(axis))]
    return lax.ppermute(value, axis, pairs)


def moved(value, axis, target):
    return lax.ppermute(value, axis, [(index, target(index)) for index in range(lax.axis_size(axis))])


def gathered_pieces(place, shard, early):
    height, gates = shard.shape
    chip = jax.ShapeDtypeStruct((2 * height, gates), shard.dtype)

    def joined_cores(own, ties=()):
        return small_call(join_kernel, [chip], [place, own, swap(own, "dp", 1)], "join", ties)[0]

    def beside(unit):
        return moved(unit, "dp", lambda index: index ^ (3 if index % 2 == 0 else 5))

    def opposite(first, second):
        unit = small_call(pick_kernel, [chip], [place, first, second], "pick")[0]
        return moved(unit, "dp", lambda index: index ^ (2 if index % 2 == 0 else 4))

    two = swap(shard, "section", 2)
    one = swap(shard, "section", 1)
    three = swap(two, "section", 1)
    units, got, across = [], [], []
    for own, ties in ((shard, []), (one, [0]), (two, []), (three, [1])):
        ties = [got[index] for index in ties] + (early if len(got) == 1 else [])
        units.append(joined_cores(own, ties))
        got.append(beside(units[-1]))
        if len(got) % 2 == 0:
            across.append(opposite(*got[-2:]))
    out = []
    for pair in range(2):
        for tap in range(2 * pair, 2 * pair + 2):
            out += [units[tap], got[tap], swap(got[tap], "dp", 1)]
        out += [across[pair], swap(across[pair], "dp", 1)]
    return out


class LayerSum:
    def __init__(self, place, kept, sent):
        self.place, self.kept, self.got = place, kept, swap(sent, "dp", 1)
        self.height, self.gates = tap_rows(kept), kept.shape[1]
        self.extra = kept.shape[0] - 8 * self.height

    def rows(self, taps, extra, dtype=BF16):
        return jax.ShapeDtypeStruct((taps * self.height + extra, self.gates), dtype)

    def corners(self, ties=()):
        by_x, by_y = small_call(
            functools.partial(corner_kernel, self.extra > 0),
            [self.rows(2 if self.extra else 1, self.extra)] * 2,
            [self.kept, self.got],
            "corners",
            ties,
        )
        self.corner_sent = by_x
        self.corner_x, self.corner_y = swap(by_x, "dp", 2), swap(by_y, "dp", 4)

    def sides(self, ties=()):
        self.by = small_call(
            functools.partial(sides_kernel, self.extra > 0),
            [self.rows(1, self.extra), self.rows(1, 0)] if self.extra else [self.rows(2, 0)] * 2,
            [self.kept, self.got, self.corner_x, self.corner_y],
            "sides",
            ties,
        )
        self.side_x, self.side_y = swap(self.by[0], "dp", 2), swap(self.by[1], "dp", 4)

    def plane(self, ties=()):
        operands = [self.place, self.kept, self.got, self.side_x, self.side_y, self.corner_x, self.corner_y]
        scratch = []
        if self.extra > 0:
            scratch = [pltpu.VMEM((4, 2, self.gates), F32)]
        self.mine, other = small_call(
            functools.partial(plane_kernel, self.extra > 0),
            [self.rows(1, self.extra, F32), self.rows(1, self.extra)],
            operands,
            "plane",
            ties,
            scratch,
        )
        self.near = swap(other, "section", 1)

    def paired(self):
        return small_call(pair_kernel, [self.rows(1, 0, F32)], [self.mine, self.near], "paired")[0]

    def crossing(self, second, columns, ties=()):
        self.pair, sent = small_call(
            functools.partial(crossing_kernel, columns),
            [self.rows(1, self.extra, F32), self.rows(1, self.extra)],
            [self.place, self.mine, self.near, second],
            "crossing",
            ties,
        )
        self.got_pair = swap(sent, "section", 2)


def all_sums(value):
    for axis in ("dp", "section"):
        mask = 1
        while mask < lax.axis_size(axis):
            value = value + swap(value, axis, mask)
            mask *= 2
    return value


def grouped(value, rows):
    length, width = value.shape
    return value.reshape(length // rows, SUBS, rows // SUBS, width).swapaxes(1, 2).reshape(length, width)


def ungrouped(value):
    rows, width = value.shape
    return value.reshape(rows // SUBS, SUBS, width).swapaxes(0, 1).reshape(rows, width)


def per_device(tokens_in, doc_starts, cotangent, tap_weight, gate_bias):
    sections = lax.axis_size("section")
    streams = lax.axis_size("dp")
    section = lax.axis_index("section")
    stream = lax.axis_index("dp")
    _, length, width = tokens_in.shape
    gates = 3 * width
    tiles = width // LANES
    rows = length // sections
    block = 256
    start = section * rows
    height = tap_weight.shape[1]
    quick = sections == 4 and streams == 8 and height % 16 == 0

    def own(value):
        return lax.dynamic_slice_in_dim(value, start, rows, 0)

    def own(value):
        return lax.dynamic_slice_in_dim(value, start, rows, 0)

    place = jnp.stack([section, stream]).astype(jnp.int32)
    keep = (1 - doc_starts[0]).astype(F32)[:, None]
    keep_own = grouped(jnp.broadcast_to(own(keep), (rows, LANES)), rows)
    keep_firsts = jnp.broadcast_to(jnp.concatenate([keep[::rows], keep[: 8 - sections]], axis=0), (8, LANES))
    x = grouped(own(tokens_in[0]), rows)
    tail = lax.dynamic_slice_in_dim(tokens_in[0], jnp.maximum(start - 16, 0), 16, 0)
    cot = grouped(own(cotangent[0]), rows)
    cot_next = lax.dynamic_slice_in_dim(cotangent[0], jnp.minimum(start + rows, length - 16), 16, 0)
    bias = gate_bias.astype(F32)

    def shape(*dims, dtype=F32):
        return jax.ShapeDtypeStruct(dims, dtype)

    def buffer(*dims, dtype=F32):
        return pltpu.VMEM(dims, dtype)

    dma = pltpu.SemaphoreType.DMA
    layer_flops = 2 * rows * width * gates * 2
    weight_bytes = 4 * width * gates
    half = shape(rows, width, dtype=BF16)
    full = shape(tiles, rows, LANES)
    scan = buffer(tiles, rows, LANES)
    matrix = shape(2 * width, gates, dtype=BF16)

    half = shape(rows, width, dtype=BF16)
    (prev,) = small_call(
        before_kernel,
        [half],
        [place, x, tail, keep_own],
        "before",
        [keep_firsts, cot, cot_next, bias],
        scratch=[buffer(tiles, rows + SUBS, LANES)],
    )
    early = [prev]
    if quick:
        weights = gathered_pieces(place, tap_weight[0], early)
    else:
        whole = lax.all_gather(tap_weight, "dp", axis=1, tiled=True)
        weights = [lax.all_gather(whole, "section", axis=0, tiled=True)]
    plan = len(weights)
    weight_count = plan

    def exchanged(summary):
        return [summary] + [swap(summary, "section", index) for index in range(1, sections)]

    candid0, forget0, gate0, summary = call(
        functools.partial(first_forward_kernel, plan, block),
        [full] * 3 + [shape(8, width)],
        [SMEM] + [VMEM] * 4 + [HBM] * len(weights),
        [VMEM] * 4,
        [buffer(2 * width, gates, dtype=BF16), dma((weight_count + 1,))],
        layer_flops,
        weight_bytes + 30 * rows * width,
        LIMITS[0],
        "first_forward",
    )(place, x, prev, keep_own, bias[0:1], *weights)

    cells0, hidden0, delayed0, last0, candid1, forget1, gate1, summary1, matrix1 = call(
        functools.partial(second_forward_kernel, plan, block),
        [shape(tiles, rows + SUBS, LANES), half, half, shape(8, width)]
        + [full] * 3
        + [shape(16, width), matrix],
        [SMEM] + [VMEM] * 10 + [HBM] * len(weights),
        [VMEM] * 9,
        [
            buffer(sections, 8, width),
            scan,
            buffer(tiles, rows + SUBS, LANES),
            dma((weight_count + 1,)),
        ],
        layer_flops,
        weight_bytes + 20 * rows * width,
        LIMITS[1],
        "second_forward",
    )(place, candid0, forget0, gate0, keep_own, cot, bias[1:2], *exchanged(summary), *weights)

    if quick:

        def kept_and_sent(columns, extra):
            return [shape(8 * height + extra, columns, dtype=BF16)] * 2

        kept_shape = kept_and_sent(gates, 0)
    else:
        kept_shape = [shape(2, width, gates, dtype=BF16)]
    wide = shape(rows, gates, dtype=BF16)

    hidden1, dpre1, shifted1, bias1, lasts, *kept1 = call(
        functools.partial(second_backward_kernel, rows, quick),
        [half, wide, wide, shape(8, gates), shape(2, 1, width)] + kept_shape,
        [SMEM] + [VMEM] * 13,
        [VMEM] * (5 + len(kept_shape)),
        [buffer(sections, 16, width), buffer(tiles, rows + SUBS, LANES), scan, buffer(3, rows + SUBS, LANES), buffer(SUBS, gates)],
        layer_flops,
        weight_bytes + 30 * rows * width,
        LIMITS[2],
        "second_backward",
    )(
        place, candid1, forget1, gate1, hidden0, delayed0, keep_own, cot, cot_next, keep_firsts,
        *exchanged(summary1),
    )

    arriving, summary0 = call(
        functools.partial(middle_kernel, rows, block),
        [half, shape(8, width)],
        [SMEM] + [VMEM] * 7,
        [VMEM] * 2,
        [scan],
        layer_flops,
        weight_bytes + 20 * rows * width,
        LIMITS[3],
        "middle",
    )(place, dpre1, shifted1, candid0, forget0, gate0, keep_own, matrix1)

    summaries = exchanged(summary0)
    ties = []
    first_shape, first_columns = kept_shape, gates
    if quick:
        second = LayerSum(place, *kept1)
        second.corners(ties=[arriving])
        second.sides(ties=summaries[1:])
        ties = second.by
        first_columns = gates // LANES * 3 // 5 * LANES
        first_shape = kept_and_sent(first_columns, BIAS_ROWS)
    dpre0, shifted0, bias_both, *kept0 = call(
        functools.partial(first_backward_kernel, rows, quick),
        [wide, wide, shape(2 * SUBS, gates)] + first_shape,
        [SMEM] + [VMEM] * 15 + [ANY] * len(ties),
        [VMEM] * (3 + len(kept_shape)),
        [buffer(sections, 8, width), scan, buffer(3, rows + SUBS, LANES), buffer(SUBS, gates)],
        layer_flops,
        weight_bytes + 30 * rows * width,
        LIMITS[4],
        "first_backward",
    )(
        place, candid0, forget0, gate0, cells0, last0, x, prev, keep_own, arriving, keep_firsts, bias1,
        *summaries, *ties,
    )
    if quick:
        later = small_call(
            functools.partial(first_weights_kernel, first_columns),
            kept_and_sent(gates - first_columns, BIAS_ROWS),
            [place, x, prev, dpre0, bias_both],
            "first_weights",
        )
        parts = [slice(0, first_columns), slice(first_columns, gates)]
        sums = [LayerSum(place, *pieces) for pieces in (kept0, later)]
        sums[0].corners()
        ties = [sums[0].corner_sent]

    input_grad = call(
        functools.partial(last_kernel, plan, block),
        shape(rows, width),
        [SMEM] + [VMEM] * 2 + [HBM] * len(weights) + [ANY] * len(ties),
        VMEM,
        [buffer(2 * width, gates, dtype=BF16), dma((weight_count + 1,))],
        COST * layer_flops,
        COST * weight_bytes,
        LIMITS[5],
        "last",
    )(place, dpre0, shifted0, *weights, *ties)

    if quick:
        second.plane(ties=[input_grad])
        sums[1].corners(ties=[second.mine])
        sums[0].sides(ties=[sums[1].corner_sent])
        pair = second.paired()
        sums[0].plane()
        sums[1].sides(ties=[sums[0].mine])
        sums[0].crossing(pair, parts[0])
        sums[1].plane(ties=[sums[0].pair])
        sums[1].crossing(pair, parts[1], ties=[sums[0].got_pair])
        weight_grad, bias_grad = small_call(
            functools.partial(whole_kernel, parts),
            [shape(height, gates), shape(2, gates)],
            [value for part in sums for value in (part.pair, part.got_pair)],
            "whole",
        )
        weight_grad = weight_grad[None]
    else:
        bias_grad = all_sums(bias_both[::8])
        stacked = jnp.concatenate([kept0[0], kept1[0]], axis=0)
        by_rows = lax.psum_scatter(stacked, "dp", scatter_dimension=1, tiled=True)
        weight_grad = lax.psum_scatter(by_rows, "section", scatter_dimension=0, tiled=True).astype(F32)
    return (ungrouped(hidden1)[None], ungrouped(input_grad)[None], weight_grad, bias_grad, lasts)


def solution(mesh):
    in_specs = (
        P("dp", None, None),
        P("dp", None),
        P("dp", None, None),
        P("section", "dp", None),
        P(),
    )
    out_specs = (
        P("dp", "section", None),
        P("dp", "section", None),
        P("section", "dp", None),
        P(),
        P(None, "dp", None),
    )
    return jax.shard_map(
        per_device, mesh=mesh, in_specs=in_specs, out_specs=out_specs, check_vma=False
    )
```

```python
import functools

import jax
import jax.numpy as jnp
from jax import lax
from jax.experimental import pallas as pl
from jax.experimental.pallas import tpu as pltpu
from jax.sharding import PartitionSpec as P

F32 = jnp.float32
BF16 = jnp.bfloat16
LANES = 128
SUBS = 8
BIAS_ROWS = 16
COST = 100
UNROLL = 32
LIMITS = (14, 16, 16, 12, 16, 12)
ANY = pl.BlockSpec(memory_space=pl.ANY)
HBM = pl.BlockSpec(memory_space=pltpu.HBM)
VMEM = pl.BlockSpec(memory_space=pltpu.VMEM)
SMEM = pl.BlockSpec(memory_space=pltpu.SMEM)


def tiles_of(ref):
    return range(ref.shape[0])


def columns_of(tile):
    return slice(tile * LANES, (tile + 1) * LANES)


def joined(tiles):
    return jnp.concatenate(tiles, axis=1)


def first_row(ref):
    return joined([ref[tile, 0:1, :] for tile in tiles_of(ref)])


def ones_and_zeros(tiles):
    return [jnp.ones((SUBS, LANES), F32)] * tiles, [jnp.zeros((SUBS, LANES), F32)] * tiles


def over_steps(steps, body, state):
    def turn(index, state):
        for part in range(UNROLL):
            state = body(index * UNROLL + part, state)
        return state

    return lax.fori_loop(0, steps // UNROLL, turn, state)


def group(step):
    row = step * SUBS
    return pl.ds(row if isinstance(row, int) else pl.multiple_of(row, SUBS), SUBS)


def forward_steps(candid, forget, keep, first, steps, gains, cells):
    def body(step, state):
        gains, cells = state
        spot = group(first + step)
        kept = keep[spot, :]
        new_gains, new_cells = [], []
        for tile, (gain, cell) in enumerate(zip(gains, cells, strict=True)):
            share = forget[tile, spot, :]
            now = share * kept
            new_cells.append(now * cell + (1.0 - share) * candid[tile, spot, :])
            new_gains.append(gain * now)
        return new_gains, new_cells

    return over_steps(steps, body, (list(gains), list(cells)))


def forward_entries(gains, cells, carry):
    gain, cell = joined(gains), joined(cells)
    entries = []
    for sub in range(SUBS):
        entries.append(carry)
        carry = cell[sub : sub + 1] + gain[sub : sub + 1] * carry
    return jnp.concatenate(entries, axis=0), carry


def forward_fill(candid, forget, keep, steps, entries, out):
    cells = [entries[:, columns_of(tile)] for tile in tiles_of(out)]
    for tile in tiles_of(out):
        out[tile, group(0), :] = cells[tile]

    def body(step, cells):
        spot = group(step)
        kept = keep[spot, :]
        new_cells = []
        for tile, cell in enumerate(cells):
            share = forget[tile, spot, :]
            cell = share * kept * cell + (1.0 - share) * candid[tile, spot, :]
            out[tile, group(step + 1), :] = cell
            new_cells.append(cell)
        return new_cells

    over_steps(steps, body, cells)


def backward_steps(forget, keep, emit, steps):
    tiles = emit.shape[0]

    def body(step, state):
        gains, backs = state
        spot = group(steps - 1 - step)
        kept = keep[spot, :]
        new_gains, new_backs = [], []
        for tile, (gain, back) in enumerate(zip(gains, backs, strict=True)):
            now = forget[tile, spot, :] * kept
            new_backs.append(now * (emit[tile, spot, :] + back))
            new_gains.append(gain * now)
        return new_gains, new_backs

    state = ones_and_zeros(tiles)
    whole = (steps - 1) // UNROLL * UNROLL
    state = over_steps(whole, body, state)
    for step in range(whole, steps - 1):
        state = body(step, state)
    first_gains, backs = state
    firsts = [emit[tile, group(0), :] + backs[tile] for tile in range(tiles)]
    gains, backs = body(steps - 1, state)
    return joined(gains), joined(backs), joined(first_gains), joined(firsts)


def backward_entries(gain, back, carry):
    entries = []
    for sub in reversed(range(SUBS)):
        entries.append(carry)
        carry = back[sub : sub + 1] + gain[sub : sub + 1] * carry
    return jnp.concatenate(entries[::-1], axis=0)


def backward_fill(forget, keep, emit, steps, entries):
    def body(step, backs):
        spot = group(steps - 1 - step)
        kept = keep[spot, :]
        new_backs = []
        for tile, back in enumerate(backs):
            now = emit[tile, spot, :] + back
            emit[tile, spot, :] = now
            new_backs.append(forget[tile, spot, :] * kept * now)
        return new_backs

    over_steps(steps, body, [entries[:, columns_of(tile)] for tile in tiles_of(emit)])


def chunk_backward_summary(forget, keep, emit, steps):
    gain, back, first_gain, first = backward_steps(forget, keep, emit, steps)
    gain_all = jnp.ones_like(gain[0:1])
    back_all = jnp.zeros_like(gain[0:1])
    for sub in reversed(range(SUBS)):
        entry_gain, entry_back = gain_all, back_all
        gain_all = gain[sub : sub + 1] * entry_gain
        back_all = back[sub : sub + 1] + gain[sub : sub + 1] * entry_back
    row_gain = first_gain[0:1] * entry_gain
    row_value = first[0:1] + first_gain[0:1] * entry_back
    return gain_all, back_all, row_gain, row_value


def store_gates(pre, here, candid_out, forget_out, gate_out):
    tiles = candid_out.shape[0]
    for tile in range(tiles):
        candid_out[tile, here, :] = jnp.tanh(pre[:, columns_of(tile)])
        forget_out[tile, here, :] = jax.nn.sigmoid(pre[:, columns_of(tiles + tile)])
        if gate_out is not None:
            gate_out[tile, here, :] = jax.nn.sigmoid(pre[:, columns_of(2 * tiles + tile)])


class Weights:
    def __init__(self, place, layer, near, far, target, sems):
        self.place, self.layer, self.target, self.sems = place, layer, target, sems
        self.near, self.far = near, far

    def each(self, pieces, act):
        section, core, chip = self.place[0], self.place[1] % 2, self.place[1] // 2
        width = self.target.shape[0] // 2
        height = pieces[0].shape[0]
        places = []
        for tap in range(2):
            places += [(tap, chip), (tap, chip ^ (2 - core)), (tap, chip ^ (1 + core))]
        places += [(core, chip ^ 3), (1 - core, chip ^ 3)]
        for index, (piece, (tap, rows)) in enumerate(zip(pieces, places, strict=True)):
            row = ((section % 2) ^ tap) * width + rows * height
            target = self.target.at[pl.ds(pl.multiple_of(row, 16), height), :]
            act(pltpu.make_async_copy(piece, target, self.sems.at[index]))

    def both(self, act):
        if self.far is None:
            width = self.target.shape[0] // 2
            for tap in range(2):
                act(
                    pltpu.make_async_copy(
                        self.near.at[2 * self.layer + tap],
                        self.target.at[pl.ds(tap * width, width), :],
                        self.sems.at[tap],
                    )
                )
            return
        is_near = self.place[0] // 2 == self.layer

        @pl.when(is_near)
        def _():
            self.each(self.near, act)

        @pl.when(jnp.logical_not(is_near))
        def _():
            self.each(self.far, act)

    def start(self):
        self.both(lambda copy: copy.start())

    def wait(self):
        self.both(lambda copy: copy.wait())


def weight_refs(refs, count):
    if count == 1:
        return refs[0], None
    return refs[: count // 2], refs[count // 2 : count]


def join_kernel(place, own, got, *refs):
    out = refs[-1]
    height = own.shape[0]
    core = place[1] % 2
    out[pl.ds(pl.multiple_of(core * height, 16), height), :] = own[...]
    out[pl.ds(pl.multiple_of((1 - core) * height, 16), height), :] = got[...]


def pick_kernel(place, first, second, out):
    @pl.when(place[1] % 2 == 0)
    def _():
        out[...] = first[...]

    @pl.when(place[1] % 2 == 1)
    def _():
        out[...] = second[...]


def before_kernel(*refs):
    place, x, tail, keep = refs[:4]
    prev, shifted = refs[-2:]
    rows, width = x.shape
    top = jnp.where(place[0] > 0, tail[...].astype(F32)[15:16], 0.0)
    for tile in range(width // LANES):
        columns = columns_of(tile)
        shifted[tile, pl.ds(SUBS, rows), :] = x[:, columns].astype(F32)
        shifted[tile, group(0), :] = jnp.concatenate(
            [top[:, columns], shifted[tile, rows : rows + SUBS - 1, :]], axis=0
        )
        prev[:, columns] = (shifted[tile, pl.ds(0, rows), :] * keep[...]).astype(BF16)


def forward_gates(x, prev, matrix, bias, keep, block, candid_out, forget_out, gate_out, finish=None):
    rows, width = x.shape
    tiles = candid_out.shape[0]
    block_steps = block // SUBS

    def part(index, state):
        here = pl.ds(pl.multiple_of(index * block, block), block)
        pre = (
            jnp.dot(x[here, :], matrix[:width, :], preferred_element_type=F32)
            + jnp.dot(prev[here, :], matrix[width:, :], preferred_element_type=F32)
            + bias[...]
        )
        store_gates(pre, here, candid_out, forget_out, gate_out)
        if finish is not None:
            finish(here)
        return forward_steps(candid_out, forget_out, keep, index * block_steps, block_steps, *state)

    return lax.fori_loop(0, rows // block, part, ones_and_zeros(tiles))


def first_forward_kernel(plan, block, *refs):
    place, x, prev, keep, bias = refs[:5]
    near, far = weight_refs(refs[5:], plan)
    candid_out, forget_out, gate_out, summary_out, matrix, weight_sems = refs[5 + plan :]
    rows, width = x.shape
    weights = Weights(place, 0, near, far, matrix, weight_sems)
    weights.start()
    weights.wait()
    gains, cells = forward_gates(x, prev, matrix, bias, keep, block, candid_out, forget_out, gate_out)
    gain_all, cell_all = jnp.ones((1, width), F32), jnp.zeros((1, width), F32)
    gain, cell = joined(gains), joined(cells)
    for sub in range(SUBS):
        cell_all = cell[sub : sub + 1] + gain[sub : sub + 1] * cell_all
        gain_all = gain[sub : sub + 1] * gain_all
    last_gate = joined([gate_out[tile, rows - 1 : rows, :] for tile in tiles_of(gate_out)])
    parts = [gain_all, cell_all, last_gate] + [jnp.zeros((1, width), F32)] * 5
    summary_out[...] = jnp.concatenate(parts, axis=0)


def second_forward_kernel(plan, block, *refs):
    place, candid, forget, gate, keep, cot, bias = refs[:7]
    summaries = refs[7:11]
    near, far = weight_refs(refs[11:], plan)
    (
        cell_out,
        hidden,
        delayed,
        last,
        candid_out,
        forget_out,
        gate_out,
        summary_out,
        matrix,
        order,
        emit,
        shifted,
        weight_sems,
    ) = refs[11 + plan :]
    section = place[0]
    rows, width = hidden.shape
    tiles = emit.shape[0]
    steps = rows // SUBS
    weights = Weights(place, 1, near, far, matrix, weight_sems)
    weights.start()

    heads = heads_of(order, summaries, section)
    carry = jnp.zeros((1, width), F32)
    carries, hiddens = [], [jnp.zeros((1, width), F32)]
    for head in heads:
        carries.append(carry)
        carry = head[1:2] + head[0:1] * carry
        hiddens.append(head[2:3] * carry)
    gains, cells = forward_steps(candid, forget, keep, 0, steps, *ones_and_zeros(tiles))
    entries, carry = forward_entries(gains, cells, pick(carries, section))
    last[...] = jnp.broadcast_to(carry, last.shape)
    forward_fill(candid, forget, keep, steps, entries, cell_out)
    top = pick(hiddens[:-1], section)
    for tile in range(tiles):
        columns = columns_of(tile)
        shifted[tile, pl.ds(SUBS, rows), :] = gate[tile, :, :] * cell_out[tile, pl.ds(SUBS, rows), :]
        shifted[tile, group(0), :] = jnp.concatenate(
            [top[:, columns], shifted[tile, rows : rows + SUBS - 1, :]], axis=0
        )
        hidden[:, columns] = shifted[tile, pl.ds(SUBS, rows), :].astype(BF16)
        delayed[:, columns] = (shifted[tile, pl.ds(0, rows), :].astype(BF16).astype(F32) * keep[...]).astype(BF16)

    weights.wait()

    def emitted(here):
        for tile in range(tiles):
            emit[tile, here, :] = cot[here, columns_of(tile)].astype(F32) * gate_out[tile, here, :]

    gains, cells = forward_gates(
        hidden, delayed, matrix, bias, keep, block, candid_out, forget_out, gate_out, emitted
    )
    cell_all = forward_entries(gains, cells, jnp.zeros((1, width), F32))[1]
    gain_all, back_all, row_gain, row_value = chunk_backward_summary(forget_out, keep, emit, steps)
    parts = [
        gain_all,
        cell_all,
        back_all,
        row_gain,
        row_value,
        first_row(candid_out),
        first_row(forget_out),
        first_row(gate_out),
        last[0:1, :],
    ]
    parts += [jnp.zeros((1, width), F32)] * (16 - len(parts))
    summary_out[...] = jnp.concatenate(parts, axis=0)


def gate_grads(dcell, before, cell, candid, forget, gate, arriving):
    return (
        dcell * (1.0 - forget) * (1.0 - candid * candid),
        dcell * (before - candid) * forget * (1.0 - forget),
        arriving * cell * gate * (1.0 - gate),
    )


def pick(values, section):
    out = values[0]
    for index in range(1, len(values)):
        out = jnp.where(section == index, values[index], out)
    return out


def first_weights_kernel(first, *refs):
    place, x, prev, dpre, bias = refs[:5]
    store_weight_grads(place, (x[...], prev[...]), dpre[:, first:], refs[-2:], bias[:, first:])


def store_weight_grads(place, lefts, right, outs, bias=None):
    for tap, left in enumerate(lefts):
        grads = lax.dot_general(left, right, (((0,), (0,)), ((), ())), preferred_element_type=F32).astype(BF16)
        if len(outs) == 1:
            outs[0][tap] = grads
            continue
        kept, sent = outs
        height = tap_rows(kept)
        chip, odd = place[1] // 2, place[1] % 2 == 1
        for index in range(4):
            even_rows = grads[2 * index * height : (2 * index + 1) * height]
            odd_rows = grads[(2 * index + 1) * height : (2 * index + 2) * height]
            here = block_of(tap, index ^ chip, height)
            kept[here, :] = jnp.where(odd, odd_rows, even_rows)
            sent[here, :] = jnp.where(odd, even_rows, odd_rows)
    if bias is not None and len(outs) > 1:
        for out in outs:
            out[8 * tap_rows(out) :, :] = bias_rows(bias)


def heads_of(order, summaries, section):
    for index, summary in enumerate(summaries):
        order[section ^ index] = summary[...]
    return [order[index] for index in range(len(summaries))]


def back_entries(heads):
    back = jnp.zeros_like(heads[0][0:1])
    backs = []
    for head in reversed(heads):
        backs.append(back)
        back = head[2:3] + head[0:1] * back
    return backs[::-1]


def following_row(heads, backs, section, keep_firsts, cell, arriving):
    nexts = [min(index + 1, len(heads) - 1) for index in range(len(heads))]
    head = pick([heads[index] for index in nexts], section)
    back = pick([backs[index] for index in nexts], section)
    valid = jnp.where(section < len(heads) - 1, 1.0, 0.0)
    keep = pick([keep_firsts[index : index + 1, :] for index in nexts], section)
    keep = joined([keep] * (cell.shape[1] // LANES))
    candid, forget, gate = head[5:6], head[6:7], head[7:8]
    if arriving is None:
        arriving = head[1:2]
    before = keep * cell
    after = forget * before + (1.0 - forget) * candid
    dcell = (head[4:5] + head[3:4] * back) * valid
    return gate_grads(dcell, before, after, candid, forget, gate, arriving * valid), keep


def store_grads(rows, dcells, cells, candid, forget, gate, arriving, keep, next_first, extra, shifted, outs):
    dpre_out, shifted_out, bias_out, after = outs
    tiles = dcells.shape[0]
    width = tiles * LANES
    part_rows = 64
    for index in range(3):
        rounded = extra[index].astype(BF16).astype(F32) * joined([next_first[:, :LANES]] * tiles)
        after[:, index * width : (index + 1) * width] = jnp.broadcast_to(rounded, (SUBS, width))

    def of_tile(tile, carry):
        def of_rows(part, sums):
            base = pl.multiple_of(part * part_rows, part_rows)
            here = pl.ds(base, part_rows)
            kept = keep[here, :]
            parts = gate_grads(
                dcells[tile, here, :],
                cells[tile, here, :] * kept,
                cells[tile, pl.ds(pl.multiple_of(base + SUBS, SUBS), part_rows), :],
                candid[tile, here, :],
                forget[tile, here, :],
                gate[tile, here, :],
                arriving[here, pl.ds(pl.multiple_of(tile * LANES, LANES), LANES)].astype(F32),
            )
            new_sums = []
            for index, part in enumerate(parts):
                rounded = part.astype(BF16)
                columns = pl.ds(pl.multiple_of((index * tiles + tile) * LANES, LANES), LANES)
                dpre_out[here, columns] = rounded
                rounded = rounded.astype(F32)
                shifted[index, here, :] = rounded * kept
                new_sums.append(
                    sums[index] + jnp.sum(rounded.reshape(part_rows // SUBS, SUBS, LANES), axis=0)
                )
            return new_sums

        sums = lax.fori_loop(0, rows // part_rows, of_rows, [jnp.zeros((SUBS, LANES), F32)] * 3)
        for index in range(3):
            columns = pl.ds(pl.multiple_of((index * tiles + tile) * LANES, LANES), LANES)
            shifted[index, pl.ds(rows, SUBS), :] = jnp.concatenate(
                [shifted[index, 1:SUBS, :], after[0:1, columns]], axis=0
            )
            shifted_out[:, columns] = shifted[index, pl.ds(SUBS, rows), :].astype(BF16)
            bias_out[:, columns] = jnp.broadcast_to(
                jnp.sum(sums[index], axis=0, keepdims=True), (bias_out.shape[0], LANES)
            )
        return carry

    lax.fori_loop(0, tiles, of_tile, 0)


def second_backward_kernel(rows, has_sent, *refs):
    (place, candid, forget, gate, hidden, delayed, keep, cot, cot_next, keep_firsts) = refs[:10]
    summaries = refs[10:14]
    outs = refs[14:]
    hidden_out, dpre_out, shifted_out, bias_out, last_out = outs[:5]
    grads = outs[5 : 7 if has_sent else 6]
    order, cells, dcells, shifted, after = refs[-5:]
    section = place[0]
    width = hidden.shape[1]
    tiles = dcells.shape[0]
    steps = rows // SUBS
    heads = heads_of(order, summaries, section)
    carry = jnp.zeros((1, width), F32)
    carries = []
    for head in heads:
        carries.append(carry)
        carry = head[1:2] + head[0:1] * carry
    last_out[0] = heads[-1][8:9]
    last_out[1] = carry
    backs = back_entries(heads)
    carry = pick(carries, section)
    back = pick(backs, section)
    for tile in range(tiles):
        dcells[tile, :, :] = cot[:, columns_of(tile)].astype(F32) * gate[tile, :, :]
    gains, ends = forward_steps(candid, forget, keep, 0, steps, *ones_and_zeros(tiles))
    entries, carry = forward_entries(gains, ends, carry)
    forward_fill(candid, forget, keep, steps, entries, cells)
    for tile in range(tiles):
        hidden_out[:, columns_of(tile)] = (gate[tile, :, :] * cells[tile, pl.ds(SUBS, rows), :]).astype(BF16)
    gain, leaving, _, _ = backward_steps(forget, keep, dcells, steps)
    backward_fill(forget, keep, dcells, steps, backward_entries(gain, leaving, back))
    extra, next_first = following_row(heads, backs, section, keep_firsts, carry, cot_next[...].astype(F32)[0:1])
    store_grads(
        rows, dcells, cells, candid, forget, gate, cot, keep, next_first, extra, shifted,
        (dpre_out, shifted_out, bias_out, after),
    )
    store_weight_grads(place, (hidden[...], delayed[...]), dpre_out[...], grads)


def input_grad_tile(dpre, shifted, matrix, here):
    width = matrix.shape[0] // 2
    contract = (((1,), (1,)), ((), ()))
    return lax.dot_general(
        dpre[here, :], matrix[:width, :], contract, preferred_element_type=F32
    ) + lax.dot_general(shifted[here, :], matrix[width:, :], contract, preferred_element_type=F32)


def middle_kernel(rows, block, *refs):
    place, dpre, shifted, candid, forget, gate, keep, matrix = refs[:8]
    arriving_out, summary_out, emit = refs[8:]

    def part(index, carry):
        here = pl.ds(pl.multiple_of(index * block, block), block)
        arriving = input_grad_tile(dpre, shifted, matrix, here).astype(BF16)
        arriving_out[here, :] = arriving
        for tile in tiles_of(emit):
            emit[tile, here, :] = arriving[:, columns_of(tile)].astype(F32) * gate[tile, here, :]
        return carry

    lax.fori_loop(0, rows // block, part, 0)
    row_arriving = arriving_out[0:16, :].astype(F32)[0:1]
    gain_all, back_all, row_gain, row_value = chunk_backward_summary(forget, keep, emit, rows // SUBS)
    parts = [
        gain_all,
        row_arriving,
        back_all,
        row_gain,
        row_value,
        first_row(candid),
        first_row(forget),
        first_row(gate),
    ]
    summary_out[...] = jnp.concatenate(parts, axis=0)


def first_backward_kernel(rows, has_sent, *refs):
    (place, candid, forget, gate, cells, last, x, prev, keep, arriving, keep_firsts, other_bias) = refs[:12]
    summaries = refs[12:16]
    order, dcells, shifted, after = refs[-4:]
    outs = refs[-11:-4] if has_sent else refs[-8:-4]
    dpre_out, shifted_out, bias_out, *grads = outs
    section = place[0]
    steps = rows // SUBS
    heads = heads_of(order, summaries, section)
    backs = back_entries(heads)
    back = pick(backs, section)
    for tile in tiles_of(dcells):
        dcells[tile, :, :] = arriving[:, columns_of(tile)].astype(F32) * gate[tile, :, :]
    gain, leaving, _, _ = backward_steps(forget, keep, dcells, steps)
    backward_fill(forget, keep, dcells, steps, backward_entries(gain, leaving, back))
    extra, next_first = following_row(heads, backs, section, keep_firsts, last[0:1, :], None)
    store_grads(
        rows, dcells, cells, candid, forget, gate, arriving, keep, next_first, extra, shifted,
        (dpre_out, shifted_out, bias_out.at[pl.ds(0, SUBS), :], after),
    )
    bias_out[SUBS:, :] = other_bias[...]
    done = 0
    for part in range(0, len(grads), 2):
        columns = slice(done, done + grads[part].shape[-1])
        store_weight_grads(
            place, (x[...], prev[...]), dpre_out[:, columns], grads[part : part + 2], bias_out[:, columns]
        )
        done = columns.stop


def last_kernel(plan, block, *refs):
    place, dpre, shifted = refs[:3]
    near, far = weight_refs(refs[3:], plan)
    out, matrix, weight_sems = refs[-3:]
    weights = Weights(place, 0, near, far, matrix, weight_sems)
    weights.start()
    weights.wait()

    def part(index, carry):
        here = pl.ds(pl.multiple_of(index * block, block), block)
        out[here, :] = input_grad_tile(dpre, shifted, matrix, here)
        return carry

    lax.fori_loop(0, dpre.shape[0] // block, part, 0)


def added(*parts):
    return functools.reduce(jnp.add, [part.astype(F32) for part in parts])


def bias_rows(bias):
    rows = []
    for row in (bias[0:1], bias[SUBS : SUBS + 1]):
        high = row.astype(BF16).astype(F32)
        rows += [high, row - high]
    rows.append(jnp.zeros((BIAS_ROWS - len(rows), bias.shape[1]), F32))
    return jnp.concatenate(rows, axis=0).astype(BF16)


def bias_of(rows):
    rows = rows.astype(F32)
    return jnp.concatenate([rows[0:1] + rows[1:2], rows[2:3] + rows[3:4]], axis=0)


def sum_in_order(order, values, position):
    for index, value in enumerate(values):
        order[position ^ index] = value
    out = order[0]
    for index in range(1, len(values)):
        out = out + order[index]
    return out


def tap_rows(kept):
    return kept.shape[0] // 8 // 16 * 16


def block_of(tap, chip, height):
    row = (tap * 4 + chip) * height
    return pl.ds(row if isinstance(row, int) else pl.multiple_of(row, 16), height)


def chip_sum(kept, got, tap, chip, *more):
    height = tap_rows(kept)
    here = block_of(tap, chip, height)
    return added(kept[here, :], got[here, :], *more)


def chip_bias(kept, got):
    height = tap_rows(kept)
    whole = bias_of(kept[8 * height :, :]) + bias_of(got[8 * height :, :])
    return bias_rows(jnp.concatenate([whole[0:1]] * SUBS + [whole[1:2]] * SUBS, axis=0))


def corner_kernel(split, *refs):
    kept, got = refs[:2]
    by_x, by_y = refs[-2:]
    height = tap_rows(kept)
    for tap, (out, chip) in enumerate(((by_x, 1), (by_y, 2))):
        out[0:height, :] = chip_sum(kept, got, tap, 3).astype(BF16)
        if split:
            out[height : 2 * height, :] = chip_sum(kept, got, tap, chip).astype(BF16)
            out[2 * height :, :] = chip_bias(kept, got)


def sides_kernel(split, *refs):
    kept, got, from_x, from_y = refs[:4]
    by_x, by_y = refs[-2:]
    height = tap_rows(kept)
    by_x[0:height, :] = chip_sum(kept, got, 1, 1, from_y[0:height, :]).astype(BF16)
    by_y[0:height, :] = chip_sum(kept, got, 0, 2, from_x[0:height, :]).astype(BF16)
    if split:
        by_x[height:, :] = from_y[2 * height :, :]
    else:
        by_x[height:, :] = chip_sum(kept, got, 0, 1).astype(BF16)
        by_y[height:, :] = chip_sum(kept, got, 1, 2).astype(BF16)


def plane_kernel(split, *refs):
    place, kept, got, from_x, from_y, corner_x, corner_y = refs[:7]
    height = tap_rows(kept)
    beside = pl.ds(height, height)
    direct = (corner_x, corner_y) if split else (from_x, from_y)
    sums = [
        chip_sum(kept, got, 0, 0, direct[0][beside, :], from_y[0:height, :]),
        chip_sum(kept, got, 1, 0, direct[1][beside, :], from_x[0:height, :]),
    ]
    if split:
        mine, other, order = refs[-3:]
        parts = [chip_bias(kept, got), corner_x[2 * height :, :], corner_y[2 * height :, :], from_x[height:, :]]
        whole = sum_in_order(order, [bias_of(part) for part in parts], place[1] // 2)
        whole = bias_rows(jnp.concatenate([whole[0:1]] * SUBS + [whole[1:2]] * SUBS, axis=0))
        mine[height:, :] = whole.astype(F32)
        other[height:, :] = whole
    else:
        mine, other = refs[-2:]
    odd = place[0] % 2 == 1
    mine[0:height, :] = jnp.where(odd, sums[1], sums[0])
    other[0:height, :] = jnp.where(odd, sums[0], sums[1]).astype(BF16)


def pair_kernel(*refs):
    mine, got, *_, out = refs
    out[...] = added(mine[...], got[...])


def crossing_kernel(columns, *refs):
    place, mine, got, second = refs[:4]
    kept, out = refs[-2:]
    height = second.shape[0]
    sums = (added(mine[0:height, :], got[0:height, :]), second[:, columns])
    upper = place[0] >= 2
    kept[0:height, :] = jnp.where(upper, sums[1], sums[0])
    out[0:height, :] = jnp.where(upper, sums[0], sums[1]).astype(BF16)
    whole = bias_of(mine[height:, :]) + bias_of(got[height:, :])
    whole = bias_rows(jnp.concatenate([whole[0:1]] * SUBS + [whole[1:2]] * SUBS, axis=0))
    kept[height:, :] = whole.astype(F32)
    out[height:, :] = whole


def whole_kernel(parts, *refs):
    out, bias_out = refs[-2:]
    height = out.shape[0]
    for index, columns in enumerate(parts):
        kept, got = refs[2 * index : 2 + 2 * index]
        out[:, columns] = added(kept[0:height, :], got[0:height, :])
        bias_out[:, columns] = bias_of(kept[height:, :]) + bias_of(got[height:, :])


def call(kernel, outs, in_specs, out_specs, scratch, flops, moved, megabytes, name):
    return pl.pallas_call(
        kernel,
        out_shape=outs,
        in_specs=in_specs,
        out_specs=out_specs,
        scratch_shapes=scratch,
        compiler_params=pltpu.CompilerParams(vmem_limit_bytes=megabytes * 2**20),
        cost_estimate=pl.CostEstimate(flops=flops // COST, bytes_accessed=moved // COST, transcendentals=0),
        name=name,
    )


def small_call(kernel, outs, operands, name, ties=(), scratch=(), flops=1000000):
    has_place = operands[0].dtype == jnp.int32
    specs = [SMEM if has_place and index == 0 else VMEM for index in range(len(operands))]
    return call(
        kernel,
        outs,
        specs + [ANY] * len(ties),
        [VMEM] * len(outs),
        list(scratch),
        flops,
        1000000,
        12,
        name,
    )(*operands, *ties)


def swap(value, axis, mask):
    pairs = [(index, index ^ mask) for index in range(lax.axis_size(axis))]
    return lax.ppermute(value, axis, pairs)


def moved(value, axis, target):
    return lax.ppermute(value, axis, [(index, target(index)) for index in range(lax.axis_size(axis))])


def gathered_pieces(place, shard, early):
    height, gates = shard.shape
    chip = jax.ShapeDtypeStruct((2 * height, gates), shard.dtype)

    def joined_cores(own, ties=()):
        return small_call(join_kernel, [chip], [place, own, swap(own, "dp", 1)], "join", ties)[0]

    def beside(unit):
        return moved(unit, "dp", lambda index: index ^ (3 if index % 2 == 0 else 5))

    def opposite(first, second):
        unit = small_call(pick_kernel, [chip], [place, first, second], "pick")[0]
        return moved(unit, "dp", lambda index: index ^ (2 if index % 2 == 0 else 4))

    two = swap(shard, "section", 2)
    one = swap(shard, "section", 1)
    three = swap(two, "section", 1)
    units, got, across = [], [], []
    for own, ties in ((shard, []), (one, [0]), (two, []), (three, [1])):
        ties = [got[index] for index in ties] + (early if len(got) == 1 else [])
        units.append(joined_cores(own, ties))
        got.append(beside(units[-1]))
        if len(got) % 2 == 0:
            across.append(opposite(*got[-2:]))
    out = []
    for pair in range(2):
        for tap in range(2 * pair, 2 * pair + 2):
            out += [units[tap], got[tap], swap(got[tap], "dp", 1)]
        out += [across[pair], swap(across[pair], "dp", 1)]
    return out


class LayerSum:
    def __init__(self, place, kept, sent):
        self.place, self.kept, self.got = place, kept, swap(sent, "dp", 1)
        self.height, self.gates = tap_rows(kept), kept.shape[1]
        self.extra = kept.shape[0] - 8 * self.height

    def rows(self, taps, extra, dtype=BF16):
        return jax.ShapeDtypeStruct((taps * self.height + extra, self.gates), dtype)

    def corners(self, ties=()):
        by_x, by_y = small_call(
            functools.partial(corner_kernel, self.extra > 0),
            [self.rows(2 if self.extra else 1, self.extra)] * 2,
            [self.kept, self.got],
            "corners",
            ties,
        )
        self.corner_sent = by_x
        self.corner_x, self.corner_y = swap(by_x, "dp", 2), swap(by_y, "dp", 4)

    def sides(self, ties=()):
        self.by = small_call(
            functools.partial(sides_kernel, self.extra > 0),
            [self.rows(1, self.extra), self.rows(1, 0)] if self.extra else [self.rows(2, 0)] * 2,
            [self.kept, self.got, self.corner_x, self.corner_y],
            "sides",
            ties,
        )
        self.side_x, self.side_y = swap(self.by[0], "dp", 2), swap(self.by[1], "dp", 4)

    def plane(self, ties=(), flops=1000000):
        operands = [self.place, self.kept, self.got, self.side_x, self.side_y, self.corner_x, self.corner_y]
        scratch = []
        if self.extra > 0:
            scratch = [pltpu.VMEM((4, 2, self.gates), F32)]
        self.mine, other = small_call(
            functools.partial(plane_kernel, self.extra > 0),
            [self.rows(1, self.extra, F32), self.rows(1, self.extra)],
            operands,
            "plane",
            ties,
            scratch,
            flops,
        )
        self.near = swap(other, "section", 1)

    def paired(self):
        return small_call(pair_kernel, [self.rows(1, 0, F32)], [self.mine, self.near], "paired")[0]

    def crossing(self, second, columns, ties=()):
        self.pair, sent = small_call(
            functools.partial(crossing_kernel, columns),
            [self.rows(1, self.extra, F32), self.rows(1, self.extra)],
            [self.place, self.mine, self.near, second],
            "crossing",
            ties,
        )
        self.got_pair = swap(sent, "section", 2)


def all_sums(value):
    for axis in ("dp", "section"):
        mask = 1
        while mask < lax.axis_size(axis):
            value = value + swap(value, axis, mask)
            mask *= 2
    return value


def grouped(value, rows):
    length, width = value.shape
    return value.reshape(length // rows, SUBS, rows // SUBS, width).swapaxes(1, 2).reshape(length, width)


def ungrouped(value):
    rows, width = value.shape
    return value.reshape(rows // SUBS, SUBS, width).swapaxes(0, 1).reshape(rows, width)


def per_device(tokens_in, doc_starts, cotangent, tap_weight, gate_bias):
    sections = lax.axis_size("section")
    streams = lax.axis_size("dp")
    section = lax.axis_index("section")
    stream = lax.axis_index("dp")
    _, length, width = tokens_in.shape
    gates = 3 * width
    tiles = width // LANES
    rows = length // sections
    block = 512
    start = section * rows
    height = tap_weight.shape[1]
    quick = sections == 4 and streams == 8 and height % 16 == 0

    def own(value):
        return lax.dynamic_slice_in_dim(value, start, rows, 0)

    def own(value):
        return lax.dynamic_slice_in_dim(value, start, rows, 0)

    place = jnp.stack([section, stream]).astype(jnp.int32)
    keep = (1 - doc_starts[0]).astype(F32)[:, None]
    keep_own = grouped(jnp.broadcast_to(own(keep), (rows, LANES)), rows)
    keep_firsts = jnp.broadcast_to(jnp.concatenate([keep[::rows], keep[: 8 - sections]], axis=0), (8, LANES))
    x = grouped(own(tokens_in[0]), rows)
    tail = lax.dynamic_slice_in_dim(tokens_in[0], jnp.maximum(start - 16, 0), 16, 0)
    cot = grouped(own(cotangent[0]), rows)
    cot_next = lax.dynamic_slice_in_dim(cotangent[0], jnp.minimum(start + rows, length - 16), 16, 0)
    bias = gate_bias.astype(F32)

    def shape(*dims, dtype=F32):
        return jax.ShapeDtypeStruct(dims, dtype)

    def buffer(*dims, dtype=F32):
        return pltpu.VMEM(dims, dtype)

    dma = pltpu.SemaphoreType.DMA
    layer_flops = 2 * rows * width * gates * 2
    weight_bytes = 4 * width * gates
    half = shape(rows, width, dtype=BF16)
    full = shape(tiles, rows, LANES)
    scan = buffer(tiles, rows, LANES)
    matrix = shape(2 * width, gates, dtype=BF16)

    half = shape(rows, width, dtype=BF16)
    (prev,) = small_call(
        before_kernel,
        [half],
        [place, x, tail, keep_own],
        "before",
        [keep_firsts, cot, cot_next, bias],
        scratch=[buffer(tiles, rows + SUBS, LANES)],
    )
    early = [prev]
    if quick:
        weights = gathered_pieces(place, tap_weight[0], early)
    else:
        whole = lax.all_gather(tap_weight, "dp", axis=1, tiled=True)
        weights = [lax.all_gather(whole, "section", axis=0, tiled=True)]
    plan = len(weights)
    weight_count = plan

    def exchanged(summary):
        return [summary] + [swap(summary, "section", index) for index in range(1, sections)]

    candid0, forget0, gate0, summary = call(
        functools.partial(first_forward_kernel, plan, block),
        [full] * 3 + [shape(8, width)],
        [SMEM] + [VMEM] * 4 + [HBM] * len(weights),
        [VMEM] * 4,
        [buffer(2 * width, gates, dtype=BF16), dma((weight_count + 1,))],
        layer_flops,
        weight_bytes + 30 * rows * width,
        LIMITS[0],
        "first_forward",
    )(place, x, prev, keep_own, bias[0:1], *weights)

    cells0, hidden0, delayed0, last0, candid1, forget1, gate1, summary1, matrix1 = call(
        functools.partial(second_forward_kernel, plan, block),
        [shape(tiles, rows + SUBS, LANES), half, half, shape(8, width)]
        + [full] * 3
        + [shape(16, width), matrix],
        [SMEM] + [VMEM] * 10 + [HBM] * len(weights),
        [VMEM] * 9,
        [
            buffer(sections, 8, width),
            scan,
            buffer(tiles, rows + SUBS, LANES),
            dma((weight_count + 1,)),
        ],
        layer_flops,
        weight_bytes + 20 * rows * width,
        LIMITS[1],
        "second_forward",
    )(place, candid0, forget0, gate0, keep_own, cot, bias[1:2], *exchanged(summary), *weights)

    if quick:

        def kept_and_sent(columns, extra):
            return [shape(8 * height + extra, columns, dtype=BF16)] * 2

        kept_shape = kept_and_sent(gates, 0)
    else:
        kept_shape = [shape(2, width, gates, dtype=BF16)]
    wide = shape(rows, gates, dtype=BF16)

    hidden1, dpre1, shifted1, bias1, lasts, *kept1 = call(
        functools.partial(second_backward_kernel, rows, quick),
        [half, wide, wide, shape(8, gates), shape(2, 1, width)] + kept_shape,
        [SMEM] + [VMEM] * 13,
        [VMEM] * (5 + len(kept_shape)),
        [buffer(sections, 16, width), buffer(tiles, rows + SUBS, LANES), scan, buffer(3, rows + SUBS, LANES), buffer(SUBS, gates)],
        layer_flops,
        weight_bytes + 30 * rows * width,
        LIMITS[2],
        "second_backward",
    )(
        place, candid1, forget1, gate1, hidden0, delayed0, keep_own, cot, cot_next, keep_firsts,
        *exchanged(summary1),
    )

    arriving, summary0 = call(
        functools.partial(middle_kernel, rows, block),
        [half, shape(8, width)],
        [SMEM] + [VMEM] * 7,
        [VMEM] * 2,
        [scan],
        layer_flops,
        weight_bytes + 20 * rows * width,
        LIMITS[3],
        "middle",
    )(place, dpre1, shifted1, candid0, forget0, gate0, keep_own, matrix1)

    summaries = exchanged(summary0)
    ties = []
    first_shape, first_columns = kept_shape, gates
    if quick:
        second = LayerSum(place, *kept1)
        second.corners(ties=[arriving])
        second.sides(ties=summaries[1:])
        ties = second.by
        first_columns = gates // LANES * 8 // 15 * LANES
        first_shape = kept_and_sent(first_columns, BIAS_ROWS) + kept_and_sent(gates - first_columns, BIAS_ROWS)
    dpre0, shifted0, bias_both, *kept0 = call(
        functools.partial(first_backward_kernel, rows, quick),
        [wide, wide, shape(2 * SUBS, gates)] + first_shape,
        [SMEM] + [VMEM] * 15 + [ANY] * len(ties),
        [VMEM] * (3 + len(first_shape)),
        [buffer(sections, 8, width), scan, buffer(3, rows + SUBS, LANES), buffer(SUBS, gates)],
        layer_flops,
        weight_bytes + 30 * rows * width,
        LIMITS[4],
        "first_backward",
    )(
        place, candid0, forget0, gate0, cells0, last0, x, prev, keep_own, arriving, keep_firsts, bias1,
        *summaries, *ties,
    )
    input_grad = call(
        functools.partial(last_kernel, plan, block),
        shape(rows, width),
        [SMEM] + [VMEM] * 2 + [HBM] * len(weights),
        VMEM,
        [buffer(2 * width, gates, dtype=BF16), dma((weight_count + 1,))],
        COST * layer_flops,
        COST * weight_bytes,
        LIMITS[5],
        "last",
    )(place, dpre0, shifted0, *weights)

    if quick:
        second.plane(ties=[input_grad], flops=COST * 3 * 10**10)
        parts = [slice(0, first_columns), slice(first_columns, gates)]
        sums = [LayerSum(place, *kept0[:2]), LayerSum(place, *kept0[2:])]
        sums[0].corners(ties=[second.mine])
        sums[1].corners(ties=[sums[0].corner_sent])
        sums[0].sides(ties=[sums[1].corner_sent])
        pair = second.paired()
        sums[0].plane()
        sums[1].sides(ties=[sums[0].mine])
        sums[0].crossing(pair, parts[0])
        sums[1].plane(ties=[sums[0].pair])
        sums[1].crossing(pair, parts[1], ties=[sums[0].got_pair])
        weight_grad, bias_grad = small_call(
            functools.partial(whole_kernel, parts),
            [shape(height, gates), shape(2, gates)],
            [value for part in sums for value in (part.pair, part.got_pair)],
            "whole",
        )
        weight_grad = weight_grad[None]
    else:
        bias_grad = all_sums(bias_both[::8])
        stacked = jnp.concatenate([kept0[0], kept1[0]], axis=0)
        by_rows = lax.psum_scatter(stacked, "dp", scatter_dimension=1, tiled=True)
        weight_grad = lax.psum_scatter(by_rows, "section", scatter_dimension=0, tiled=True).astype(F32)
    return (ungrouped(hidden1)[None], ungrouped(input_grad)[None], weight_grad, bias_grad, lasts)


def solution(mesh):
    in_specs = (
        P("dp", None, None),
        P("dp", None),
        P("dp", None, None),
        P("section", "dp", None),
        P(),
    )
    out_specs = (
        P("dp", "section", None),
        P("dp", "section", None),
        P("section", "dp", None),
        P(),
        P(None, "dp", None),
    )
    return jax.shard_map(
        per_device, mesh=mesh, in_specs=in_specs, out_specs=out_specs, check_vma=False
    )
```

```python
import functools

import jax
import jax.numpy as jnp
from jax import lax
from jax.experimental import pallas as pl
from jax.experimental.pallas import tpu as pltpu
from jax.sharding import PartitionSpec as P

F32 = jnp.float32
BF16 = jnp.bfloat16
LANES = 128
SUBS = 8
BIAS_ROWS = 16
COST = 100
UNROLL = 64
LIMITS = (14, 16, 16, 12, 16, 12)
ANY = pl.BlockSpec(memory_space=pl.ANY)
HBM = pl.BlockSpec(memory_space=pltpu.HBM)
VMEM = pl.BlockSpec(memory_space=pltpu.VMEM)
SMEM = pl.BlockSpec(memory_space=pltpu.SMEM)


def tiles_of(ref):
    return range(ref.shape[0])


def columns_of(tile):
    return slice(tile * LANES, (tile + 1) * LANES)


def joined(tiles):
    return jnp.concatenate(tiles, axis=1)


def first_row(ref):
    return joined([ref[tile, 0:1, :] for tile in tiles_of(ref)])


def ones_and_zeros(tiles):
    return [jnp.ones((SUBS, LANES), F32)] * tiles, [jnp.zeros((SUBS, LANES), F32)] * tiles


def over_steps(steps, body, state):
    def turn(index, state):
        for part in range(UNROLL):
            state = body(index * UNROLL + part, state)
        return state

    return lax.fori_loop(0, steps // UNROLL, turn, state)


def group(step):
    row = step * SUBS
    return pl.ds(row if isinstance(row, int) else pl.multiple_of(row, SUBS), SUBS)


def forward_steps(candid, forget, keep, first, steps, gains, cells):
    def body(step, state):
        gains, cells = state
        spot = group(first + step)
        kept = keep[spot, :]
        new_gains, new_cells = [], []
        for tile, (gain, cell) in enumerate(zip(gains, cells, strict=True)):
            share = forget[tile, spot, :]
            now = share * kept
            new_cells.append(now * cell + (1.0 - share) * candid[tile, spot, :])
            new_gains.append(gain * now)
        return new_gains, new_cells

    return over_steps(steps, body, (list(gains), list(cells)))


def forward_entries(gains, cells, carry):
    gain, cell = joined(gains), joined(cells)
    entries = []
    for sub in range(SUBS):
        entries.append(carry)
        carry = cell[sub : sub + 1] + gain[sub : sub + 1] * carry
    return jnp.concatenate(entries, axis=0), carry


def forward_fill(candid, forget, keep, steps, entries, out):
    cells = [entries[:, columns_of(tile)] for tile in tiles_of(out)]
    for tile in tiles_of(out):
        out[tile, group(0), :] = cells[tile]

    def body(step, cells):
        spot = group(step)
        kept = keep[spot, :]
        new_cells = []
        for tile, cell in enumerate(cells):
            share = forget[tile, spot, :]
            cell = share * kept * cell + (1.0 - share) * candid[tile, spot, :]
            out[tile, group(step + 1), :] = cell
            new_cells.append(cell)
        return new_cells

    over_steps(steps, body, cells)


def backward_steps(forget, keep, emit, steps):
    tiles = emit.shape[0]

    def body(step, state):
        gains, backs = state
        spot = group(steps - 1 - step)
        kept = keep[spot, :]
        new_gains, new_backs = [], []
        for tile, (gain, back) in enumerate(zip(gains, backs, strict=True)):
            now = forget[tile, spot, :] * kept
            new_backs.append(now * (emit[tile, spot, :] + back))
            new_gains.append(gain * now)
        return new_gains, new_backs

    state = ones_and_zeros(tiles)
    whole = (steps - 1) // UNROLL * UNROLL
    state = over_steps(whole, body, state)
    for step in range(whole, steps - 1):
        state = body(step, state)
    first_gains, backs = state
    firsts = [emit[tile, group(0), :] + backs[tile] for tile in range(tiles)]
    gains, backs = body(steps - 1, state)
    return joined(gains), joined(backs), joined(first_gains), joined(firsts)


def backward_entries(gain, back, carry):
    entries = []
    for sub in reversed(range(SUBS)):
        entries.append(carry)
        carry = back[sub : sub + 1] + gain[sub : sub + 1] * carry
    return jnp.concatenate(entries[::-1], axis=0)


def backward_fill(forget, keep, emit, steps, entries):
    def body(step, backs):
        spot = group(steps - 1 - step)
        kept = keep[spot, :]
        new_backs = []
        for tile, back in enumerate(backs):
            now = emit[tile, spot, :] + back
            emit[tile, spot, :] = now
            new_backs.append(forget[tile, spot, :] * kept * now)
        return new_backs

    over_steps(steps, body, [entries[:, columns_of(tile)] for tile in tiles_of(emit)])


def chunk_backward_summary(forget, keep, emit, steps):
    gain, back, first_gain, first = backward_steps(forget, keep, emit, steps)
    gain_all = jnp.ones_like(gain[0:1])
    back_all = jnp.zeros_like(gain[0:1])
    for sub in reversed(range(SUBS)):
        entry_gain, entry_back = gain_all, back_all
        gain_all = gain[sub : sub + 1] * entry_gain
        back_all = back[sub : sub + 1] + gain[sub : sub + 1] * entry_back
    row_gain = first_gain[0:1] * entry_gain
    row_value = first[0:1] + first_gain[0:1] * entry_back
    return gain_all, back_all, row_gain, row_value


def store_gates(pre, here, candid_out, forget_out, gate_out):
    tiles = candid_out.shape[0]
    for tile in range(tiles):
        candid_out[tile, here, :] = jnp.tanh(pre[:, columns_of(tile)])
        forget_out[tile, here, :] = jax.nn.sigmoid(pre[:, columns_of(tiles + tile)])
        if gate_out is not None:
            gate_out[tile, here, :] = jax.nn.sigmoid(pre[:, columns_of(2 * tiles + tile)])


class Weights:
    def __init__(self, place, layer, near, far, target, sems):
        self.place, self.layer, self.target, self.sems = place, layer, target, sems
        self.near, self.far = near, far

    def each(self, pieces, act):
        section, core, chip = self.place[0], self.place[1] % 2, self.place[1] // 2
        width = self.target.shape[0] // 2
        height = pieces[0].shape[0]
        places = []
        for tap in range(2):
            places += [(tap, chip), (tap, chip ^ (2 - core)), (tap, chip ^ (1 + core))]
        places += [(core, chip ^ 3), (1 - core, chip ^ 3)]
        for index, (piece, (tap, rows)) in enumerate(zip(pieces, places, strict=True)):
            row = ((section % 2) ^ tap) * width + rows * height
            target = self.target.at[pl.ds(pl.multiple_of(row, 16), height), :]
            act(pltpu.make_async_copy(piece, target, self.sems.at[index]))

    def both(self, act):
        if self.far is None:
            width = self.target.shape[0] // 2
            for tap in range(2):
                act(
                    pltpu.make_async_copy(
                        self.near.at[2 * self.layer + tap],
                        self.target.at[pl.ds(tap * width, width), :],
                        self.sems.at[tap],
                    )
                )
            return
        is_near = self.place[0] // 2 == self.layer

        @pl.when(is_near)
        def _():
            self.each(self.near, act)

        @pl.when(jnp.logical_not(is_near))
        def _():
            self.each(self.far, act)

    def start(self):
        self.both(lambda copy: copy.start())

    def wait(self):
        self.both(lambda copy: copy.wait())


def weight_refs(refs, count):
    if count == 1:
        return refs[0], None
    return refs[: count // 2], refs[count // 2 : count]


def join_kernel(place, own, got, *refs):
    out = refs[-1]
    height = own.shape[0]
    core = place[1] % 2
    out[pl.ds(pl.multiple_of(core * height, 16), height), :] = own[...]
    out[pl.ds(pl.multiple_of((1 - core) * height, 16), height), :] = got[...]


def pick_kernel(place, first, second, out):
    @pl.when(place[1] % 2 == 0)
    def _():
        out[...] = first[...]

    @pl.when(place[1] % 2 == 1)
    def _():
        out[...] = second[...]


def before_kernel(*refs):
    place, x, tail, keep = refs[:4]
    prev, shifted = refs[-2:]
    rows, width = x.shape
    top = jnp.where(place[0] > 0, tail[...].astype(F32)[15:16], 0.0)
    for tile in range(width // LANES):
        columns = columns_of(tile)
        shifted[tile, pl.ds(SUBS, rows), :] = x[:, columns].astype(F32)
        shifted[tile, group(0), :] = jnp.concatenate(
            [top[:, columns], shifted[tile, rows : rows + SUBS - 1, :]], axis=0
        )
        prev[:, columns] = (shifted[tile, pl.ds(0, rows), :] * keep[...]).astype(BF16)


def forward_gates(x, prev, matrix, bias, keep, block, candid_out, forget_out, gate_out, finish=None):
    rows, width = x.shape
    tiles = candid_out.shape[0]
    block_steps = block // SUBS

    def part(index, state):
        here = pl.ds(pl.multiple_of(index * block, block), block)
        pre = (
            jnp.dot(x[here, :], matrix[:width, :], preferred_element_type=F32)
            + jnp.dot(prev[here, :], matrix[width:, :], preferred_element_type=F32)
            + bias[...]
        )
        store_gates(pre, here, candid_out, forget_out, gate_out)
        if finish is not None:
            finish(here)
        return forward_steps(candid_out, forget_out, keep, index * block_steps, block_steps, *state)

    return lax.fori_loop(0, rows // block, part, ones_and_zeros(tiles))


def first_forward_kernel(plan, block, *refs):
    place, x, prev, keep, bias = refs[:5]
    near, far = weight_refs(refs[5:], plan)
    candid_out, forget_out, gate_out, summary_out, matrix, weight_sems = refs[5 + plan :]
    rows, width = x.shape
    weights = Weights(place, 0, near, far, matrix, weight_sems)
    weights.start()
    weights.wait()
    gains, cells = forward_gates(x, prev, matrix, bias, keep, block, candid_out, forget_out, gate_out)
    gain_all, cell_all = jnp.ones((1, width), F32), jnp.zeros((1, width), F32)
    gain, cell = joined(gains), joined(cells)
    for sub in range(SUBS):
        cell_all = cell[sub : sub + 1] + gain[sub : sub + 1] * cell_all
        gain_all = gain[sub : sub + 1] * gain_all
    last_gate = joined([gate_out[tile, rows - 1 : rows, :] for tile in tiles_of(gate_out)])
    parts = [gain_all, cell_all, last_gate] + [jnp.zeros((1, width), F32)] * 5
    summary_out[...] = jnp.concatenate(parts, axis=0)


def second_forward_kernel(plan, block, *refs):
    place, candid, forget, gate, keep, cot, bias = refs[:7]
    summaries = refs[7:11]
    near, far = weight_refs(refs[11:], plan)
    (
        cell_out,
        hidden,
        delayed,
        last,
        candid_out,
        forget_out,
        gate_out,
        summary_out,
        matrix,
        order,
        emit,
        shifted,
        weight_sems,
    ) = refs[11 + plan :]
    section = place[0]
    rows, width = hidden.shape
    tiles = emit.shape[0]
    steps = rows // SUBS
    weights = Weights(place, 1, near, far, matrix, weight_sems)
    weights.start()

    heads = heads_of(order, summaries, section)
    carry = jnp.zeros((1, width), F32)
    carries, hiddens = [], [jnp.zeros((1, width), F32)]
    for head in heads:
        carries.append(carry)
        carry = head[1:2] + head[0:1] * carry
        hiddens.append(head[2:3] * carry)
    gains, cells = forward_steps(candid, forget, keep, 0, steps, *ones_and_zeros(tiles))
    entries, carry = forward_entries(gains, cells, pick(carries, section))
    last[...] = jnp.broadcast_to(carry, last.shape)
    forward_fill(candid, forget, keep, steps, entries, cell_out)
    top = pick(hiddens[:-1], section)
    for tile in range(tiles):
        columns = columns_of(tile)
        shifted[tile, pl.ds(SUBS, rows), :] = gate[tile, :, :] * cell_out[tile, pl.ds(SUBS, rows), :]
        shifted[tile, group(0), :] = jnp.concatenate(
            [top[:, columns], shifted[tile, rows : rows + SUBS - 1, :]], axis=0
        )
        hidden[:, columns] = shifted[tile, pl.ds(SUBS, rows), :].astype(BF16)
        delayed[:, columns] = (shifted[tile, pl.ds(0, rows), :].astype(BF16).astype(F32) * keep[...]).astype(BF16)

    weights.wait()

    def emitted(here):
        for tile in range(tiles):
            emit[tile, here, :] = cot[here, columns_of(tile)].astype(F32) * gate_out[tile, here, :]

    gains, cells = forward_gates(
        hidden, delayed, matrix, bias, keep, block, candid_out, forget_out, gate_out, emitted
    )
    cell_all = forward_entries(gains, cells, jnp.zeros((1, width), F32))[1]
    gain_all, back_all, row_gain, row_value = chunk_backward_summary(forget_out, keep, emit, steps)
    parts = [
        gain_all,
        cell_all,
        back_all,
        row_gain,
        row_value,
        first_row(candid_out),
        first_row(forget_out),
        first_row(gate_out),
        last[0:1, :],
    ]
    parts += [jnp.zeros((1, width), F32)] * (16 - len(parts))
    summary_out[...] = jnp.concatenate(parts, axis=0)


def gate_grads(dcell, before, cell, candid, forget, gate, arriving):
    return (
        dcell * (1.0 - forget) * (1.0 - candid * candid),
        dcell * (before - candid) * forget * (1.0 - forget),
        arriving * cell * gate * (1.0 - gate),
    )


def pick(values, section):
    out = values[0]
    for index in range(1, len(values)):
        out = jnp.where(section == index, values[index], out)
    return out


def first_weights_kernel(first, *refs):
    place, x, prev, dpre, bias = refs[:5]
    store_weight_grads(place, (x[...], prev[...]), dpre[:, first:], refs[-2:], bias[:, first:])


def store_weight_grads(place, lefts, right, outs, bias=None):
    for tap, left in enumerate(lefts):
        grads = lax.dot_general(left, right, (((0,), (0,)), ((), ())), preferred_element_type=F32).astype(BF16)
        if len(outs) == 1:
            outs[0][tap] = grads
            continue
        kept, sent = outs
        height = tap_rows(kept)
        chip, odd = place[1] // 2, place[1] % 2 == 1
        for index in range(4):
            even_rows = grads[2 * index * height : (2 * index + 1) * height]
            odd_rows = grads[(2 * index + 1) * height : (2 * index + 2) * height]
            here = block_of(tap, index ^ chip, height)
            kept[here, :] = jnp.where(odd, odd_rows, even_rows)
            sent[here, :] = jnp.where(odd, even_rows, odd_rows)
    if bias is not None and len(outs) > 1:
        for out in outs:
            out[8 * tap_rows(out) :, :] = bias_rows(bias)


def heads_of(order, summaries, section):
    for index, summary in enumerate(summaries):
        order[section ^ index] = summary[...]
    return [order[index] for index in range(len(summaries))]


def back_entries(heads):
    back = jnp.zeros_like(heads[0][0:1])
    backs = []
    for head in reversed(heads):
        backs.append(back)
        back = head[2:3] + head[0:1] * back
    return backs[::-1]


def following_row(heads, backs, section, keep_firsts, cell, arriving):
    nexts = [min(index + 1, len(heads) - 1) for index in range(len(heads))]
    head = pick([heads[index] for index in nexts], section)
    back = pick([backs[index] for index in nexts], section)
    valid = jnp.where(section < len(heads) - 1, 1.0, 0.0)
    keep = pick([keep_firsts[index : index + 1, :] for index in nexts], section)
    keep = joined([keep] * (cell.shape[1] // LANES))
    candid, forget, gate = head[5:6], head[6:7], head[7:8]
    if arriving is None:
        arriving = head[1:2]
    before = keep * cell
    after = forget * before + (1.0 - forget) * candid
    dcell = (head[4:5] + head[3:4] * back) * valid
    return gate_grads(dcell, before, after, candid, forget, gate, arriving * valid), keep


def store_grads(rows, dcells, cells, candid, forget, gate, arriving, keep, next_first, extra, shifted, outs):
    dpre_out, shifted_out, bias_out, after = outs
    tiles = dcells.shape[0]
    width = tiles * LANES
    part_rows = 64
    for index in range(3):
        rounded = extra[index].astype(BF16).astype(F32) * joined([next_first[:, :LANES]] * tiles)
        after[:, index * width : (index + 1) * width] = jnp.broadcast_to(rounded, (SUBS, width))

    def of_tile(tile, carry):
        def of_rows(part, sums):
            base = pl.multiple_of(part * part_rows, part_rows)
            here = pl.ds(base, part_rows)
            kept = keep[here, :]
            parts = gate_grads(
                dcells[tile, here, :],
                cells[tile, here, :] * kept,
                cells[tile, pl.ds(pl.multiple_of(base + SUBS, SUBS), part_rows), :],
                candid[tile, here, :],
                forget[tile, here, :],
                gate[tile, here, :],
                arriving[here, pl.ds(pl.multiple_of(tile * LANES, LANES), LANES)].astype(F32),
            )
            new_sums = []
            for index, part in enumerate(parts):
                rounded = part.astype(BF16)
                columns = pl.ds(pl.multiple_of((index * tiles + tile) * LANES, LANES), LANES)
                dpre_out[here, columns] = rounded
                rounded = rounded.astype(F32)
                shifted[index, here, :] = rounded * kept
                new_sums.append(
                    sums[index] + jnp.sum(rounded.reshape(part_rows // SUBS, SUBS, LANES), axis=0)
                )
            return new_sums

        sums = lax.fori_loop(0, rows // part_rows, of_rows, [jnp.zeros((SUBS, LANES), F32)] * 3)
        for index in range(3):
            columns = pl.ds(pl.multiple_of((index * tiles + tile) * LANES, LANES), LANES)
            shifted[index, pl.ds(rows, SUBS), :] = jnp.concatenate(
                [shifted[index, 1:SUBS, :], after[0:1, columns]], axis=0
            )
            shifted_out[:, columns] = shifted[index, pl.ds(SUBS, rows), :].astype(BF16)
            bias_out[:, columns] = jnp.broadcast_to(
                jnp.sum(sums[index], axis=0, keepdims=True), (bias_out.shape[0], LANES)
            )
        return carry

    lax.fori_loop(0, tiles, of_tile, 0)


def second_backward_kernel(rows, has_sent, *refs):
    (place, candid, forget, gate, hidden, delayed, keep, cot, cot_next, keep_firsts) = refs[:10]
    summaries = refs[10:14]
    outs = refs[14:]
    hidden_out, dpre_out, shifted_out, bias_out, last_out = outs[:5]
    grads = outs[5 : 7 if has_sent else 6]
    order, cells, dcells, shifted, after = refs[-5:]
    section = place[0]
    width = hidden.shape[1]
    tiles = dcells.shape[0]
    steps = rows // SUBS
    heads = heads_of(order, summaries, section)
    carry = jnp.zeros((1, width), F32)
    carries = []
    for head in heads:
        carries.append(carry)
        carry = head[1:2] + head[0:1] * carry
    last_out[0] = heads[-1][8:9]
    last_out[1] = carry
    backs = back_entries(heads)
    carry = pick(carries, section)
    back = pick(backs, section)
    for tile in range(tiles):
        dcells[tile, :, :] = cot[:, columns_of(tile)].astype(F32) * gate[tile, :, :]
    gains, ends = forward_steps(candid, forget, keep, 0, steps, *ones_and_zeros(tiles))
    entries, carry = forward_entries(gains, ends, carry)
    forward_fill(candid, forget, keep, steps, entries, cells)
    for tile in range(tiles):
        hidden_out[:, columns_of(tile)] = (gate[tile, :, :] * cells[tile, pl.ds(SUBS, rows), :]).astype(BF16)
    gain, leaving, _, _ = backward_steps(forget, keep, dcells, steps)
    backward_fill(forget, keep, dcells, steps, backward_entries(gain, leaving, back))
    extra, next_first = following_row(heads, backs, section, keep_firsts, carry, cot_next[...].astype(F32)[0:1])
    store_grads(
        rows, dcells, cells, candid, forget, gate, cot, keep, next_first, extra, shifted,
        (dpre_out, shifted_out, bias_out, after),
    )
    store_weight_grads(place, (hidden[...], delayed[...]), dpre_out[...], grads)


def input_grad_tile(dpre, shifted, matrix, here):
    width = matrix.shape[0] // 2
    contract = (((1,), (1,)), ((), ()))
    return lax.dot_general(
        dpre[here, :], matrix[:width, :], contract, preferred_element_type=F32
    ) + lax.dot_general(shifted[here, :], matrix[width:, :], contract, preferred_element_type=F32)


def middle_kernel(rows, block, *refs):
    place, dpre, shifted, candid, forget, gate, keep, matrix = refs[:8]
    arriving_out, summary_out, emit = refs[8:]

    def part(index, carry):
        here = pl.ds(pl.multiple_of(index * block, block), block)
        arriving = input_grad_tile(dpre, shifted, matrix, here).astype(BF16)
        arriving_out[here, :] = arriving
        for tile in tiles_of(emit):
            emit[tile, here, :] = arriving[:, columns_of(tile)].astype(F32) * gate[tile, here, :]
        return carry

    lax.fori_loop(0, rows // block, part, 0)
    row_arriving = arriving_out[0:16, :].astype(F32)[0:1]
    gain_all, back_all, row_gain, row_value = chunk_backward_summary(forget, keep, emit, rows // SUBS)
    parts = [
        gain_all,
        row_arriving,
        back_all,
        row_gain,
        row_value,
        first_row(candid),
        first_row(forget),
        first_row(gate),
    ]
    summary_out[...] = jnp.concatenate(parts, axis=0)


def first_backward_kernel(rows, has_sent, *refs):
    (place, candid, forget, gate, cells, last, x, prev, keep, arriving, keep_firsts, other_bias) = refs[:12]
    summaries = refs[12:16]
    order, dcells, shifted, after = refs[-4:]
    outs = refs[-11:-4] if has_sent else refs[-8:-4]
    dpre_out, shifted_out, bias_out, *grads = outs
    section = place[0]
    steps = rows // SUBS
    heads = heads_of(order, summaries, section)
    backs = back_entries(heads)
    back = pick(backs, section)
    for tile in tiles_of(dcells):
        dcells[tile, :, :] = arriving[:, columns_of(tile)].astype(F32) * gate[tile, :, :]
    gain, leaving, _, _ = backward_steps(forget, keep, dcells, steps)
    backward_fill(forget, keep, dcells, steps, backward_entries(gain, leaving, back))
    extra, next_first = following_row(heads, backs, section, keep_firsts, last[0:1, :], None)
    store_grads(
        rows, dcells, cells, candid, forget, gate, arriving, keep, next_first, extra, shifted,
        (dpre_out, shifted_out, bias_out.at[pl.ds(0, SUBS), :], after),
    )
    bias_out[SUBS:, :] = other_bias[...]
    done = 0
    for part in range(0, len(grads), 2):
        columns = slice(done, done + grads[part].shape[-1])
        store_weight_grads(
            place, (x[...], prev[...]), dpre_out[:, columns], grads[part : part + 2], bias_out[:, columns]
        )
        done = columns.stop


def last_kernel(plan, block, *refs):
    place, dpre, shifted = refs[:3]
    near, far = weight_refs(refs[3:], plan)
    out, matrix, weight_sems = refs[-3:]
    weights = Weights(place, 0, near, far, matrix, weight_sems)
    weights.start()
    weights.wait()

    def part(index, carry):
        here = pl.ds(pl.multiple_of(index * block, block), block)
        out[here, :] = input_grad_tile(dpre, shifted, matrix, here)
        return carry

    lax.fori_loop(0, dpre.shape[0] // block, part, 0)


def added(*parts):
    return functools.reduce(jnp.add, [part.astype(F32) for part in parts])


def bias_rows(bias):
    rows = []
    for row in (bias[0:1], bias[SUBS : SUBS + 1]):
        high = row.astype(BF16).astype(F32)
        rows += [high, row - high]
    rows.append(jnp.zeros((BIAS_ROWS - len(rows), bias.shape[1]), F32))
    return jnp.concatenate(rows, axis=0).astype(BF16)


def bias_of(rows):
    rows = rows.astype(F32)
    return jnp.concatenate([rows[0:1] + rows[1:2], rows[2:3] + rows[3:4]], axis=0)


def sum_in_order(order, values, position):
    for index, value in enumerate(values):
        order[position ^ index] = value
    out = order[0]
    for index in range(1, len(values)):
        out = out + order[index]
    return out


def tap_rows(kept):
    return kept.shape[0] // 8 // 16 * 16


def block_of(tap, chip, height):
    row = (tap * 4 + chip) * height
    return pl.ds(row if isinstance(row, int) else pl.multiple_of(row, 16), height)


def chip_sum(kept, got, tap, chip, *more):
    height = tap_rows(kept)
    here = block_of(tap, chip, height)
    return added(kept[here, :], got[here, :], *more)


def chip_bias(kept, got):
    height = tap_rows(kept)
    whole = bias_of(kept[8 * height :, :]) + bias_of(got[8 * height :, :])
    return bias_rows(jnp.concatenate([whole[0:1]] * SUBS + [whole[1:2]] * SUBS, axis=0))


def corner_kernel(split, *refs):
    kept, got = refs[:2]
    by_x, by_y = refs[-2:]
    height = tap_rows(kept)
    for tap, (out, chip) in enumerate(((by_x, 1), (by_y, 2))):
        out[0:height, :] = chip_sum(kept, got, tap, 3).astype(BF16)
        if split:
            out[height : 2 * height, :] = chip_sum(kept, got, tap, chip).astype(BF16)
            out[2 * height :, :] = chip_bias(kept, got)


def sides_kernel(split, *refs):
    kept, got, from_x, from_y = refs[:4]
    by_x, by_y = refs[-2:]
    height = tap_rows(kept)
    by_x[0:height, :] = chip_sum(kept, got, 1, 1, from_y[0:height, :]).astype(BF16)
    by_y[0:height, :] = chip_sum(kept, got, 0, 2, from_x[0:height, :]).astype(BF16)
    if split:
        by_x[height:, :] = from_y[2 * height :, :]
    else:
        by_x[height:, :] = chip_sum(kept, got, 0, 1).astype(BF16)
        by_y[height:, :] = chip_sum(kept, got, 1, 2).astype(BF16)


def plane_kernel(split, *refs):
    place, kept, got, from_x, from_y, corner_x, corner_y = refs[:7]
    height = tap_rows(kept)
    beside = pl.ds(height, height)
    direct = (corner_x, corner_y) if split else (from_x, from_y)
    sums = [
        chip_sum(kept, got, 0, 0, direct[0][beside, :], from_y[0:height, :]),
        chip_sum(kept, got, 1, 0, direct[1][beside, :], from_x[0:height, :]),
    ]
    if split:
        mine, other, order = refs[-3:]
        parts = [chip_bias(kept, got), corner_x[2 * height :, :], corner_y[2 * height :, :], from_x[height:, :]]
        whole = sum_in_order(order, [bias_of(part) for part in parts], place[1] // 2)
        whole = bias_rows(jnp.concatenate([whole[0:1]] * SUBS + [whole[1:2]] * SUBS, axis=0))
        mine[height:, :] = whole.astype(F32)
        other[height:, :] = whole
    else:
        mine, other = refs[-2:]
    odd = place[0] % 2 == 1
    mine[0:height, :] = jnp.where(odd, sums[1], sums[0])
    other[0:height, :] = jnp.where(odd, sums[0], sums[1]).astype(BF16)


def pair_kernel(*refs):
    mine, got, *_, out = refs
    out[...] = added(mine[...], got[...])


def crossing_kernel(columns, *refs):
    place, mine, got, second = refs[:4]
    kept, out = refs[-2:]
    height = second.shape[0]
    sums = (added(mine[0:height, :], got[0:height, :]), second[:, columns])
    upper = place[0] >= 2
    kept[0:height, :] = jnp.where(upper, sums[1], sums[0])
    out[0:height, :] = jnp.where(upper, sums[0], sums[1]).astype(BF16)
    whole = bias_of(mine[height:, :]) + bias_of(got[height:, :])
    whole = bias_rows(jnp.concatenate([whole[0:1]] * SUBS + [whole[1:2]] * SUBS, axis=0))
    kept[height:, :] = whole.astype(F32)
    out[height:, :] = whole


def whole_kernel(parts, *refs):
    out, bias_out = refs[-2:]
    height = out.shape[0]
    for index, columns in enumerate(parts):
        kept, got = refs[2 * index : 2 + 2 * index]
        out[:, columns] = added(kept[0:height, :], got[0:height, :])
        bias_out[:, columns] = bias_of(kept[height:, :]) + bias_of(got[height:, :])


def call(kernel, outs, in_specs, out_specs, scratch, flops, moved, megabytes, name):
    return pl.pallas_call(
        kernel,
        out_shape=outs,
        in_specs=in_specs,
        out_specs=out_specs,
        scratch_shapes=scratch,
        compiler_params=pltpu.CompilerParams(vmem_limit_bytes=megabytes * 2**20),
        cost_estimate=pl.CostEstimate(flops=flops // COST, bytes_accessed=moved // COST, transcendentals=0),
        name=name,
    )


def small_call(kernel, outs, operands, name, ties=(), scratch=(), flops=1000000):
    has_place = operands[0].dtype == jnp.int32
    specs = [SMEM if has_place and index == 0 else VMEM for index in range(len(operands))]
    return call(
        kernel,
        outs,
        specs + [ANY] * len(ties),
        [VMEM] * len(outs),
        list(scratch),
        flops,
        1000000,
        12,
        name,
    )(*operands, *ties)


def swap(value, axis, mask):
    pairs = [(index, index ^ mask) for index in range(lax.axis_size(axis))]
    return lax.ppermute(value, axis, pairs)


def moved(value, axis, target):
    return lax.ppermute(value, axis, [(index, target(index)) for index in range(lax.axis_size(axis))])


def gathered_pieces(place, shard, early):
    height, gates = shard.shape
    chip = jax.ShapeDtypeStruct((2 * height, gates), shard.dtype)

    def joined_cores(own, ties=()):
        return small_call(join_kernel, [chip], [place, own, swap(own, "dp", 1)], "join", ties)[0]

    def beside(unit):
        return moved(unit, "dp", lambda index: index ^ (3 if index % 2 == 0 else 5))

    def opposite(first, second):
        unit = small_call(pick_kernel, [chip], [place, first, second], "pick")[0]
        return moved(unit, "dp", lambda index: index ^ (2 if index % 2 == 0 else 4))

    two = swap(shard, "section", 2)
    one = swap(shard, "section", 1)
    three = swap(two, "section", 1)
    units, got, across = [], [], []
    for own, ties in ((shard, []), (one, [0]), (two, []), (three, [1])):
        ties = [got[index] for index in ties] + (early if len(got) == 1 else [])
        units.append(joined_cores(own, ties))
        got.append(beside(units[-1]))
        if len(got) % 2 == 0:
            across.append(opposite(*got[-2:]))
    out = []
    for pair in range(2):
        for tap in range(2 * pair, 2 * pair + 2):
            out += [units[tap], got[tap], swap(got[tap], "dp", 1)]
        out += [across[pair], swap(across[pair], "dp", 1)]
    return out


class LayerSum:
    def __init__(self, place, kept, sent):
        self.place, self.kept, self.got = place, kept, swap(sent, "dp", 1)
        self.height, self.gates = tap_rows(kept), kept.shape[1]
        self.extra = kept.shape[0] - 8 * self.height

    def rows(self, taps, extra, dtype=BF16):
        return jax.ShapeDtypeStruct((taps * self.height + extra, self.gates), dtype)

    def corners(self, ties=()):
        by_x, by_y = small_call(
            functools.partial(corner_kernel, self.extra > 0),
            [self.rows(2 if self.extra else 1, self.extra)] * 2,
            [self.kept, self.got],
            "corners",
            ties,
        )
        self.corner_sent = by_x
        self.corner_x, self.corner_y = swap(by_x, "dp", 2), swap(by_y, "dp", 4)

    def sides(self, ties=()):
        self.by = small_call(
            functools.partial(sides_kernel, self.extra > 0),
            [self.rows(1, self.extra), self.rows(1, 0)] if self.extra else [self.rows(2, 0)] * 2,
            [self.kept, self.got, self.corner_x, self.corner_y],
            "sides",
            ties,
        )
        self.side_x, self.side_y = swap(self.by[0], "dp", 2), swap(self.by[1], "dp", 4)

    def plane(self, ties=(), flops=1000000):
        operands = [self.place, self.kept, self.got, self.side_x, self.side_y, self.corner_x, self.corner_y]
        scratch = []
        if self.extra > 0:
            scratch = [pltpu.VMEM((4, 2, self.gates), F32)]
        self.mine, other = small_call(
            functools.partial(plane_kernel, self.extra > 0),
            [self.rows(1, self.extra, F32), self.rows(1, self.extra)],
            operands,
            "plane",
            ties,
            scratch,
            flops,
        )
        self.near = swap(other, "section", 1)

    def paired(self):
        return small_call(pair_kernel, [self.rows(1, 0, F32)], [self.mine, self.near], "paired")[0]

    def crossing(self, second, columns, ties=()):
        self.pair, sent = small_call(
            functools.partial(crossing_kernel, columns),
            [self.rows(1, self.extra, F32), self.rows(1, self.extra)],
            [self.place, self.mine, self.near, second],
            "crossing",
            ties,
        )
        self.got_pair = swap(sent, "section", 2)


def all_sums(value):
    for axis in ("dp", "section"):
        mask = 1
        while mask < lax.axis_size(axis):
            value = value + swap(value, axis, mask)
            mask *= 2
    return value


def grouped(value, rows):
    length, width = value.shape
    return value.reshape(length // rows, SUBS, rows // SUBS, width).swapaxes(1, 2).reshape(length, width)


def ungrouped(value):
    rows, width = value.shape
    return value.reshape(rows // SUBS, SUBS, width).swapaxes(0, 1).reshape(rows, width)


def per_device(tokens_in, doc_starts, cotangent, tap_weight, gate_bias):
    sections = lax.axis_size("section")
    streams = lax.axis_size("dp")
    section = lax.axis_index("section")
    stream = lax.axis_index("dp")
    _, length, width = tokens_in.shape
    gates = 3 * width
    tiles = width // LANES
    rows = length // sections
    block = 512
    start = section * rows
    height = tap_weight.shape[1]
    quick = sections == 4 and streams == 8 and height % 16 == 0

    def own(value):
        return lax.dynamic_slice_in_dim(value, start, rows, 0)

    def own(value):
        return lax.dynamic_slice_in_dim(value, start, rows, 0)

    place = jnp.stack([section, stream]).astype(jnp.int32)
    keep = (1 - doc_starts[0]).astype(F32)[:, None]
    keep_own = grouped(jnp.broadcast_to(own(keep), (rows, LANES)), rows)
    keep_firsts = jnp.broadcast_to(jnp.concatenate([keep[::rows], keep[: 8 - sections]], axis=0), (8, LANES))
    x = grouped(own(tokens_in[0]), rows)
    tail = lax.dynamic_slice_in_dim(tokens_in[0], jnp.maximum(start - 16, 0), 16, 0)
    cot = grouped(own(cotangent[0]), rows)
    cot_next = lax.dynamic_slice_in_dim(cotangent[0], jnp.minimum(start + rows, length - 16), 16, 0)
    bias = gate_bias.astype(F32)

    def shape(*dims, dtype=F32):
        return jax.ShapeDtypeStruct(dims, dtype)

    def buffer(*dims, dtype=F32):
        return pltpu.VMEM(dims, dtype)

    dma = pltpu.SemaphoreType.DMA
    layer_flops = 2 * rows * width * gates * 2
    weight_bytes = 4 * width * gates
    half = shape(rows, width, dtype=BF16)
    full = shape(tiles, rows, LANES)
    scan = buffer(tiles, rows, LANES)
    matrix = shape(2 * width, gates, dtype=BF16)

    half = shape(rows, width, dtype=BF16)
    (prev,) = small_call(
        before_kernel,
        [half],
        [place, x, tail, keep_own],
        "before",
        [keep_firsts, cot, cot_next, bias],
        scratch=[buffer(tiles, rows + SUBS, LANES)],
    )
    early = [prev]
    if quick:
        weights = gathered_pieces(place, tap_weight[0], early)
    else:
        whole = lax.all_gather(tap_weight, "dp", axis=1, tiled=True)
        weights = [lax.all_gather(whole, "section", axis=0, tiled=True)]
    plan = len(weights)
    weight_count = plan

    def exchanged(summary):
        return [summary] + [swap(summary, "section", index) for index in range(1, sections)]

    candid0, forget0, gate0, summary = call(
        functools.partial(first_forward_kernel, plan, block),
        [full] * 3 + [shape(8, width)],
        [SMEM] + [VMEM] * 4 + [HBM] * len(weights),
        [VMEM] * 4,
        [buffer(2 * width, gates, dtype=BF16), dma((weight_count + 1,))],
        layer_flops,
        weight_bytes + 30 * rows * width,
        LIMITS[0],
        "first_forward",
    )(place, x, prev, keep_own, bias[0:1], *weights)

    cells0, hidden0, delayed0, last0, candid1, forget1, gate1, summary1, matrix1 = call(
        functools.partial(second_forward_kernel, plan, block),
        [shape(tiles, rows + SUBS, LANES), half, half, shape(8, width)]
        + [full] * 3
        + [shape(16, width), matrix],
        [SMEM] + [VMEM] * 10 + [HBM] * len(weights),
        [VMEM] * 9,
        [
            buffer(sections, 8, width),
            scan,
            buffer(tiles, rows + SUBS, LANES),
            dma((weight_count + 1,)),
        ],
        layer_flops,
        weight_bytes + 20 * rows * width,
        LIMITS[1],
        "second_forward",
    )(place, candid0, forget0, gate0, keep_own, cot, bias[1:2], *exchanged(summary), *weights)

    if quick:

        def kept_and_sent(columns, extra):
            return [shape(8 * height + extra, columns, dtype=BF16)] * 2

        kept_shape = kept_and_sent(gates, 0)
    else:
        kept_shape = [shape(2, width, gates, dtype=BF16)]
    wide = shape(rows, gates, dtype=BF16)

    hidden1, dpre1, shifted1, bias1, lasts, *kept1 = call(
        functools.partial(second_backward_kernel, rows, quick),
        [half, wide, wide, shape(8, gates), shape(2, 1, width)] + kept_shape,
        [SMEM] + [VMEM] * 13,
        [VMEM] * (5 + len(kept_shape)),
        [buffer(sections, 16, width), buffer(tiles, rows + SUBS, LANES), scan, buffer(3, rows + SUBS, LANES), buffer(SUBS, gates)],
        layer_flops,
        weight_bytes + 30 * rows * width,
        LIMITS[2],
        "second_backward",
    )(
        place, candid1, forget1, gate1, hidden0, delayed0, keep_own, cot, cot_next, keep_firsts,
        *exchanged(summary1),
    )

    arriving, summary0 = call(
        functools.partial(middle_kernel, rows, block),
        [half, shape(8, width)],
        [SMEM] + [VMEM] * 7,
        [VMEM] * 2,
        [scan],
        layer_flops,
        weight_bytes + 20 * rows * width,
        LIMITS[3],
        "middle",
    )(place, dpre1, shifted1, candid0, forget0, gate0, keep_own, matrix1)

    summaries = exchanged(summary0)
    ties = []
    first_shape, first_columns = kept_shape, gates
    if quick:
        second = LayerSum(place, *kept1)
        second.corners(ties=[arriving])
        second.sides(ties=summaries[1:])
        ties = second.by
        first_columns = gates // LANES * 8 // 15 * LANES
        first_shape = kept_and_sent(first_columns, BIAS_ROWS) + kept_and_sent(gates - first_columns, BIAS_ROWS)
    dpre0, shifted0, bias_both, *kept0 = call(
        functools.partial(first_backward_kernel, rows, quick),
        [wide, wide, shape(2 * SUBS, gates)] + first_shape,
        [SMEM] + [VMEM] * 15 + [ANY] * len(ties),
        [VMEM] * (3 + len(first_shape)),
        [buffer(sections, 8, width), scan, buffer(3, rows + SUBS, LANES), buffer(SUBS, gates)],
        layer_flops,
        weight_bytes + 30 * rows * width,
        LIMITS[4],
        "first_backward",
    )(
        place, candid0, forget0, gate0, cells0, last0, x, prev, keep_own, arriving, keep_firsts, bias1,
        *summaries, *ties,
    )
    input_grad = call(
        functools.partial(last_kernel, plan, block),
        shape(rows, width),
        [SMEM] + [VMEM] * 2 + [HBM] * len(weights),
        VMEM,
        [buffer(2 * width, gates, dtype=BF16), dma((weight_count + 1,))],
        COST * layer_flops,
        COST * weight_bytes,
        LIMITS[5],
        "last",
    )(place, dpre0, shifted0, *weights)

    if quick:
        second.plane(ties=[input_grad], flops=COST * 3 * 10**10)
        parts = [slice(0, first_columns), slice(first_columns, gates)]
        sums = [LayerSum(place, *kept0[:2]), LayerSum(place, *kept0[2:])]
        sums[0].corners(ties=[second.mine])
        sums[1].corners(ties=[sums[0].corner_sent])
        sums[0].sides(ties=[sums[1].corner_sent])
        pair = second.paired()
        sums[0].plane()
        sums[1].sides(ties=[sums[0].mine])
        sums[0].crossing(pair, parts[0])
        sums[1].plane(ties=[sums[0].pair])
        sums[1].crossing(pair, parts[1], ties=[sums[0].got_pair])
        weight_grad, bias_grad = small_call(
            functools.partial(whole_kernel, parts),
            [shape(height, gates), shape(2, gates)],
            [value for part in sums for value in (part.pair, part.got_pair)],
            "whole",
        )
        weight_grad = weight_grad[None]
    else:
        bias_grad = all_sums(bias_both[::8])
        stacked = jnp.concatenate([kept0[0], kept1[0]], axis=0)
        by_rows = lax.psum_scatter(stacked, "dp", scatter_dimension=1, tiled=True)
        weight_grad = lax.psum_scatter(by_rows, "section", scatter_dimension=0, tiled=True).astype(F32)
    return (ungrouped(hidden1)[None], ungrouped(input_grad)[None], weight_grad, bias_grad, lasts)


def solution(mesh):
    in_specs = (
        P("dp", None, None),
        P("dp", None),
        P("dp", None, None),
        P("section", "dp", None),
        P(),
    )
    out_specs = (
        P("dp", "section", None),
        P("dp", "section", None),
        P("section", "dp", None),
        P(),
        P(None, "dp", None),
    )
    return jax.shard_map(
        per_device, mesh=mesh, in_specs=in_specs, out_specs=out_specs, check_vma=False
    )
```
